32 devices in a mesh: mod: 16 (over z, y, core), pair: 2 (over x).
Axes of the slice: x: 2, y: 2, z: 4, core: 2. Of those that a mesh axis runs over, the one named last changes fastest.
Arguments:
- rows_input: bfloat16 [65536, 768], P(('mod', 'pair')), may hold values from -6 to 6
- grad_out: bfloat16 [65536, 768], P(('mod', 'pair')), may hold values from -6 to 6
- w_qkv: bfloat16 [768, 2304], P('pair', 'mod'), may hold values from -0.21875 to 0.21875
- w_out: bfloat16 [768, 768], P('pair', 'mod'), may hold values from -0.625 to 0.625
- w_up: bfloat16 [768, 3072], P('pair', 'mod'), may hold values from -0.21875 to 0.21875
- w_down: bfloat16 [3072, 768], P('pair', 'mod'), may hold values from -0.109375 to 0.109375
- vectors: bfloat16 [8, 768], P('pair', 'mod'), may hold values from -1.6 to 1.6
- b_up: bfloat16 [8, 384], P('pair', 'mod'), may hold values from -3 to 3
- live_rows: int32 [1024], P(('mod', 'pair')), may hold values from 16 to 64, as said below
Outputs:
- rows_output: bfloat16 [65536, 768], P(('mod', 'pair'))
- grad_input: float32 [65536, 768], P(('mod', 'pair'))
- grad_w_qkv: float32 [768, 2304], P('pair', 'mod')
- grad_w_out: float32 [768, 768], P('pair', 'mod')
- grad_w_up: float32 [768, 3072], P('pair', 'mod')
- grad_w_down: float32 [3072, 768], P('pair', 'mod')
- grad_vectors: float32 [8, 768], P('pair', 'mod')
- grad_b_up: float32 [8, 384], P('pair', 'mod')
The draws below stay inside these ranges and needn't reach their ends.
Inputs may be any that keep to these rules, and one draw needn't show every extreme that they name: `live_rows`: each entry lies between 16 and 64; both ends occur in every draw.
All inputs are finite; a program needn't handle non-finite values.
Results may differ from the reference program's by a relative error of at most 0.019.
Values may be sent and summed in bfloat16 or wider, within the bound.
No kernel may reach another device: no remote copies, remote signals or barrier semaphores. Data moves between devices by JAX's collectives and lax.ppermute only.
A program may use at most 320 MiB of HBM per device.

```python
import math
import jax
import jax.numpy as jnp
from jax import lax

D = 768
HEADS = 12
HEAD_DIM = 64
FF = 3072
SLOTS = 64
PAIRS_DEV = 8
MICRO = 4
ROWS_ALL = 65536
LIVE_N = 1024
N_MOD = 16
N_PAIR = 2


def draw_live_rows(key, part):
    first_key = jax.random.fold_in(key, 11)
    second_key = jax.random.fold_in(key, 12)
    third_key = jax.random.fold_in(key, 13)
    counts = jax.random.randint(first_key, (LIVE_N,), SLOTS // 4, SLOTS + 1)
    top_place = jax.random.randint(second_key, (), 0, LIVE_N)
    offset = jax.random.randint(third_key, (), 1, LIVE_N)
    bottom_place = (top_place + offset) % LIVE_N
    counts = counts.at[top_place].set(SLOTS)
    counts = counts.at[bottom_place].set(SLOTS // 4)
    return counts.astype(jnp.int32)


def draw_vectors(key, part):
    bias_key = jax.random.fold_in(key, 21)
    gain_key = jax.random.fold_in(key, 22)
    biases = jnp.clip(0.4 * jax.random.normal(bias_key, (8, D), jnp.float32), -1.6, 1.6)
    gains = jax.random.uniform(gain_key, (8, D), jnp.float32, 0.5, 1.5)
    rows = jnp.arange(8)[:, None]
    is_gain = (rows == 4) | (rows == 6)
    return jnp.where(is_gain, gains, biases).astype(jnp.bfloat16)


def levels(stream_key, shape, cuts, smallest, top_value):
    factor_of = 1.0
    for dim, shards_of in cuts:
        draws = jax.random.uniform(jax.random.fold_in(jax.random.fold_in(stream_key, 6), dim), (shards_of,), jnp.float32, smallest / len(cuts), top_value / len(cuts))
        factor_of = factor_of * jnp.repeat(jnp.exp(draws), shape[dim] // shards_of).reshape((-1,) + (1,) * (len(shape) - 1 - dim))
    return factor_of


def noise(own_key, shape, deviation, limit, split=(), held_as=jnp.bfloat16):
    factor_of = levels(own_key, shape, split, -0.22, 0.18) if split else 1.0
    values = jax.random.normal(own_key, shape, jnp.float32) * deviation * factor_of
    return jnp.minimum(jnp.maximum(values, -limit), limit).astype(held_as)


def setup_inputs(seed: int = 0) -> dict:
    key_list = jax.random.split(jax.random.key(seed), 10)
    return {
        "rows_input": noise(key_list[0], (ROWS_ALL, D), 1.0, 6.0, ((0, 32),)),
        "grad_out": noise(key_list[1], (ROWS_ALL, D), 1.0, 6.0, ((0, 32),)),
        "w_qkv": noise(key_list[2], (D, 3 * D), D ** -0.5, 0.21875, ((0, 2), (1, 16))),
        "w_out": noise(key_list[3], (D, D), (D // 8) ** -0.5, 0.625, ((0, 2), (1, 16))),
        "w_up": noise(key_list[4], (D, FF), D ** -0.5, 0.21875, ((0, 2), (1, 16))),
        "w_down": noise(key_list[5], (FF, D), FF ** -0.5, 0.109375, ((0, 2), (1, 16))),
        "vectors": draw_vectors(jax.random.fold_in(key_list[9], 71), 0),
        "b_up": noise(key_list[7], (8, FF // 8), 0.5, 3.0, ((0, 2), (1, 16))),
        "live_rows": draw_live_rows(jax.random.fold_in(key_list[9], 71), 0),
    }


EPS = 1e-05
NEG = -1000000000.0

@jax.custom_vjp
def low(v):
    return lax.optimization_barrier(v.astype(jnp.bfloat16)).astype(jnp.float32)

@jax.custom_vjp
def low_back(v):
    return v

def low_keep(v):
    return (low(v), None)

def low_pass(kept, grad):
    return (grad,)

def back_keep(v):
    return (v, None)

def back_low(kept, grad):
    return (low(grad),)
low.defvjp(low_keep, low_pass)
low_back.defvjp(back_keep, back_low)

def norm_rows(values, gain, shift):
    centre = values - lax.optimization_barrier(jnp.mean(values, -1, keepdims=True))
    spread = lax.optimization_barrier(jnp.mean(centre * centre, -1, keepdims=True))
    return centre * lax.rsqrt(spread + EPS) * gain + shift

def matmul(left, right):
    return jnp.dot(left, right, precision=lax.Precision.HIGHEST)

def layer(rows_in, live, wqkv, wout, wup, wdown, vec, bias_up):
    group, doubled, width = rows_in.shape
    slots = doubled // 2
    scale = HEAD_DIM ** (-0.5)
    bias_qkv = jnp.concatenate([vec[0], jnp.zeros_like(vec[0]), vec[1]])
    projected = low(low_back(matmul(rows_in, wqkv) + bias_qkv))
    queries = projected[..., :width].reshape(group, doubled, HEADS, HEAD_DIM)
    keys_all = projected[..., width:2 * width].reshape(group, doubled, HEADS, HEAD_DIM)
    values_all = projected[..., 2 * width:].reshape(group, doubled, HEADS, HEAD_DIM)
    scores = low_back(jnp.einsum('pqhd,pkhd->phqk', queries, keys_all, precision=lax.Precision.HIGHEST) * scale)
    position = jnp.arange(doubled)
    valid = jnp.where(position[None, :] < slots, position[None, :] < live[:, 0:1], position[None, :] - slots < live[:, 1:2])
    scores = jnp.where(valid[:, None, None, :], scores, NEG)
    peak = lax.optimization_barrier(jnp.max(scores, -1, keepdims=True))
    expo = jnp.exp(scores - peak)
    attend = expo / lax.optimization_barrier(jnp.sum(expo, -1, keepdims=True))
    mixed = jnp.einsum('phqk,pkhd->pqhd', low(attend), values_all, precision=lax.Precision.HIGHEST)
    mixed = low(low_back(mixed)).reshape(group, doubled, width)
    branch = low_back(matmul(mixed, wout) + vec[2])
    first = norm_rows(rows_in + branch, vec[4], vec[5])
    inner = low_back(matmul(low(first), wup) + bias_up)
    outer = low_back(matmul(low(jax.nn.gelu(inner, approximate=False)), wdown) + vec[3])
    return norm_rows(first + outer, vec[6], vec[7])

def reference(rows_input, grad_out, w_qkv, w_out, w_up, w_down, vectors, b_up, live_rows):
    half = N_MOD // 2
    count = half * N_PAIR * MICRO * PAIRS_DEV
    group = math.gcd(count, 32)
    blocks = count // group

    def to_pairs(array):
        shaped = array.reshape(2, half, N_PAIR, MICRO, PAIRS_DEV, SLOTS, D)
        return shaped.transpose(1, 2, 3, 4, 0, 5, 6).reshape(count, 2 * SLOTS, D)

    def from_pairs(array):
        shaped = array.reshape(half, N_PAIR, MICRO, PAIRS_DEV, 2, SLOTS, D)
        return shaped.transpose(4, 0, 1, 2, 3, 5, 6).reshape(ROWS_ALL, D)
    live = live_rows.reshape(2, half, N_PAIR, MICRO, PAIRS_DEV).transpose(1, 2, 3, 4, 0).reshape(count, 2)
    live_blocks = live.reshape(blocks, group, 2)

    def whole(rows_all, wqkv, wout, wup, wdown, vec, bias_rows):
        bias_up = bias_rows.reshape(FF)

        def block(item):
            rows_in, live_in = item
            return layer(rows_in, live_in, wqkv, wout, wup, wdown, vec, bias_up)
        result = lax.map(jax.checkpoint(block), (rows_all.reshape(blocks, group, 2 * SLOTS, D), live_blocks))
        return result.reshape(count, 2 * SLOTS, D)
    params = (w_qkv.astype(jnp.float32), w_out.astype(jnp.float32), w_up.astype(jnp.float32), w_down.astype(jnp.float32), vectors.astype(jnp.float32), b_up.astype(jnp.float32))
    output, pullback = jax.vjp(whole, to_pairs(rows_input.astype(jnp.float32)), *params)
    grads = pullback(to_pairs(grad_out.astype(jnp.float32)))
    return (from_pairs(output).astype(jnp.bfloat16), from_pairs(grads[0]), grads[1], grads[2], grads[3], grads[4], grads[5], grads[6])
```

```python
import jax
import jax.numpy as jnp
from jax import lax
from jax.experimental import pallas as pl
from jax.experimental.pallas import tpu as pltpu
from jax.sharding import PartitionSpec as P

HEADS = 12
HEAD_DIM = 64
SLOTS = 64
CHUNKS = 4
EPS = 1e-05
NEG = -1000000000.0
FB = 512
LIMIT = 60 * 2**20
F32 = jnp.float32
BF = jnp.bfloat16
ANY = pl.BlockSpec(memory_space=pl.ANY)


def nt(a,b): return lax.dot_general(a,b,(((1,),(1,)),((),())),preferred_element_type=F32)
def nn(a,b): return lax.dot_general(a,b,(((1,),(0,)),((),())),preferred_element_type=F32)
def tn(a,b): return lax.dot_general(a,b,(((0,),(0,)),((),())),preferred_element_type=F32)
def colsum(v): return jnp.sum(v,0,keepdims=True)
VM=pl.BlockSpec(memory_space=pltpu.VMEM)
SM=pl.BlockSpec(memory_space=pltpu.SMEM)

def pulls(pieces, core, first_row, rows, into, sem):
    copies = []
    for which, ref in enumerate(pieces):
        place = core if which == 0 else 1 - core
        for group in range(ref.shape[0]):
            start = pl.multiple_of((2 * group + place) * rows, 8)
            copies.append(
                pltpu.make_async_copy(
                    ref.at[group, pl.ds(first_row, rows), :], into.at[pl.ds(start, rows), :], sem
                )
            )
    return copies


def start_all(copies):
    for copy in copies:
        copy.start()


def wait_whole(into, sem):
    pltpu.make_async_copy(into, into, sem).wait()


def attend_kernel(core_ref, live_ref, own_ref, far_ref, wa_ref, wb_ref, vec_ref, qkv_ref, prob_ref, mixed_ref, sum1_ref, wqkv_ref, wout_ref, sems):
    core = core_ref[0]
    per = 2 * wa_ref.shape[0]
    rq, ro = wqkv_ref.shape[0] // per, wout_ref.shape[0] // per
    start_all(pulls((wa_ref, wb_ref), core, 0, rq, wqkv_ref, sems.at[0]))
    start_all(pulls((wa_ref, wb_ref), core, rq, ro, wout_ref, sems.at[1]))
    wait_whole(wqkv_ref, sems.at[0])
    h,width=own_ref.shape
    seqs=prob_ref.shape[0]; slots=h//seqs
    x=jnp.concatenate([own_ref[...],far_ref[...]],0)
    for part in range(3):
        cols=slice(part*width,(part+1)*width)
        acc=nt(x,wqkv_ref[cols,:])
        if part==0: acc=(acc+vec_ref[0:1,:])
        if part==2: acc=acc+vec_ref[1:2,:]
        qkv_ref[:,cols]=acc.astype(BF)
    lane=lax.broadcasted_iota(jnp.int32,(2*slots,2*HEAD_DIM),1)
    low_half=lane<HEAD_DIM
    key=lax.broadcasted_iota(jnp.int32,(2*slots,4*slots),1)%(2*slots)
    def seq(s,_):
        a=pl.multiple_of(s*slots,slots); b=pl.multiple_of(h+s*slots,slots)
        live_own=live_ref[0,s]; live_far=live_ref[1,s]
        valid=key<jnp.where(key<slots,live_own,live_far+slots)
        for p in range(HEADS//2):
            def take(part):
                c=slice(part*width+p*128,part*width+(p+1)*128)
                return jnp.concatenate([qkv_ref[pl.ds(a,slots),c],qkv_ref[pl.ds(b,slots),c]],0)
            q,k,v=take(0),take(1),take(2)
            zero=jnp.zeros_like(k)
            k2=jnp.concatenate([jnp.where(low_half,k,zero),jnp.where(low_half,zero,k)],0)
            v2=jnp.concatenate([jnp.where(low_half,v,zero),jnp.where(low_half,zero,v)],0)
            sc=jnp.where(valid,nt(q,k2)*(HEAD_DIM**-0.5),NEG)
            halves=[]
            for half in (sc[:,:2*slots],sc[:,2*slots:]):
                e=jnp.exp(half-jnp.max(half,-1,keepdims=True))
                halves.append((e/jnp.sum(e,-1,keepdims=True)).astype(BF))
            prob=jnp.concatenate(halves,1)
            prob_ref[s,p]=prob
            o=nn(prob,v2).astype(BF)
            c=slice(p*128,(p+1)*128)
            mixed_ref[pl.ds(a,slots),c]=o[:slots]
            mixed_ref[pl.ds(b,slots),c]=o[slots:]
        return 0
    lax.fori_loop(0,seqs,seq,0)
    wait_whole(wout_ref, sems.at[1])
    branch=nt(mixed_ref[...],wout_ref[...])
    sum1_ref[...]=x.astype(F32)+branch+vec_ref[2:3,:]

def attend(core,live,own,far,wa,wb,vec):
    h,width=own.shape; seqs=live.shape[1]
    return pl.pallas_call(attend_kernel,
        out_shape=(jax.ShapeDtypeStruct((2*h,3*width),BF),jax.ShapeDtypeStruct((seqs,HEADS//2,128,256),BF),
                   jax.ShapeDtypeStruct((2*h,width),BF),jax.ShapeDtypeStruct((2*h,width),F32)),
        in_specs=[SM,SM,VM,VM,ANY,ANY,VM],out_specs=(VM,)*4,
        scratch_shapes=[pltpu.VMEM((3*width,width),BF),pltpu.VMEM((width,width),BF),pltpu.SemaphoreType.DMA((2,))],
        compiler_params=pltpu.CompilerParams(vmem_limit_bytes=LIMIT),name="attend")(core,live,own,far,wa,wb,vec)

def normed(v):
    c=v-jnp.mean(v,-1,keepdims=True)
    r=lax.rsqrt(jnp.mean(c*c,-1,keepdims=True)+EPS)
    return c*r,r
def norm_back(g,n,r):
    return r*(g-jnp.mean(g,-1,keepdims=True)-n*jnp.mean(g*n,-1,keepdims=True))

def feed_kernel(core_ref,sum1_ref,gown_ref,gfar_ref,ua_ref,ub_ref,da_ref,db_ref,vec_ref,bup_ref,
                yown_ref,yfar_ref,act_ref,dinner_ref,first_ref,dout_ref,dbranch_ref,vsum_ref,bsum_ref,
                wup_ref,wdown_ref,sems,slope_ref,acc_ref,n1_ref):
    h,width=gown_ref.shape; ff=wup_ref.shape[0]
    core = core_ref[0]
    per = 2 * ua_ref.shape[0]
    start_all(pulls((ua_ref, ub_ref), core, 0, ff // per, wup_ref, sems.at[0]))
    start_all(pulls((da_ref, db_ref), core, 0, width // per, wdown_ref, sems.at[1]))
    n1,r1=normed(sum1_ref[...])
    n1_ref[...]=n1
    first=n1*vec_ref[4:5,:]+vec_ref[5:6,:]
    first_ref[...]=first.astype(BF)
    acc_ref[...]=first+vec_ref[3:4,:]
    def up(j,_):
        o=pl.multiple_of(j*FB,FB)
        inner=nt(first_ref[...],wup_ref[pl.ds(o,FB),:])+bup_ref[0:1,pl.ds(o,FB)]
        phi=0.5+0.5*lax.erf(inner*(2**-0.5))
        act=(inner*phi).astype(BF)
        act_ref[:,pl.ds(o,FB)]=act
        slope_ref[:,pl.ds(o,FB)]=(phi+inner*(jnp.exp(-0.5*inner*inner)*0.3989422804014327)).astype(slope_ref.dtype)
        acc_ref[...]+=nt(act,wdown_ref[:,pl.ds(o,FB)])
        return 0
    wait_whole(wup_ref, sems.at[0])
    wait_whole(wdown_ref, sems.at[1])
    lax.fori_loop(0,ff//FB,up,0)
    n2,r2=normed(acc_ref[...])
    y=(n2*vec_ref[6:7,:]+vec_ref[7:8,:]).astype(BF)
    yown_ref[...]=y[:h]; yfar_ref[...]=y[h:]
    g=jnp.concatenate([gown_ref[...],gfar_ref[...]],0).astype(F32)
    vsum_ref[4:5,:]=colsum(g*n2); vsum_ref[5:6,:]=colsum(g)
    dz2=norm_back(g*vec_ref[6:7,:],n2,r2)
    dout=dz2.astype(BF)
    dout_ref[...]=dout
    vsum_ref[1:2,:]=colsum(dz2)
    acc_ref[...]=dz2
    def down(j,_):
        o=pl.multiple_of(j*FB,FB)
        dinner=nn(dout_ref[...],wdown_ref[:,pl.ds(o,FB)])*slope_ref[:,pl.ds(o,FB)].astype(F32)
        bsum_ref[0:1,pl.ds(o,FB)]=colsum(dinner)
        dlow=dinner.astype(BF)
        dinner_ref[:,pl.ds(o,FB)]=dlow
        acc_ref[...]+=nn(dlow,wup_ref[pl.ds(o,FB),:])
        return 0
    lax.fori_loop(0,ff//FB,down,0)
    d=acc_ref[...]; n1=n1_ref[...]
    _,r1=normed(sum1_ref[...])
    vsum_ref[2:3,:]=colsum(d*n1); vsum_ref[3:4,:]=colsum(d)
    dz1=norm_back(d*vec_ref[4:5,:],n1,r1)
    dbranch_ref[...]=dz1.astype(BF)
    vsum_ref[0:1,:]=colsum(dz1)

def feed(core,sum1,gown,gfar,ua,ub,da,db,vec,bup):
    h,width=gown.shape; ff=bup.shape[1]; r=2*h
    S=jax.ShapeDtypeStruct
    return pl.pallas_call(feed_kernel,
        out_shape=(S((h,width),BF),S((h,width),BF),S((r,ff),BF),S((r,ff),BF),S((r,width),BF),S((r,width),BF),S((r,width),BF),S((8,width),F32),S((1,ff),F32)),
        in_specs=[SM,VM,VM,VM,ANY,ANY,ANY,ANY,VM,VM],out_specs=(VM,)*9,
        scratch_shapes=[pltpu.VMEM((ff,width),BF),pltpu.VMEM((width,ff),BF),pltpu.SemaphoreType.DMA((2,)),pltpu.VMEM((r,ff),BF),pltpu.VMEM((r,width),F32),pltpu.VMEM((r,width),F32)],
        compiler_params=pltpu.CompilerParams(vmem_limit_bytes=LIMIT),name="feed")(core,sum1,gown,gfar,ua,ub,da,db,vec,bup)

def back_kernel(core_ref,dbranch_ref,qkv_ref,prob_ref,wa_ref,wb_ref,dqkv_ref,dxown_ref,dxfar_ref,vsum_ref,wqkv_ref,wout_ref,sems,dmix_ref):
    r,width=dbranch_ref.shape; h=r//2
    core = core_ref[0]
    per = 2 * wa_ref.shape[0]
    rq, ro = wqkv_ref.shape[0] // per, wout_ref.shape[0] // per
    start_all(pulls((wa_ref, wb_ref), core, rq, ro, wout_ref, sems.at[1]))
    start_all(pulls((wa_ref, wb_ref), core, 0, rq, wqkv_ref, sems.at[0]))
    wait_whole(wout_ref, sems.at[1])
    seqs=prob_ref.shape[0]; slots=h//seqs
    dmix_ref[...]=nn(dbranch_ref[...],wout_ref[...]).astype(BF)
    lane=lax.broadcasted_iota(jnp.int32,(2*slots,2*HEAD_DIM),1)
    low_half=lane<HEAD_DIM
    def seq(s,_):
        a=pl.multiple_of(s*slots,slots); b=pl.multiple_of(h+s*slots,slots)
        for p in range(HEADS//2):
            def rows(ref,part):
                c=slice(part*width+p*128,part*width+(p+1)*128)
                return jnp.concatenate([ref[pl.ds(a,slots),c],ref[pl.ds(b,slots),c]],0)
            q,k,v=rows(qkv_ref,0),rows(qkv_ref,1),rows(qkv_ref,2)
            do=rows(dmix_ref,0)
            zero=jnp.zeros_like(k)
            k2=jnp.concatenate([jnp.where(low_half,k,zero),jnp.where(low_half,zero,k)],0)
            v2=jnp.concatenate([jnp.where(low_half,v,zero),jnp.where(low_half,zero,v)],0)
            prob=prob_ref[s,p]
            dp=nt(do,v2)
            pf=prob.astype(F32)
            halves=[]
            for u in range(2):
                c=slice(u*2*slots,(u+1)*2*slots)
                w=pf[:,c]*dp[:,c]
                halves.append((w-pf[:,c]*jnp.sum(w,-1,keepdims=True)).astype(BF))
            ds=jnp.concatenate(halves,1)
            sc=HEAD_DIM**-0.5
            dq=nn(ds,k2)*sc
            dk=tn(ds,q)*sc
            dv=tn(prob,do)
            dk=jnp.where(low_half,dk[:2*slots],dk[2*slots:])
            dv=jnp.where(low_half,dv[:2*slots],dv[2*slots:])
            for part,val in enumerate((dq,dk,dv)):
                c=slice(part*width+p*128,part*width+(p+1)*128)
                dqkv_ref[pl.ds(a,slots),c]=val[:slots].astype(BF)
                dqkv_ref[pl.ds(b,slots),c]=val[slots:].astype(BF)
        return 0
    lax.fori_loop(0,seqs,seq,0)
    wait_whole(wqkv_ref, sems.at[0])
    dx=dbranch_ref[...].astype(F32)+nn(dqkv_ref[...],wqkv_ref[...])
    dxown_ref[...]=dx[:h]; dxfar_ref[...]=dx[h:].astype(BF)
    vsum_ref[...]=jnp.zeros_like(vsum_ref)
    vsum_ref[0:1,:]=colsum(dqkv_ref[:,:width].astype(F32))
    vsum_ref[1:2,:]=colsum(dqkv_ref[:,2*width:].astype(F32))

def back(core,dbranch,qkv,prob,wa,wb):
    r,width=dbranch.shape; h=r//2
    S=jax.ShapeDtypeStruct
    return pl.pallas_call(back_kernel,
        out_shape=(S((r,3*width),BF),S((h,width),F32),S((h,width),BF),S((8,width),F32)),
        in_specs=[SM,VM,VM,VM,ANY,ANY],out_specs=(VM,)*4,
        scratch_shapes=[pltpu.VMEM((3*width,width),BF),pltpu.VMEM((width,width),BF),pltpu.SemaphoreType.DMA((2,)),pltpu.VMEM((r,width),BF)],
        compiler_params=pltpu.CompilerParams(vmem_limit_bytes=LIMIT),name="back")(core,dbranch,qkv,prob,wa,wb)

def bits_of(axis):
    return (lax.axis_size(axis) - 1).bit_length()


def swapped(values, axis, mask):
    count = lax.axis_size(axis)
    return lax.ppermute(values, axis, [(i, i ^ mask) for i in range(count)])


def bit_at(axis, bit):
    return (lax.axis_index(axis) >> bit) & 1


def stages(pair_first):
    mod_bits = bits_of("mod")
    top = [("mod", bit) for bit in range(mod_bits - 1, 1, -1)]
    low = [("mod", 1)]
    pairs = [("pair", bit) for bit in range(bits_of("pair"))]
    return top + (pairs + low if pair_first else low + pairs)


def gather(slab, pair_first):
    held = slab
    depth = 0
    for axis, bit in stages(pair_first):
        other = swapped(held, axis, 1 << bit)
        upper = bit_at(axis, bit) == 1
        first, second = jnp.where(upper, other, held), jnp.where(upper, held, other)
        if axis == "mod":
            held = jnp.stack([first, second], depth)
            depth += 1
        else:
            held = jnp.concatenate([first, second], -1)
    held = held.reshape((-1,) + held.shape[depth:])
    return held, swapped(held, "mod", 1)


def scatter_sum(keep, send, pair_first):
    steps = stages(pair_first)
    depth = sum(axis == "mod" for axis, bit in steps)
    lead = (2,) * depth
    held = keep.reshape(lead + keep.shape[1:])
    came = swapped(send, "mod", 1).reshape(held.shape)
    for axis, bit in reversed(steps):
        mine = bit_at(axis, bit)
        if axis == "mod":
            depth -= 1
            dim, size = depth, 1
        else:
            dim = held.ndim - 1
            size = held.shape[-1] // 2

        def part(values, which):
            return lax.dynamic_slice_in_dim(values, which * size, size, dim)

        away = (part(held, 1 - mine).astype(F32) + part(came, 1 - mine).astype(F32)).astype(BF)
        held = part(held, mine).astype(F32) + part(came, mine).astype(F32)
        came = swapped(away, axis, 1 << bit)
    return (held + came.astype(F32)).reshape(held.shape[-2:])


def split_cores(full, core, groups):
    view = full.reshape(groups, 2, -1, full.shape[-1])
    keep = lax.dynamic_index_in_dim(view, core, 1, keepdims=False)
    send = lax.dynamic_index_in_dim(view, 1 - core, 1, keepdims=False)
    return keep, send


def per_device(rows_input, grad_out, w_qkv, w_out, w_up, w_down, vectors, b_up, live_rows):
    mod_size = lax.axis_size("mod")
    pair_size = lax.axis_size("pair")
    groups = mod_size // 2
    half = mod_size // 2
    rows, width = rows_input.shape
    moved = rows // 2
    step = moved // CHUNKS
    seqs = step // SLOTS
    place = lax.axis_index("mod")
    upper = place >= half
    core = place & 1
    core_ref = core.reshape(1)
    own_start = jnp.where(upper, moved, 0)
    away_start = jnp.where(upper, 0, moved)

    def over(values):
        return swapped(values, "mod", half)

    own_rows, far_rows = [], []
    live_own = lax.dynamic_slice_in_dim(live_rows, own_start // SLOTS, moved // SLOTS)
    live_far = over(lax.dynamic_slice_in_dim(live_rows, away_start // SLOTS, moved // SLOTS))
    live = jnp.stack([live_own, live_far])
    for c in range(CHUNKS):
        own_rows.append(lax.dynamic_slice_in_dim(rows_input, own_start + c * step, step))
        far_rows.append(over(lax.dynamic_slice_in_dim(rows_input, away_start + c * step, step)))

    small = jnp.concatenate([vectors.reshape(-1), b_up.reshape(-1)])
    line = w_qkv.shape[0]
    small_rows = -(-small.shape[0] // line)
    small = jnp.pad(small, (0, 16 * line - small.shape[0])).reshape(16, line)
    proj_slab = jnp.concatenate([w_qkv.T, w_out.T, small], 0)
    wa, wb = gather(proj_slab, True)
    tiny_at = w_qkv.shape[1] + w_out.shape[1]
    tiny_a = wa[:, tiny_at : tiny_at + small_rows].reshape(groups, small_rows, pair_size, line)
    tiny_b = wb[:, tiny_at : tiny_at + small_rows].reshape(groups, small_rows, pair_size, line)
    flip = core == 1
    tiny = jnp.stack([jnp.where(flip, tiny_b, tiny_a), jnp.where(flip, tiny_a, tiny_b)], 1)
    tiny = tiny.reshape(mod_size, small_rows, pair_size, line).transpose(2, 0, 1, 3).reshape(pair_size, mod_size, -1)
    count = vectors.size
    vec = tiny[:, :, :count].reshape((pair_size, mod_size) + vectors.shape).transpose(0, 2, 1, 3)
    vec = vec.reshape(8, width).astype(F32)
    bup = tiny[:, :, count : count + b_up.size].reshape((pair_size, mod_size) + b_up.shape).transpose(0, 2, 1, 3)
    bup = bup.reshape(1, -1).astype(F32)

    ua, ub = gather(w_up.T, False)
    da, db = gather(w_down.T, True)

    own_grads, far_grads = [], []
    for c in range(CHUNKS):
        own_grads.append(lax.dynamic_slice_in_dim(grad_out, own_start + c * step, step))
        far_grads.append(over(lax.dynamic_slice_in_dim(grad_out, away_start + c * step, step)))

    result = jnp.zeros((rows, width), BF)
    input_grad = jnp.zeros((rows, width), F32)
    kept = []
    for c in range(CHUNKS):
        kept.append(attend(core_ref, live[:, c * seqs : (c + 1) * seqs], own_rows[c], far_rows[c], wa, wb, vec))
    fed, backed = [], []
    for c in range(CHUNKS):
        qkv, prob, mixed, sum1 = kept[c]
        out = feed(core_ref, sum1, own_grads[c], far_grads[c], ua, ub, da, db, vec, bup)
        fed.append(out)
        result = lax.dynamic_update_slice_in_dim(result, out[0], own_start + c * step, 0)
        result = lax.dynamic_update_slice_in_dim(result, over(out[1]), away_start + c * step, 0)
        dqkv, dx_own, dx_far, vsum = back(core_ref, out[6], qkv, prob, wa, wb)
        backed.append((dqkv, vsum))
        input_grad = lax.dynamic_update_slice_in_dim(input_grad, dx_own, own_start + c * step, 0)
        input_grad = lax.dynamic_update_slice_in_dim(input_grad, over(dx_far).astype(F32), away_start + c * step, 0)

    def joined(parts):
        return jnp.concatenate(parts, 0)

    def weight(left, right, pair_first):
        full = tn(joined(left), joined(right)).astype(BF)
        keep, send = split_cores(full, core, groups)
        return scatter_sum(keep, send, pair_first).T

    both = [jnp.concatenate([a, b], 0) for a, b in zip(own_rows, far_rows)]
    g_up = weight([f[3] for f in fed], [f[4] for f in fed], False)
    g_down = weight([f[5] for f in fed], [f[2] for f in fed], True)
    g_out = weight([f[6] for f in fed], [k[2] for k in kept], False)
    g_qkv = weight([b[0] for b in backed], both, True)

    vec_sum = sum(f[7] for f in fed)
    qv_sum = sum(b[1] for b in backed)
    bup_sum = sum(f[8] for f in fed)
    vec_grad = jnp.concatenate([qv_sum[:2], vec_sum[:6]], 0).reshape(pair_size, -1, mod_size, vectors.shape[1])
    bup_grad = bup_sum.reshape(pair_size, -1, mod_size, b_up.shape[1])
    tiny_grad = jnp.concatenate(
        [vec_grad.transpose(2, 0, 1, 3).reshape(mod_size, pair_size, -1), bup_grad.transpose(2, 0, 1, 3).reshape(mod_size, pair_size, -1)], -1
    )
    tiny_sum = lax.psum(tiny_grad.astype(BF), ("mod", "pair"))
    tiny_mine = tiny_sum[place, lax.axis_index("pair")].astype(F32)
    g_vec = tiny_mine[: vectors.size].reshape(vectors.shape)
    g_bup = tiny_mine[vectors.size :].reshape(b_up.shape)
    return (result, input_grad, g_qkv, g_out, g_up, g_down, g_vec, g_bup)


def solution(mesh):
    sharded = P("pair", "mod")
    spread = P(("mod", "pair"), None)
    weights = (sharded,) * 6
    return jax.shard_map(
        per_device,
        mesh=mesh,
        in_specs=(spread, spread) + weights + (P(("mod", "pair")),),
        out_specs=(spread, spread) + weights,
        check_vma=False,
    )
```

```python
import functools

import jax
import jax.numpy as jnp
from jax import lax
from jax.experimental import pallas as pl
from jax.experimental.pallas import tpu as pltpu
from jax.sharding import PartitionSpec as P

HEADS = 12
HEAD_DIM = 64
SLOTS = 64
CHUNKS = 4
X_UNITS = (1, 1, 1, 1)
ATTENDS_BEFORE = (0, 2)
FEED_UNITS = (1, 1, 2)
Y_UNITS = (2, 2)
BACK_UNITS = (1, 1, 1, 1)
DX_UNITS = (1, 1, 1, 1)
BLOCKS = 4
EPS = 1e-05
NEG = -1000000000.0
LIMIT = 60 * 2**20
F32 = jnp.float32
BF = jnp.bfloat16
ANY = pl.BlockSpec(memory_space=pl.ANY)
VM = pl.BlockSpec(memory_space=pltpu.VMEM)
SM = pl.BlockSpec(memory_space=pltpu.SMEM)
S = jax.ShapeDtypeStruct
QUICK = pl.CostEstimate(flops=1, bytes_accessed=1, transcendentals=0)
SLOW = pl.CostEstimate(flops=10**10, bytes_accessed=30 * 10**6, transcendentals=0)
DMA = pltpu.SemaphoreType.DMA


def nt(a, b):
    return lax.dot_general(a, b, (((1,), (1,)), ((), ())), preferred_element_type=F32)


def nn(a, b):
    return lax.dot_general(a, b, (((1,), (0,)), ((), ())), preferred_element_type=F32)


def tn(a, b):
    return lax.dot_general(a, b, (((0,), (0,)), ((), ())), preferred_element_type=F32)


def colsum(v):
    return jnp.sum(v, 0, keepdims=True)


def copy(src, dst, sem):
    pltpu.make_async_copy(src, dst, sem).start()


def wait_for(ref, sem):
    pltpu.make_async_copy(ref, ref, sem).wait()


def pull(where, views, part, into, sem):
    core, low, side = where[0], where[1], where[2]
    for piece, (dc, dy, dx) in views:
        slab = (low ^ dy) * 2 + (core ^ dc)
        cols = piece.shape[-1]
        lane = pl.multiple_of((side ^ dx) * cols, cols)
        mid = (slice(None),) * (len(into.shape) - 3)
        copy(piece.at[:, part], into.at[(slice(None), slab) + mid + (pl.ds(lane, cols),)], sem)


def proj_views(refs):
    return [(ref.at[2 * dy + dx], (dc, dy, dx)) for dc, ref in enumerate(refs) for dy in (0, 1) for dx in (0, 1)]


def wide_views(refs):
    first, second = [], []
    for dc in (0, 1):
        for later in (0, 1):
            for early in (0, 1):
                first.append((refs[4 * dc + later].at[early], (dc, later, early)))
                second.append((refs[4 * dc + 2 + later].at[early], (dc, early, later)))
    return first, second


def attend_kernel(c, skip, where, live, rows, far, vec, *refs):
    views, refs = proj_views(refs[:2]), refs[-11:]
    qkv_all, prob_all, mixed_all, x_all, done, wqkv, xs, qkv, prob, mixed, sems = refs
    r, width = xs.shape
    h = r // 2
    seqs = prob.shape[0]
    done[...] = jnp.zeros_like(done)
    start = pl.multiple_of(where[3] + c * h, h)
    copy(rows.at[pl.ds(start, h)], xs.at[pl.ds(0, h)], sems.at[0])
    copy(far.at[pl.ds(skip * h, h)], xs.at[pl.ds(h, h)], sems.at[0])
    pull(where, views, pl.ds(0, wqkv.shape[2]), wqkv, sems.at[1])
    wait_for(xs, sems.at[0])
    span = pl.ds(c * r, r)
    copy(xs, x_all.at[span], sems.at[2])
    wait_for(wqkv, sems.at[1])
    flat = wqkv.reshape(3 * width, width)
    x = xs[...]
    for part in range(3):
        cols = slice(part * width, (part + 1) * width)
        acc = nt(x, flat[cols, :])
        if part == 0:
            acc = acc + vec[0:1, :]
        if part == 2:
            acc = acc + vec[1:2, :]
        qkv[:, cols] = acc.astype(BF)
    copy(qkv, qkv_all.at[span], sems.at[3])
    lane = lax.broadcasted_iota(jnp.int32, (2 * SLOTS, 2 * HEAD_DIM), 1)
    low_half = lane < HEAD_DIM
    key = lax.broadcasted_iota(jnp.int32, (2 * SLOTS, 4 * SLOTS), 1) % (2 * SLOTS)

    def seq(s, carry):
        a = pl.multiple_of(s * SLOTS, SLOTS)
        b = pl.multiple_of(h + s * SLOTS, SLOTS)
        at = c * seqs + s
        valid = key < jnp.where(key < SLOTS, live[0, at], live[1, at] + SLOTS)
        for p in range(HEADS // 2):

            def take(part):
                cols = slice(part * width + p * 128, part * width + (p + 1) * 128)
                return jnp.concatenate([qkv[pl.ds(a, SLOTS), cols], qkv[pl.ds(b, SLOTS), cols]], 0)

            q, k, v = take(0), take(1), take(2)
            zero = jnp.zeros_like(k)
            k2 = jnp.concatenate([jnp.where(low_half, k, zero), jnp.where(low_half, zero, k)], 0)
            v2 = jnp.concatenate([jnp.where(low_half, v, zero), jnp.where(low_half, zero, v)], 0)
            score = jnp.where(valid, nt(q, k2) * (HEAD_DIM**-0.5), NEG)
            halves = []
            for one in (score[:, : 2 * SLOTS], score[:, 2 * SLOTS :]):
                e = jnp.exp(one - jnp.max(one, -1, keepdims=True))
                halves.append((e / jnp.sum(e, -1, keepdims=True)).astype(BF))
            both = jnp.concatenate(halves, 1)
            prob[s, p] = both
            o = nn(both, v2).astype(BF)
            cols = slice(p * 128, (p + 1) * 128)
            mixed[pl.ds(a, SLOTS), cols] = o[:SLOTS]
            mixed[pl.ds(b, SLOTS), cols] = o[SLOTS:]
        copy(prob.at[s], prob_all.at[at], sems.at[4])
        return carry

    lax.fori_loop(0, seqs, seq, 0)
    copy(mixed, mixed_all.at[span], sems.at[5])
    wait_for(xs, sems.at[2])
    wait_for(qkv, sems.at[3])
    wait_for(prob, sems.at[4])
    wait_for(mixed, sems.at[5])


def attend(c, skip, where, live, rows, far, vec, pieces, before, tokens):
    width = far.shape[1]
    total = rows.shape[0]
    r = total // CHUNKS
    seqs = r // 2 // SLOTS
    groups = pieces[0].shape[1]
    per = 3 * width // (4 * groups)
    shapes = (
        S((total, 3 * width), BF),
        S((CHUNKS * seqs, HEADS // 2, 2 * SLOTS, 4 * SLOTS), BF),
        S((total, width), BF),
        S((total, width), BF),
    )
    return pl.pallas_call(
        functools.partial(attend_kernel, c, skip),
        out_shape=shapes + (S((8, 128), F32),),
        in_specs=[SM, SM, ANY, ANY, VM] + [ANY] * (2 + len(before) + len(tokens)),
        out_specs=(ANY,) * 4 + (VM,),
        input_output_aliases={7 + i: i for i in range(len(before))},
        scratch_shapes=[
            pltpu.VMEM((groups, 4, per, width), BF),
            pltpu.VMEM((r, width), BF),
            pltpu.VMEM((r, 3 * width), BF),
            pltpu.VMEM((seqs,) + shapes[1].shape[1:], BF),
            pltpu.VMEM((r, width), BF),
            DMA((6,)),
        ],
        compiler_params=pltpu.CompilerParams(vmem_limit_bytes=LIMIT),
        cost_estimate=SLOW,
        name="attend",
    )(where, live, rows, far, vec, *pieces, *before, *tokens)


def normed(v):
    c = v - jnp.mean(v, -1, keepdims=True)
    r = lax.rsqrt(jnp.mean(c * c, -1, keepdims=True) + EPS)
    return c * r, r


def norm_back(g, n, r):
    return r * (g - jnp.mean(g, -1, keepdims=True) - n * jnp.mean(g * n, -1, keepdims=True))


def feed_kernel(c0, subs, skip, sides, where, grads, far, x_all, mixed_all, vec, bup, *refs):
    first_views, second_views = wide_views(refs[:8])
    refs = refs[-27:]
    outs, sums, refs = refs[:8], refs[8:10], refs[10:]
    y_all, act_all, dinner_all, first_all, dout_all, dbranch_all, dmix_all, y_far = outs
    vsum, bsum = sums
    wout, wup, wdown, xs, mixed, gs, ys, act, slope, dinner, first, dout, dbranch, dmix, acc, n1, sems = refs
    r, width = xs.shape
    h = r // 2
    pull(where, first_views, pl.ds(0, 1), wout, sems.at[0])
    pull(where, first_views, pl.ds(1, BLOCKS), wup, sems.at[1])
    pull(where, second_views, pl.ds(0, BLOCKS), wdown, sems.at[2])
    out_flat = wout.reshape(width, width)
    ff = BLOCKS * width
    up_flat = wup.reshape(ff, width)
    step = width // sides

    def up_block(b):
        parts = [up_flat[pl.ds(side * BLOCKS * step + b * step, step), :] for side in range(sides)]
        return jnp.concatenate(parts, 0)

    def down_block(b):
        return wdown[:, :, b].reshape(width, width)

    for t in range(subs):
        c = c0 + t
        span = pl.ds(c * r, r)
        start = pl.multiple_of(where[3] + c * h, h)
        ins = (
            pltpu.make_async_copy(x_all.at[span], xs, sems.at[3]),
            pltpu.make_async_copy(mixed_all.at[span], mixed, sems.at[3]),
            pltpu.make_async_copy(grads.at[pl.ds(start, h)], gs.at[pl.ds(0, h)], sems.at[4]),
            pltpu.make_async_copy(far.at[pl.ds(t * h, h)], gs.at[pl.ds(h, h)], sems.at[4]),
        )
        for one in ins:
            one.start()
        wait_for(xs, sems.at[3])
        wait_for(mixed, sems.at[3])
        if t == 0:
            wait_for(wout, sems.at[0])
        sum1 = xs[...].astype(F32) + nt(mixed[...], out_flat[...]) + vec[2:3, :]
        hat, r1 = normed(sum1)
        n1[...] = hat
        top = hat * vec[4:5, :] + vec[5:6, :]
        if t:
            for ref in (act, dinner, first, dout, dbranch, dmix, ys):
                wait_for(ref, sems.at[5])
        first[...] = top.astype(BF)
        copy(first, first_all.at[span], sems.at[5])
        acc[...] = top + vec[3:4, :]
        if t == 0:
            wait_for(wup, sems.at[1])
            wait_for(wdown, sems.at[2])
        for b in range(BLOCKS):
            cols = slice(b * width, (b + 1) * width)
            inner = nt(first[...], up_block(b)) + bup[b : b + 1, :]
            phi = 0.5 + 0.5 * lax.erf(inner * (2**-0.5))
            low = (inner * phi).astype(BF)
            act[:, cols] = low
            copy(act.at[:, cols], act_all.at[span, cols], sems.at[5])
            slope[:, cols] = (phi + inner * (jnp.exp(-0.5 * inner * inner) * 0.3989422804014327)).astype(BF)
            acc[...] += nt(low, down_block(b))
        n2, r2 = normed(acc[...])
        ys[...] = (n2 * vec[6:7, :] + vec[7:8, :]).astype(BF)
        copy(ys.at[pl.ds(0, h)], y_all.at[pl.ds(start, h)], sems.at[5])
        copy(ys.at[pl.ds(h, h)], y_far.at[pl.ds((skip + t) * h, h)], sems.at[5])
        wait_for(gs, sems.at[4])
        g = gs[...].astype(F32)
        sums_of = [None] * 6
        sums_of[4] = colsum(g * n2)
        sums_of[5] = colsum(g)
        dz2 = norm_back(g * vec[6:7, :], n2, r2)
        dout[...] = dz2.astype(BF)
        copy(dout, dout_all.at[span], sems.at[5])
        sums_of[1] = colsum(dz2)
        acc[...] = dz2
        for b in range(BLOCKS):
            cols = slice(b * width, (b + 1) * width)
            grad = nn(dout[...], down_block(b)) * slope[:, cols].astype(F32)
            part = colsum(grad)
            bsum[0:1, cols] = part if t == 0 else bsum[0:1, cols] + part
            low = grad.astype(BF)
            dinner[:, cols] = low
            copy(dinner.at[:, cols], dinner_all.at[span, cols], sems.at[5])
            acc[...] += nn(low, up_block(b))
        d = acc[...]
        hat = n1[...]
        sums_of[2] = colsum(d * hat)
        sums_of[3] = colsum(d)
        dz1 = norm_back(d * vec[4:5, :], hat, r1)
        sums_of[0] = colsum(dz1)
        low = dz1.astype(BF)
        dbranch[...] = low
        copy(dbranch, dbranch_all.at[span], sems.at[5])
        dmix[...] = nn(low, out_flat[...]).astype(BF)
        copy(dmix, dmix_all.at[span], sems.at[5])
        for i, part in enumerate(sums_of):
            vsum[i : i + 1, :] = part if t == 0 else vsum[i : i + 1, :] + part
    for ref in (act, dinner, first, dout, dbranch, dmix, ys):
        wait_for(ref, sems.at[5])


def feed(c0, subs, skip, y_rows, sides, where, grads, far, x_all, mixed_all, vec, bup, pieces, before, tokens):
    total, width = x_all.shape
    r = total // CHUNKS
    ff = BLOCKS * width
    groups, thin = pieces[0].shape[1], pieces[0].shape[3]
    shapes = (
        S(grads.shape, BF),
        S((total, ff), BF),
        S((total, ff), BF),
        S((total, width), BF),
        S((total, width), BF),
        S((total, width), BF),
        S((total, width), BF),
    )
    return pl.pallas_call(
        functools.partial(feed_kernel, c0, subs, skip, sides),
        out_shape=shapes + (S((y_rows, width), BF), S((8, width), F32), S((1, ff), F32)),
        in_specs=[SM, ANY, ANY, ANY, ANY, VM, VM] + [ANY] * (8 + len(before) + len(tokens)),
        out_specs=(ANY,) * 8 + (VM,) * 2,
        input_output_aliases={15 + i: i for i in range(len(before))},
        scratch_shapes=[
            pltpu.VMEM((groups, 4, 1, thin, width), BF),
            pltpu.VMEM((groups, 4, BLOCKS, thin, width), BF),
            pltpu.VMEM((groups, 4, BLOCKS, thin, width), BF),
            pltpu.VMEM((r, width), BF),
            pltpu.VMEM((r, width), BF),
            pltpu.VMEM((r, width), BF),
            pltpu.VMEM((r, width), BF),
            pltpu.VMEM((r, ff), BF),
            pltpu.VMEM((r, ff), BF),
            pltpu.VMEM((r, ff), BF),
            pltpu.VMEM((r, width), BF),
            pltpu.VMEM((r, width), BF),
            pltpu.VMEM((r, width), BF),
            pltpu.VMEM((r, width), BF),
            pltpu.VMEM((r, width), F32),
            pltpu.VMEM((r, width), F32),
            DMA((6,)),
        ],
        compiler_params=pltpu.CompilerParams(vmem_limit_bytes=LIMIT),
        cost_estimate=QUICK,
        name="feed",
    )(where, grads, far, x_all, mixed_all, vec, bup, *pieces, *before, *tokens)


def back_kernel(c0, skip, where, qkv_all, prob_all, dbranch_all, dmix_all, *refs):
    views, refs = proj_views(refs[:2]), refs[-13:]
    dx_all, dqkv_all, dx_far, vsum, wqkv, qkv, prob, dbranch, dmix, dqkv, dxs, dxf, sems = refs
    r, width = dbranch.shape
    h = dx_all.shape[0] // (2 * CHUNKS)
    subs = r // (2 * h)
    seqs = h // SLOTS
    span = pl.ds(c0 * 2 * h, r)
    copy(qkv_all.at[span], qkv, sems.at[0])
    copy(dmix_all.at[span], dmix, sems.at[1])
    copy(prob_all.at[pl.ds(c0 * seqs, subs * seqs)], prob, sems.at[2])
    pull(where, views, pl.ds(0, wqkv.shape[2]), wqkv, sems.at[3])
    copy(dbranch_all.at[span], dbranch, sems.at[4])
    wait_for(qkv, sems.at[0])
    wait_for(dmix, sems.at[1])
    wait_for(prob, sems.at[2])
    lane = lax.broadcasted_iota(jnp.int32, (2 * SLOTS, 2 * HEAD_DIM), 1)
    low_half = lane < HEAD_DIM

    def seq(t, s):
        a = pl.multiple_of(2 * h * t + s * SLOTS, SLOTS)
        b = pl.multiple_of(2 * h * t + h + s * SLOTS, SLOTS)
        for p in range(HEADS // 2):

            def take(ref, part):
                cols = slice(part * width + p * 128, part * width + (p + 1) * 128)
                return jnp.concatenate([ref[pl.ds(a, SLOTS), cols], ref[pl.ds(b, SLOTS), cols]], 0)

            q, k, v = take(qkv, 0), take(qkv, 1), take(qkv, 2)
            do = take(dmix, 0)
            zero = jnp.zeros_like(k)
            k2 = jnp.concatenate([jnp.where(low_half, k, zero), jnp.where(low_half, zero, k)], 0)
            v2 = jnp.concatenate([jnp.where(low_half, v, zero), jnp.where(low_half, zero, v)], 0)
            both = prob[t * seqs + s, p]
            dp = nt(do, v2)
            wide = both.astype(F32)
            halves = []
            for u in range(2):
                cols = slice(u * 2 * SLOTS, (u + 1) * 2 * SLOTS)
                w = wide[:, cols] * dp[:, cols]
                halves.append((w - wide[:, cols] * jnp.sum(w, -1, keepdims=True)).astype(BF))
            ds = jnp.concatenate(halves, 1)
            scale = HEAD_DIM**-0.5
            dq = nn(ds, k2) * scale
            dk = tn(ds, q) * scale
            dv = tn(both, do)
            dk = jnp.where(low_half, dk[: 2 * SLOTS], dk[2 * SLOTS :])
            dv = jnp.where(low_half, dv[: 2 * SLOTS], dv[2 * SLOTS :])
            for part, val in enumerate((dq, dk, dv)):
                cols = slice(part * width + p * 128, part * width + (p + 1) * 128)
                dqkv[pl.ds(a, SLOTS), cols] = val[:SLOTS].astype(BF)
                dqkv[pl.ds(b, SLOTS), cols] = val[SLOTS:].astype(BF)

    vsum[...] = jnp.zeros_like(vsum)
    for t in range(subs):
        chunk = pl.ds(t * 2 * h, 2 * h)

        def step(s, carry, t=t):
            seq(t, s)
            return carry

        lax.fori_loop(0, seqs, step, 0)
        copy(dqkv.at[chunk], dqkv_all.at[pl.ds((c0 + t) * 2 * h, 2 * h)], sems.at[5])
        if t == 0:
            wait_for(wqkv, sems.at[3])
            wait_for(dbranch, sems.at[4])
        mine = dqkv[chunk]
        dx = dbranch[chunk].astype(F32) + nn(mine, wqkv.reshape(3 * width, width)[...])
        dxs[t * h : (t + 1) * h, :] = dx[:h]
        start = pl.multiple_of(where[3] + (c0 + t) * h, h)
        copy(dxs.at[pl.ds(t * h, h)], dx_all.at[pl.ds(start, h)], sems.at[6])
        dxf[t * h : (t + 1) * h, :] = dx[h:].astype(BF)
        copy(dxf.at[pl.ds(t * h, h)], dx_far.at[pl.ds((skip + t) * h, h)], sems.at[7])
        vsum[0:1, :] += colsum(mine[:, :width].astype(F32))
        vsum[1:2, :] += colsum(mine[:, 2 * width :].astype(F32))
    wait_for(dqkv, sems.at[5])
    wait_for(dxs, sems.at[6])
    wait_for(dxf, sems.at[7])


def back(c0, subs, skip, dx_rows, where, rows, qkv_all, prob_all, dbranch_all, dmix_all, pieces, before, tokens):
    total, width = dbranch_all.shape
    r = subs * total // CHUNKS
    h = r // 2
    seqs = h // SLOTS
    groups = pieces[0].shape[1]
    per = 3 * width // (4 * groups)
    return pl.pallas_call(
        functools.partial(back_kernel, c0, skip),
        out_shape=(S((rows, width), F32), S((total, 3 * width), BF), S((dx_rows, width), BF), S((8, width), F32)),
        in_specs=[SM] + [ANY] * (6 + len(before) + len(tokens)),
        out_specs=(ANY, ANY, ANY, VM),
        input_output_aliases={7 + i: i for i in range(len(before))},
        scratch_shapes=[
            pltpu.VMEM((groups, 4, per, width), BF),
            pltpu.VMEM((r, 3 * width), BF),
            pltpu.VMEM((seqs,) + prob_all.shape[1:], BF),
            pltpu.VMEM((r, width), BF),
            pltpu.VMEM((r, width), BF),
            pltpu.VMEM((r, 3 * width), BF),
            pltpu.VMEM((h, width), F32),
            pltpu.VMEM((h, width), BF),
            DMA((8,)),
        ],
        compiler_params=pltpu.CompilerParams(vmem_limit_bytes=LIMIT),
        cost_estimate=QUICK,
        name="back",
    )(where, qkv_all, prob_all, dbranch_all, dmix_all, *pieces, *before, *tokens)


def put(buf, where, mod, value, dims, by_pair=False):
    core, low, side = where[0], where[1], where[2]
    cols = buf.shape[-1]
    dc = core ^ (mod & 1)
    dy = low ^ ((mod >> 1) & 1)
    for half in range(2):
        dx = side ^ half
        at = dx * 2 + dy if by_pair else dy * 2 + dx
        buf[(dc, at, mod >> 2) + dims] = value[..., half * cols : (half + 1) * cols]


def hand_over(bufs, outs, sems):
    copies = []
    for i, buf in enumerate(bufs):
        for dc in (1, 0):
            at = 2 * i + dc
            copies.append(pltpu.make_async_copy(buf.at[dc], outs[at], sems.at[at]))
    for one in copies:
        one.start()
    for one in copies:
        one.wait()


def wide_grads_kernel(sides, where, dinner, act, first, dout, dbranch, mixed, *refs):
    outs, (one, two, sems) = refs[-7:-3], refs[-3:]
    b = pl.program_id(0)
    width = first.shape[1]
    thin = one.shape[4]
    mods = 4 * one.shape[2]

    @pl.when(b == 0)
    def _():
        whole = tn(dbranch[...], mixed[...]).astype(BF)
        for mod in range(mods):
            put(one, where, mod, whole[mod * thin : (mod + 1) * thin], (0,))

    up = tn(dinner[...], first[...]).astype(BF)
    step = width // sides
    tall = BLOCKS * thin
    for side in range(sides):
        for i in range(step // tall):
            mod = side * BLOCKS * step // tall + b * (step // tall) + i
            rows = slice(side * step + i * tall, side * step + (i + 1) * tall)
            put(one, where, mod, up[rows].reshape(BLOCKS, thin, width), (pl.ds(1, BLOCKS),))
    down = tn(dout[...], act[...]).astype(BF)
    for mod in range(mods):
        put(two, where, mod, down[mod * thin : (mod + 1) * thin], (b,), True)

    @pl.when(b == BLOCKS - 1)
    def _():
        hand_over((one, two), outs, sems)


def wide_grads(sides, where, dinner, act, first, dout, dbranch, mixed, groups, tokens):
    total, width = first.shape
    thin = width // (4 * groups)
    shapes = [(4, groups, 1 + BLOCKS, thin, width // 2), (4, groups, BLOCKS, thin, width // 2)]

    def whole(array):
        return pl.BlockSpec(array.shape, lambda b: (0, 0), pipeline_mode=pl.Buffered(1))

    block = pl.BlockSpec((total, width), lambda b: (0, b))
    return pl.pallas_call(
        functools.partial(wide_grads_kernel, sides),
        grid=(BLOCKS,),
        out_shape=(S(shapes[0], BF),) * 2 + (S(shapes[1], BF),) * 2,
        in_specs=[SM, block, block, whole(first), whole(dout), whole(dbranch), whole(mixed)] + [ANY] * len(tokens),
        out_specs=(ANY,) * 4,
        scratch_shapes=[pltpu.VMEM((2,) + shapes[0], BF), pltpu.VMEM((2,) + shapes[1], BF), DMA((4,))],
        compiler_params=pltpu.CompilerParams(vmem_limit_bytes=LIMIT),
        cost_estimate=QUICK,
        name="wide_grads",
    )(where, dinner, act, first, dout, dbranch, mixed, *tokens)


def proj_grads_kernel(where, dqkv, x, tiny, *refs):
    keep, send, buf, sems = refs[-4:]
    b = pl.program_id(0)
    mods = 4 * buf.shape[2]
    per = buf.shape[3] - tiny.shape[1]
    part = tn(dqkv[...], x[...]).astype(BF)
    for i in range(mods // 2):
        put(buf, where, b * (mods // 2) + i, part[i * per : (i + 1) * per], (pl.ds(0, per),))

    @pl.when(b == 1)
    def _():
        for mod in range(mods):
            put(buf, where, mod, tiny[mod], (pl.ds(per, tiny.shape[1]),))
        hand_over((buf,), (keep, send), sems)


def proj_grads(where, dqkv, x, tiny, groups, tokens):
    total, width = x.shape
    per = 3 * width // (4 * groups)
    shape = (4, groups, per + tiny.shape[1], width // 2)
    half = dqkv.shape[1] // 2
    return pl.pallas_call(
        proj_grads_kernel,
        grid=(2,),
        out_shape=(S(shape, BF),) * 2,
        in_specs=[
            SM,
            pl.BlockSpec((total, half), lambda b: (0, b)),
            pl.BlockSpec(x.shape, lambda b: (0, 0), pipeline_mode=pl.Buffered(1)),
            pl.BlockSpec(tiny.shape, lambda b: (0, 0, 0), pipeline_mode=pl.Buffered(1)),
        ]
        + [ANY] * len(tokens),
        out_specs=(ANY, ANY),
        scratch_shapes=[pltpu.VMEM((2,) + shape, BF), DMA((2,))],
        compiler_params=pltpu.CompilerParams(vmem_limit_bytes=LIMIT),
        cost_estimate=QUICK,
        name="proj_grads",
    )(where, dqkv, x, tiny, *tokens)


def bits_of(axis):
    return (lax.axis_size(axis) - 1).bit_length()


def swapped(values, axis, mask):
    return lax.ppermute(values, axis, [(i, i ^ mask) for i in range(lax.axis_size(axis))])


def across(values, dc, dy, dx):
    pairs = lax.axis_size("pair")
    mask = (2 * dy + dc) * pairs + dx * (pairs // 2)
    count = lax.axis_size("mod") * pairs
    return lax.ppermute(values, ("mod", "pair"), [(i, i ^ mask) for i in range(count)])


def bit_at(axis, bit):
    return (lax.axis_index(axis) >> bit) & 1


def gather_far(slab, came=None):
    held = slab
    depth = 0
    for bit in range(bits_of("mod") - 1, 1, -1):
        other = swapped(held, "mod", 1 << bit) if depth or came is None else came
        upper = bit_at("mod", bit) == 1
        held = jnp.stack([jnp.where(upper, other, held), jnp.where(upper, held, other)], depth)
        depth += 1
    held = held.reshape((-1,) + slab.shape)
    for bit in range(bits_of("pair") - 1):
        other = swapped(held, "pair", 1 << bit)
        upper = bit_at("pair", bit) == 1
        held = jnp.concatenate([jnp.where(upper, other, held), jnp.where(upper, held, other)], -1)
    return held


def after(values, tokens):
    return lax.optimization_barrier((values, tokens))[0]


def gather_proj(slab):
    held = gather_far(slab)
    near = jnp.stack([held] + [across(held, 0, dy, dx) for dy, dx in ((0, 1), (1, 0), (1, 1))])
    return [near, across(near, 1, 0, 0)]


def gather_wide(slab, came, first):
    held = gather_far(slab, came)
    one, two = held[:, :first], held[:, first:]
    one = jnp.stack([one, across(one, 0, 0, 1)])
    two = jnp.stack([two, across(two, 0, 1, 0)])
    (one, two), early = lax.optimization_barrier(((one, two), (yield)))
    near = [one, across(one, 0, 1, 0), two, across(two, 0, 0, 1)]
    near, late = lax.optimization_barrier((near, (yield)))
    yield near + [across(piece, 1, 0, 0) for piece in near], early[:1] + late[:1]


def low(values):
    return values.astype(BF)


def wide(values):
    return values.astype(F32)


def reduce_proj(keep, send, gate_one, gate_two):
    came = across(send, 1, 0, 0)
    held = wide(keep[0]) + wide(came[0])
    ready = after([low(wide(keep[i]) + wide(came[i])) for i in (1, 2, 3)], gate_one)
    for part, (dy, dx) in zip(ready, ((0, 1), (1, 0), (1, 1))):
        held = held + wide(across(part, 0, dy, dx))
    *_, (held,) = reduce_far(after(held, gate_two))
    return held


def reduce_wide(keep_one, send_one, keep_two, send_two):
    came = across(send_one, 1, 0, 0), across(send_two, 1, 0, 0)
    gate = yield
    came_one, came_two = after(came, gate)
    go_one = low(wide(keep_one[2:]) + wide(came_one[2:]))
    go_two = low(wide(keep_two[2:]) + wide(came_two[2:]))
    back = across(go_one, 0, 1, 0), across(go_two, 0, 0, 1)
    gate = yield [go_one, go_two]
    back_one, back_two = after(back, gate)
    next_one = low(wide(keep_one[1]) + wide(came_one[1]) + wide(back_one[1]))
    next_two = low(wide(keep_two[1]) + wide(came_two[1]) + wide(back_two[1]))
    last = across(next_one, 0, 0, 1), across(next_two, 0, 1, 0)
    gate = yield [next_one, next_two]
    last_one, last_two = after(last, gate)
    held_one = wide(keep_one[0]) + wide(came_one[0]) + wide(back_one[0]) + wide(last_one)
    held_two = wide(keep_two[0]) + wide(came_two[0]) + wide(back_two[0]) + wide(last_two)
    held = jnp.concatenate([held_one, held_two], 1)
    yield [held]
    yield from reduce_far(held)


def reduce_far(held):
    def halved(held, axis, bit, dim):
        size = held.shape[dim] // 2
        mine = bit_at(axis, bit)
        away = low(lax.dynamic_slice_in_dim(held, (1 - mine) * size, size, dim))
        stay = lax.dynamic_slice_in_dim(held, mine * size, size, dim)
        return stay + wide(swapped(away, axis, 1 << bit))

    for bit in range(bits_of("pair") - 2, -1, -1):
        held = halved(held, "pair", bit, held.ndim - 1)
    depth = bits_of("mod") - 2
    rest = held.shape[1:]
    held = held.reshape((2,) * depth + rest)
    for bit in range(2, bits_of("mod")):
        held = halved(held, "mod", bit, depth - 1 - (bit - 2))
        yield [held.reshape((-1,) + rest)]


def settle(pieces, row, rows):
    part = jnp.stack([piece[:, :, row : row + rows] for piece in pieces])
    groups, rows, cols = part.shape[2:]
    part = part.reshape((2, 2, 2) + part.shape[2:])
    bits = (bit_at("mod", 0), bit_at("mod", 1), bit_at("pair", bits_of("pair") - 1))
    for dim, bit in enumerate(bits):
        part = jnp.where(bit == 1, jnp.flip(part, dim), part)
    return part.transpose(3, 1, 0, 4, 2, 5).reshape(4 * groups, rows, 2 * cols)


def per_device(rows_input, grad_out, w_qkv, w_out, w_up, w_down, vectors, b_up, live_rows):
    mods, pairs = lax.axis_size("mod"), lax.axis_size("pair")
    groups = mods // 4
    rows, width = rows_input.shape
    moved = rows // 2
    place = lax.axis_index("mod")
    upper = place >= mods // 2
    own_start = jnp.where(upper, moved, 0)
    away_start = jnp.where(upper, 0, moved)
    where = jnp.stack([place & 1, (place >> 1) & 1, bit_at("pair", bits_of("pair") - 1), own_start])

    def over(values):
        return swapped(values, "mod", mods // 2)

    chunk = moved // CHUNKS

    def units(sizes):
        return [(sum(sizes[:i]), size) for i, size in enumerate(sizes)]

    def over_units(array, sizes):
        return [
            over(lax.dynamic_slice_in_dim(array, away_start + c * chunk, n * chunk)) for c, n in units(sizes)
        ]

    line = w_qkv.shape[0]
    per, thin = w_qkv.shape[1], w_out.shape[1]
    small = jnp.concatenate([vectors.reshape(-1), b_up.reshape(-1)])
    small_rows = -(-small.shape[0] // line)
    small = jnp.pad(small, (0, 16 * line - small.shape[0])).reshape(16, line)
    proj_slab = jnp.concatenate([w_qkv.T, small], 0)
    down = w_down.T.reshape(thin, BLOCKS, line).transpose(1, 0, 2)
    slab = [w_out.T.reshape(1, thin, line), w_up.T.reshape(BLOCKS, thin, line), down]
    slab = jnp.concatenate(slab, 0)

    live_own = lax.dynamic_slice_in_dim(live_rows, own_start // SLOTS, moved // SLOTS)
    live_away = lax.dynamic_slice_in_dim(live_rows, away_start // SLOTS, moved // SLOTS)
    head = jnp.pad(live_away.astype(BF)[None], ((0, 15), (0, width - moved // SLOTS)))
    folded = jnp.concatenate(jnp.split(slab.reshape(-1, line), width // line, 0), 1)
    first_rows = lax.dynamic_slice_in_dim(rows_input, away_start, X_UNITS[0] * chunk)
    parcel = over(jnp.concatenate([first_rows, folded, head], 0))
    tall = folded.shape[0]
    came = parcel[first_rows.shape[0] : first_rows.shape[0] + tall]
    came = jnp.concatenate(jnp.split(came, width // line, 1), 0).reshape(slab.shape)
    live = jnp.stack([live_own, parcel[first_rows.shape[0] + tall, : moved // SLOTS].astype(jnp.int32)])

    proj = gather_proj(proj_slab)
    far_rows = [parcel] + over_units(rows_input, X_UNITS)[1:]
    wide_steps = gather_wide(slab, came, 1 + BLOCKS)
    next(wide_steps)
    far_grads = over_units(grad_out, FEED_UNITS)

    tiny = settle(proj, per, small_rows).reshape(mods, small_rows, pairs, line)
    tiny = tiny.transpose(2, 0, 1, 3).reshape(pairs, mods, -1)
    count = vectors.size
    vec = tiny[:, :, :count].reshape((pairs, mods) + vectors.shape).transpose(0, 2, 1, 3)
    vec = vec.reshape(8, width).astype(F32)
    bup = tiny[:, :, count : count + b_up.size].reshape((pairs, mods) + b_up.shape).transpose(0, 2, 1, 3)
    bup = bup.reshape(pairs, BLOCKS, line).transpose(1, 0, 2).reshape(BLOCKS, width).astype(F32)

    kept = ()
    for (c0, n), far in zip(units(X_UNITS), far_rows):
        for i in range(n):
            *kept, done = attend(c0 + i, i, where, live, rows_input, far, vec, proj, kept, [])
            if c0 + i in ATTENDS_BEFORE:
                arrived = far_rows[3:] + far_grads[:1] if c0 + i else []
                gathered = wide_steps.send([done] + arrived)
    wide_pieces, gates = gathered
    qkv_all, prob_all, mixed_all, x_all = kept
    fed, back_rows = (), []
    vec_sum, bup_sum = 0.0, 0.0
    for (c0, n), far in zip(units(FEED_UNITS), far_grads):
        (y0, size), = [unit for unit in units(Y_UNITS) if unit[0] <= c0 < unit[0] + unit[1]]
        fed = fed[: 7 if c0 == y0 else 8]
        out = feed(
            c0, n, c0 - y0, size * chunk, pairs, where, grad_out, far, x_all, mixed_all, vec, bup, wide_pieces, fed, gates
        )
        gates = []
        fed = out[:8]
        if c0 + n == y0 + size:
            back_rows.append(over(out[7]))
        vec_sum, bup_sum = vec_sum + out[8], bup_sum + out[9]
    result, act_all, dinner_all, first_all, dout_all, dbranch_all, dmix_all = fed[:7]
    wide_pair = wide_grads(
        pairs, where, dinner_all, act_all, first_all, dout_all, dbranch_all, mixed_all, groups, back_rows[:1]
    )
    wide_steps = reduce_wide(*after(wide_pair, back_rows[1:]))
    next(wide_steps)
    backed, back_grads = (), []
    qv_sum, done = 0.0, None
    for c0, n in units(BACK_UNITS):
        (d0, size), = [unit for unit in units(DX_UNITS) if unit[0] <= c0 < unit[0] + unit[1]]
        backed = backed[: 2 if c0 == d0 else 3]
        tokens = []
        if c0 in (1, 3):
            tokens = wide_steps.send(done)
        if c0 == 3:
            tokens = tokens + back_grads[:1]
        out = back(
            c0, n, c0 - d0, size * chunk, where, rows, qkv_all, prob_all, dbranch_all, dmix_all, proj, backed, tokens
        )
        backed, done = out[:3], out[3]
        if c0 + n == d0 + size:
            back_grads.append(over(out[2]))
        qv_sum = qv_sum + out[3]
    input_grad, dqkv_all = backed[:2]

    vec_grad = jnp.concatenate([qv_sum[:2], vec_sum[:6]], 0).reshape(pairs, -1, mods, vectors.shape[1])
    bup_grad = bup_sum.reshape(BLOCKS, pairs, line).transpose(1, 0, 2).reshape(pairs, -1, mods, b_up.shape[1])
    tiny_grad = [g.transpose(2, 0, 1, 3).reshape(mods, pairs, -1) for g in (vec_grad, bup_grad)]
    tiny_grad = jnp.concatenate(tiny_grad, -1)
    tiny_grad = jnp.pad(tiny_grad, ((0, 0), (0, 0), (0, 16 * line - small_size(vectors, b_up))))
    tiny_grad = tiny_grad.reshape(mods, pairs, 16, line).transpose(0, 2, 1, 3).reshape(mods, 16, width).astype(BF)
    tokens = wide_steps.send(done) + back_grads[1:2]
    proj_pair = proj_grads(where, dqkv_all, x_all, tiny_grad, groups, tokens)
    *gates, g_wide = wide_steps
    g_proj = reduce_proj(*after(proj_pair, back_grads[2:3] + gates[0]), [], g_wide)[0]
    g_wide = g_wide[0][0]

    for (c0, n), part in zip(units(Y_UNITS), back_rows):
        result = lax.dynamic_update_slice_in_dim(result, part, away_start + c0 * chunk, 0)
    for (c0, n), part in zip(units(DX_UNITS), back_grads):
        input_grad = lax.dynamic_update_slice_in_dim(input_grad, wide(part), away_start + c0 * chunk, 0)
    g_small = g_proj[per:].reshape(-1)
    return (
        result,
        input_grad,
        g_proj[:per].T,
        g_wide[0].T,
        g_wide[1 : 1 + BLOCKS].reshape(-1, line).T,
        g_wide[1 + BLOCKS :].transpose(1, 0, 2).reshape(thin, -1).T,
        g_small[:count].reshape(vectors.shape),
        g_small[count : count + b_up.size].reshape(b_up.shape),
    )


def small_size(vectors, b_up):
    return vectors.size + b_up.size


def solution(mesh):
    sharded = P("pair", "mod")
    spread = P(("mod", "pair"), None)
    weights = (sharded,) * 6
    return jax.shard_map(
        per_device,
        mesh=mesh,
        in_specs=(spread, spread) + weights + (P(("mod", "pair")),),
        out_specs=(spread, spread) + weights,
        check_vma=False,
    )
```

```python
import functools

import jax
import jax.numpy as jnp
from jax import lax
from jax.experimental import pallas as pl
from jax.experimental.pallas import tpu as pltpu
from jax.sharding import PartitionSpec as P

HEADS = 12
HEAD_DIM = 64
SLOTS = 64
CHUNKS = 4
X_UNITS = (1, 1, 1, 1)
FEED_UNITS = (1, 1, 2)
Y_UNITS = (2, 2)
BACK_UNITS = (1, 1, 1, 1)
DX_UNITS = (1, 1, 1, 1)
BLOCKS = 4
EPS = 1e-05
NEG = -1000000000.0
SCALE = HEAD_DIM**-0.5
LIMIT = 60 * 2**20
F32 = jnp.float32
BF = jnp.bfloat16
ANY = pl.BlockSpec(memory_space=pl.ANY)
VM = pl.BlockSpec(memory_space=pltpu.VMEM)
SM = pl.BlockSpec(memory_space=pltpu.SMEM)
S = jax.ShapeDtypeStruct
QUICK = pl.CostEstimate(flops=1, bytes_accessed=1, transcendentals=0)
SLOW = pl.CostEstimate(flops=10**10, bytes_accessed=30 * 10**6, transcendentals=0)
DMA = pltpu.SemaphoreType.DMA


def nt(a, b):
    return lax.dot_general(a, b, (((1,), (1,)), ((), ())), preferred_element_type=F32)


def nn(a, b):
    return lax.dot_general(a, b, (((1,), (0,)), ((), ())), preferred_element_type=F32)


def tn(a, b):
    return lax.dot_general(a, b, (((0,), (0,)), ((), ())), preferred_element_type=F32)


def colsum(v):
    return jnp.sum(v, 0, keepdims=True)


def copy(src, dst, sem):
    pltpu.make_async_copy(src, dst, sem).start()


def wait_for(ref, sem):
    pltpu.make_async_copy(ref, ref, sem).wait()


def pull(where, views, part, into, sem):
    core, low, side = where[0], where[1], where[2]
    for piece, (dc, dy, dx) in views:
        slab = (low ^ dy) * 2 + (core ^ dc)
        cols = piece.shape[-1]
        lane = pl.multiple_of((side ^ dx) * cols, cols)
        mid = (slice(None),) * (len(into.shape) - 3)
        copy(piece.at[:, part], into.at[(slice(None), slab) + mid + (pl.ds(lane, cols),)], sem)


def proj_views(refs):
    return [(ref.at[2 * dy + dx], (dc, dy, dx)) for dc, ref in enumerate(refs) for dy in (0, 1) for dx in (0, 1)]


def wide_views(refs):
    first, second = [], []
    for dc in (0, 1):
        for later in (0, 1):
            for early in (0, 1):
                first.append((refs[4 * dc + later].at[early], (dc, later, early)))
                second.append((refs[4 * dc + 2 + later].at[early], (dc, early, later)))
    return first, second


def attend_kernel(c, skip, where, live, rows, far, vec, *refs):
    views, refs = proj_views(refs[:2]), refs[-11:]
    qkv_all, prob_all, mixed_all, x_all, done, wqkv, xs, qkv, prob, mixed, sems = refs
    r, width = xs.shape
    h = r // 2
    seqs = prob.shape[0]
    done[...] = jnp.zeros_like(done)
    start = pl.multiple_of(where[3] + c * h, h)
    copy(rows.at[pl.ds(start, h)], xs.at[pl.ds(0, h)], sems.at[0])
    copy(far.at[pl.ds(skip * h, h)], xs.at[pl.ds(h, h)], sems.at[0])
    halves = wqkv.shape[0] // 2
    for i in (0, 1):
        some = [(piece.at[pl.ds(i * halves, halves)], bits) for piece, bits in views]
        pull(where, some, pl.ds(0, wqkv.shape[2]), wqkv.at[pl.ds(i * halves, halves)], sems.at[(1, 6)[i]])
    wait_for(xs, sems.at[0])
    span = pl.ds(c * r, r)
    copy(xs, x_all.at[span], sems.at[2])
    flat = wqkv.reshape(3 * width, width)
    x = xs[...]
    middle = width // 2
    for part in range(2):
        cols = slice(3 * part * middle, 3 * (part + 1) * middle)
        wait_for(wqkv.at[pl.ds(part * halves, halves)], sems.at[(1, 6)[part]])
        acc = nt(x, flat[cols, :])
        if part == 0:
            bias = jnp.concatenate([vec[0:1, :], jnp.zeros((1, middle), F32)], 1)
        else:
            bias = jnp.concatenate([jnp.zeros((1, middle), F32), vec[1:2, :]], 1)
        qkv[:, cols] = (acc + bias).astype(BF)
    copy(qkv, qkv_all.at[span], sems.at[3])
    lane = lax.broadcasted_iota(jnp.int32, (2 * SLOTS, 2 * HEAD_DIM), 1)
    low_half = lane < HEAD_DIM
    key = lax.broadcasted_iota(jnp.int32, (2 * SLOTS, 4 * SLOTS), 1) % (2 * SLOTS)

    def seq(s, carry):
        a = pl.multiple_of(s * SLOTS, SLOTS)
        b = pl.multiple_of(h + s * SLOTS, SLOTS)
        at = c * seqs + s
        valid = key < jnp.where(key < SLOTS, live[0, at], live[1, at] + SLOTS)
        for p in range(HEADS // 2):

            def take(part):
                cols = slice(part * width + p * 128, part * width + (p + 1) * 128)
                return jnp.concatenate([qkv[pl.ds(a, SLOTS), cols], qkv[pl.ds(b, SLOTS), cols]], 0)

            q, k, v = take(0), take(1), take(2)
            zero = jnp.zeros_like(k)
            k2 = jnp.concatenate([jnp.where(low_half, k, zero), jnp.where(low_half, zero, k)], 0)
            v2 = jnp.concatenate([jnp.where(low_half, v, zero), jnp.where(low_half, zero, v)], 0)
            score = jnp.where(valid, nt(q * SCALE, k2), NEG)
            halves = []
            for one in (score[:, : 2 * SLOTS], score[:, 2 * SLOTS :]):
                e = jnp.exp(one - jnp.max(one, -1, keepdims=True))
                halves.append((e * (1.0 / jnp.sum(e, -1, keepdims=True))).astype(BF))
            both = jnp.concatenate(halves, 1)
            prob[s, p] = both
            o = nn(both, v2).astype(BF)
            cols = slice(p * 128, (p + 1) * 128)
            mixed[pl.ds(a, SLOTS), cols] = o[:SLOTS]
            mixed[pl.ds(b, SLOTS), cols] = o[SLOTS:]
        copy(prob.at[s], prob_all.at[at], sems.at[4])
        return carry

    lax.fori_loop(0, seqs, seq, 0, unroll=2)
    copy(mixed, mixed_all.at[span], sems.at[5])
    wait_for(xs, sems.at[2])
    wait_for(qkv, sems.at[3])
    wait_for(prob, sems.at[4])
    wait_for(mixed, sems.at[5])


def attend(c, skip, where, live, rows, far, vec, pieces, before, tokens):
    width = far.shape[1]
    total = rows.shape[0]
    r = total // CHUNKS
    seqs = r // 2 // SLOTS
    groups = pieces[0].shape[1]
    per = 3 * width // (4 * groups)
    shapes = (
        S((total, 3 * width), BF),
        S((CHUNKS * seqs, HEADS // 2, 2 * SLOTS, 4 * SLOTS), BF),
        S((total, width), BF),
        S((total, width), BF),
    )
    return pl.pallas_call(
        functools.partial(attend_kernel, c, skip),
        out_shape=shapes + (S((8, 128), F32),),
        in_specs=[SM, SM, ANY, ANY, VM] + [ANY] * (2 + len(before) + len(tokens)),
        out_specs=(ANY,) * 4 + (VM,),
        input_output_aliases={7 + i: i for i in range(len(before))},
        scratch_shapes=[
            pltpu.VMEM((groups, 4, per, width), BF),
            pltpu.VMEM((r, width), BF),
            pltpu.VMEM((r, 3 * width), BF),
            pltpu.VMEM((seqs,) + shapes[1].shape[1:], BF),
            pltpu.VMEM((r, width), BF),
            DMA((7,)),
        ],
        compiler_params=pltpu.CompilerParams(vmem_limit_bytes=LIMIT),
        cost_estimate=SLOW,
        name="attend",
    )(where, live, rows, far, vec, *pieces, *before, *tokens)


def normed(v):
    c = v - jnp.mean(v, -1, keepdims=True)
    r = lax.rsqrt(jnp.mean(c * c, -1, keepdims=True) + EPS)
    return c * r, r


def norm_back(g, n, r):
    return r * (g - jnp.mean(g, -1, keepdims=True) - n * jnp.mean(g * n, -1, keepdims=True))


def feed_kernel(c0, subs, skip, sides, where, grads, far, x_all, mixed_all, vec, bup, *refs):
    first_views, second_views = wide_views(refs[:8])
    refs = refs[-27:]
    outs, sums, refs = refs[:8], refs[8:10], refs[10:]
    y_all, act_all, dinner_all, first_all, dout_all, dbranch_all, dmix_all, y_far = outs
    vsum, bsum = sums
    wout, wup, wdown, xs_all, mixed_in, gs_all, ys, act, slope, dinner, first, dout, dbranch, dmix, acc, n1, sems = refs
    r, width = ys.shape
    h = r // 2
    for t in range(subs):
        span = pl.ds((c0 + t) * r, r)
        start = pl.multiple_of(where[3] + (c0 + t) * h, h)
        copy(x_all.at[span], xs_all.at[t], sems.at[3, t])
        copy(mixed_all.at[span], mixed_in.at[t], sems.at[3, t])
        if t == 0:
            pull(where, first_views, pl.ds(0, 1), wout, sems.at[0, 0])
            pull(where, first_views, pl.ds(1, BLOCKS), wup, sems.at[1, 0])
        copy(grads.at[pl.ds(start, h)], gs_all.at[t, pl.ds(0, h)], sems.at[4, t])
        copy(far.at[pl.ds(t * h, h)], gs_all.at[t, pl.ds(h, h)], sems.at[4, t])
        if t == 0:
            pull(where, second_views, pl.ds(0, BLOCKS), wdown, sems.at[2, 0])
    out_flat = wout.reshape(width, width)
    ff = BLOCKS * width
    up_flat = wup.reshape(ff, width)
    step = width // sides

    def up_block(b):
        parts = [up_flat[pl.ds(side * BLOCKS * step + b * step, step), :] for side in range(sides)]
        return jnp.concatenate(parts, 0)

    def down_block(b):
        return wdown[:, :, b].reshape(width, width)

    for t in range(subs):
        c = c0 + t
        span = pl.ds(c * r, r)
        start = pl.multiple_of(where[3] + c * h, h)
        xs, mixed, gs = xs_all.at[t], mixed_in.at[t], gs_all.at[t]
        wait_for(xs, sems.at[3, t])
        wait_for(mixed, sems.at[3, t])
        if t == 0:
            wait_for(wout, sems.at[0, 0])
        sum1 = xs[...].astype(F32) + nt(mixed[...], out_flat[...]) + vec[2:3, :]
        hat, r1 = normed(sum1)
        n1[...] = hat
        top = hat * vec[4:5, :] + vec[5:6, :]
        if t:
            for ref in (act, dinner, first, dout, dbranch, dmix, ys):
                wait_for(ref, sems.at[5, 0])
        first[...] = top.astype(BF)
        copy(first, first_all.at[span], sems.at[5, 0])
        acc[...] = top + vec[3:4, :]
        if t == 0:
            wait_for(wup, sems.at[1, 0])
        for b in range(BLOCKS):
            cols = slice(b * width, (b + 1) * width)
            inner = nt(first[...], up_block(b)) + bup[b : b + 1, :]
            phi = 0.5 + 0.5 * lax.erf(inner * (2**-0.5))
            low = (inner * phi).astype(BF)
            act[:, cols] = low
            copy(act.at[:, cols], act_all.at[span, cols], sems.at[5, 0])
            slope[:, cols] = (phi + inner * (jnp.exp(-0.5 * inner * inner) * 0.3989422804014327)).astype(BF)
            if t == 0 and b == 0:
                wait_for(wdown, sems.at[2, 0])
            acc[...] += nt(low, down_block(b))
        n2, r2 = normed(acc[...])
        ys[...] = (n2 * vec[6:7, :] + vec[7:8, :]).astype(BF)
        copy(ys.at[pl.ds(0, h)], y_all.at[pl.ds(start, h)], sems.at[5, 0])
        copy(ys.at[pl.ds(h, h)], y_far.at[pl.ds((skip + t) * h, h)], sems.at[5, 0])
        wait_for(gs, sems.at[4, t])
        g = gs[...].astype(F32)
        sums_of = [None] * 6
        sums_of[4] = colsum(g * n2)
        sums_of[5] = colsum(g)
        dz2 = norm_back(g * vec[6:7, :], n2, r2)
        dout[...] = dz2.astype(BF)
        copy(dout, dout_all.at[span], sems.at[5, 0])
        sums_of[1] = colsum(dz2)
        acc[...] = dz2
        for b in range(BLOCKS):
            cols = slice(b * width, (b + 1) * width)
            grad = nn(dout[...], down_block(b)) * slope[:, cols].astype(F32)
            part = colsum(grad)
            bsum[0:1, cols] = part if t == 0 else bsum[0:1, cols] + part
            low = grad.astype(BF)
            dinner[:, cols] = low
            copy(dinner.at[:, cols], dinner_all.at[span, cols], sems.at[5, 0])
            acc[...] += nn(low, up_block(b))
        d = acc[...]
        hat = n1[...]
        sums_of[2] = colsum(d * hat)
        sums_of[3] = colsum(d)
        dz1 = norm_back(d * vec[4:5, :], hat, r1)
        sums_of[0] = colsum(dz1)
        low = dz1.astype(BF)
        dbranch[...] = low
        copy(dbranch, dbranch_all.at[span], sems.at[5, 0])
        dmix[...] = nn(low, out_flat[...]).astype(BF)
        copy(dmix, dmix_all.at[span], sems.at[5, 0])
        for i, part in enumerate(sums_of):
            vsum[i : i + 1, :] = part if t == 0 else vsum[i : i + 1, :] + part
    for ref in (act, dinner, first, dout, dbranch, dmix, ys):
        wait_for(ref, sems.at[5, 0])


def feed(c0, subs, skip, y_rows, sides, where, grads, far, x_all, mixed_all, vec, bup, pieces, before, tokens):
    total, width = x_all.shape
    r = total // CHUNKS
    ff = BLOCKS * width
    groups, thin = pieces[0].shape[1], pieces[0].shape[3]
    shapes = (
        S(grads.shape, BF),
        S((total, ff), BF),
        S((total, ff), BF),
        S((total, width), BF),
        S((total, width), BF),
        S((total, width), BF),
        S((total, width), BF),
    )
    return pl.pallas_call(
        functools.partial(feed_kernel, c0, subs, skip, sides),
        out_shape=shapes + (S((y_rows, width), BF), S((8, width), F32), S((1, ff), F32)),
        in_specs=[SM, ANY, ANY, ANY, ANY, VM, VM] + [ANY] * (8 + len(before) + len(tokens)),
        out_specs=(ANY,) * 8 + (VM,) * 2,
        input_output_aliases={15 + i: i for i in range(len(before))},
        scratch_shapes=[
            pltpu.VMEM((groups, 4, 1, thin, width), BF),
            pltpu.VMEM((groups, 4, BLOCKS, thin, width), BF),
            pltpu.VMEM((groups, 4, BLOCKS, thin, width), BF),
            pltpu.VMEM((subs, r, width), BF),
            pltpu.VMEM((subs, r, width), BF),
            pltpu.VMEM((subs, r, width), BF),
            pltpu.VMEM((r, width), BF),
            pltpu.VMEM((r, ff), BF),
            pltpu.VMEM((r, ff), BF),
            pltpu.VMEM((r, ff), BF),
            pltpu.VMEM((r, width), BF),
            pltpu.VMEM((r, width), BF),
            pltpu.VMEM((r, width), BF),
            pltpu.VMEM((r, width), BF),
            pltpu.VMEM((r, width), F32),
            pltpu.VMEM((r, width), F32),
            DMA((6, subs)),
        ],
        compiler_params=pltpu.CompilerParams(vmem_limit_bytes=LIMIT),
        cost_estimate=QUICK,
        name="feed",
    )(where, grads, far, x_all, mixed_all, vec, bup, *pieces, *before, *tokens)


def back_kernel(c0, skip, where, qkv_all, prob_all, dbranch_all, dmix_all, *refs):
    views, refs = proj_views(refs[:2]), refs[-14:]
    dx_all, dqkv_all, dx_far, vsum, wqkv, qkv, prob, dbranch, dmix, dqkv, dxs, dxf, sems, seq_sems = refs
    r, width = dbranch.shape
    h = dx_all.shape[0] // (2 * CHUNKS)
    subs = r // (2 * h)
    seqs = h // SLOTS
    span = pl.ds(c0 * 2 * h, r)
    for t in range(subs):
        for s in range(seqs):
            sem = seq_sems.at[t * seqs + s]
            for at in (2 * h * t + s * SLOTS, 2 * h * t + h + s * SLOTS):
                rows, there = pl.ds(at, SLOTS), pl.ds(c0 * 2 * h + at, SLOTS)
                copy(qkv_all.at[there], qkv.at[rows], sem)
                copy(dmix_all.at[there], dmix.at[rows], sem)
            copy(prob_all.at[(c0 + t) * seqs + s], prob.at[t * seqs + s], sem)
    pull(where, views, pl.ds(0, wqkv.shape[2]), wqkv, sems.at[3])
    copy(dbranch_all.at[span], dbranch, sems.at[4])
    lane = lax.broadcasted_iota(jnp.int32, (2 * SLOTS, 2 * HEAD_DIM), 1)
    low_half = lane < HEAD_DIM

    def seq(t, s):
        a = pl.multiple_of(2 * h * t + s * SLOTS, SLOTS)
        b = pl.multiple_of(2 * h * t + h + s * SLOTS, SLOTS)
        for p in range(HEADS // 2):

            def take(ref, part):
                cols = slice(part * width + p * 128, part * width + (p + 1) * 128)
                return jnp.concatenate([ref[pl.ds(a, SLOTS), cols], ref[pl.ds(b, SLOTS), cols]], 0)

            q, k, v = take(qkv, 0), take(qkv, 1), take(qkv, 2)
            do = take(dmix, 0)
            zero = jnp.zeros_like(k)
            k2 = jnp.concatenate([jnp.where(low_half, k, zero), jnp.where(low_half, zero, k)], 0)
            v2 = jnp.concatenate([jnp.where(low_half, v, zero), jnp.where(low_half, zero, v)], 0)
            both = prob[t * seqs + s, p]
            dp = nt(do, v2)
            wide = both.astype(F32)
            halves = []
            for u in range(2):
                cols = slice(u * 2 * SLOTS, (u + 1) * 2 * SLOTS)
                w = wide[:, cols] * dp[:, cols]
                halves.append((w - wide[:, cols] * jnp.sum(w, -1, keepdims=True)).astype(BF))
            ds = jnp.concatenate(halves, 1)
            dq = nn(ds, k2 * SCALE)
            dk = tn(ds, q * SCALE)
            dv = tn(both, do)
            dk = jnp.where(low_half, dk[: 2 * SLOTS], dk[2 * SLOTS :])
            dv = jnp.where(low_half, dv[: 2 * SLOTS], dv[2 * SLOTS :])
            for part, val in enumerate((dq, dk, dv)):
                cols = slice(part * width + p * 128, part * width + (p + 1) * 128)
                dqkv[pl.ds(a, SLOTS), cols] = val[:SLOTS].astype(BF)
                dqkv[pl.ds(b, SLOTS), cols] = val[SLOTS:].astype(BF)

    vsum[...] = jnp.zeros_like(vsum)
    for t in range(subs):
        chunk = pl.ds(t * 2 * h, 2 * h)

        def step(s, carry, t=t):
            sem = seq_sems.at[t * seqs + s]
            wait_for(qkv.at[pl.ds(0, 2 * SLOTS)], sem)
            wait_for(dmix.at[pl.ds(0, 2 * SLOTS)], sem)
            wait_for(prob.at[0], sem)
            seq(t, s)
            return carry

        lax.fori_loop(0, seqs, step, 0)
        copy(dqkv.at[chunk], dqkv_all.at[pl.ds((c0 + t) * 2 * h, 2 * h)], sems.at[5])
        if t == 0:
            wait_for(wqkv, sems.at[3])
            wait_for(dbranch, sems.at[4])
        mine = dqkv[chunk]
        dx = dbranch[chunk].astype(F32) + nn(mine, wqkv.reshape(3 * width, width)[...])
        dxs[t * h : (t + 1) * h, :] = dx[:h]
        start = pl.multiple_of(where[3] + (c0 + t) * h, h)
        copy(dxs.at[pl.ds(t * h, h)], dx_all.at[pl.ds(start, h)], sems.at[6])
        dxf[t * h : (t + 1) * h, :] = dx[h:].astype(BF)
        copy(dxf.at[pl.ds(t * h, h)], dx_far.at[pl.ds((skip + t) * h, h)], sems.at[7])
        vsum[0:1, :] += colsum(mine[:, :width].astype(F32))
        vsum[1:2, :] += colsum(mine[:, 2 * width :].astype(F32))
    wait_for(dqkv, sems.at[5])
    wait_for(dxs, sems.at[6])
    wait_for(dxf, sems.at[7])


def back(c0, subs, skip, dx_rows, where, rows, qkv_all, prob_all, dbranch_all, dmix_all, pieces, before, tokens):
    total, width = dbranch_all.shape
    r = subs * total // CHUNKS
    h = r // 2
    seqs = h // SLOTS
    groups = pieces[0].shape[1]
    per = 3 * width // (4 * groups)
    return pl.pallas_call(
        functools.partial(back_kernel, c0, skip),
        out_shape=(S((rows, width), F32), S((total, 3 * width), BF), S((dx_rows, width), BF), S((8, width), F32)),
        in_specs=[SM] + [ANY] * (6 + len(before) + len(tokens)),
        out_specs=(ANY, ANY, ANY, VM),
        input_output_aliases={7 + i: i for i in range(len(before))},
        scratch_shapes=[
            pltpu.VMEM((groups, 4, per, width), BF),
            pltpu.VMEM((r, 3 * width), BF),
            pltpu.VMEM((seqs,) + prob_all.shape[1:], BF),
            pltpu.VMEM((r, width), BF),
            pltpu.VMEM((r, width), BF),
            pltpu.VMEM((r, 3 * width), BF),
            pltpu.VMEM((h, width), F32),
            pltpu.VMEM((h, width), BF),
            DMA((8,)),
            DMA((seqs,)),
        ],
        compiler_params=pltpu.CompilerParams(vmem_limit_bytes=LIMIT),
        cost_estimate=QUICK,
        name="back",
    )(where, qkv_all, prob_all, dbranch_all, dmix_all, *pieces, *before, *tokens)


def put(buf, where, mod, value, dims, by_pair=False):
    core, low, side = where[0], where[1], where[2]
    cols = buf.shape[-1]
    dc = core ^ (mod & 1)
    dy = low ^ ((mod >> 1) & 1)
    for half in range(2):
        dx = side ^ half
        at = dx * 2 + dy if by_pair else dy * 2 + dx
        buf[(dc, at, mod >> 2) + dims] = value[..., half * cols : (half + 1) * cols]


def hand_over(bufs, outs, sems):
    copies = []
    for i, buf in enumerate(bufs):
        for dc in (1, 0):
            at = 2 * i + dc
            copies.append(pltpu.make_async_copy(buf.at[dc], outs[at], sems.at[at]))
    for one in copies:
        one.start()
    for one in copies:
        one.wait()


def wide_grads_kernel(sides, where, dinner, act, first, dout, dbranch, mixed, *refs):
    outs, (one, two, sems) = refs[-7:-3], refs[-3:]
    b = pl.program_id(0)
    width = first.shape[1]
    thin = one.shape[4]
    mods = 4 * one.shape[2]

    @pl.when(b == 0)
    def _():
        whole = tn(dbranch[...], mixed[...]).astype(BF)
        for mod in range(mods):
            put(one, where, mod, whole[mod * thin : (mod + 1) * thin], (0,))

    up = tn(dinner[...], first[...]).astype(BF)
    step = width // sides
    tall = BLOCKS * thin
    for side in range(sides):
        for i in range(step // tall):
            mod = side * BLOCKS * step // tall + b * (step // tall) + i
            rows = slice(side * step + i * tall, side * step + (i + 1) * tall)
            put(one, where, mod, up[rows].reshape(BLOCKS, thin, width), (pl.ds(1, BLOCKS),))
    down = tn(dout[...], act[...]).astype(BF)
    for mod in range(mods):
        put(two, where, mod, down[mod * thin : (mod + 1) * thin], (b,), True)

    @pl.when(b == BLOCKS - 1)
    def _():
        hand_over((one, two), outs, sems)


def wide_grads(sides, where, dinner, act, first, dout, dbranch, mixed, groups, tokens):
    total, width = first.shape
    thin = width // (4 * groups)
    shapes = [(4, groups, 1 + BLOCKS, thin, width // 2), (4, groups, BLOCKS, thin, width // 2)]

    def whole(array):
        return pl.BlockSpec(array.shape, lambda b: (0, 0), pipeline_mode=pl.Buffered(1))

    block = pl.BlockSpec((total, width), lambda b: (0, b))
    return pl.pallas_call(
        functools.partial(wide_grads_kernel, sides),
        grid=(BLOCKS,),
        out_shape=(S(shapes[0], BF),) * 2 + (S(shapes[1], BF),) * 2,
        in_specs=[SM, block, block, whole(first), whole(dout), whole(dbranch), whole(mixed)] + [ANY] * len(tokens),
        out_specs=(ANY,) * 4,
        scratch_shapes=[pltpu.VMEM((2,) + shapes[0], BF), pltpu.VMEM((2,) + shapes[1], BF), DMA((4,))],
        compiler_params=pltpu.CompilerParams(vmem_limit_bytes=LIMIT),
        cost_estimate=QUICK,
        name="wide_grads",
    )(where, dinner, act, first, dout, dbranch, mixed, *tokens)


def proj_grads_kernel(where, dqkv, x, tiny, *refs):
    keep, send, buf, sems = refs[-4:]
    b = pl.program_id(0)
    mods = 4 * buf.shape[2]
    per = buf.shape[3] - tiny.shape[1]
    part = tn(dqkv[...], x[...]).astype(BF)
    for i in range(mods // 2):
        put(buf, where, b * (mods // 2) + i, part[i * per : (i + 1) * per], (pl.ds(0, per),))

    @pl.when(b == 1)
    def _():
        for mod in range(mods):
            put(buf, where, mod, tiny[mod], (pl.ds(per, tiny.shape[1]),))
        hand_over((buf,), (keep, send), sems)


def proj_grads(where, dqkv, x, tiny, groups, tokens):
    total, width = x.shape
    per = 3 * width // (4 * groups)
    shape = (4, groups, per + tiny.shape[1], width // 2)
    half = dqkv.shape[1] // 2
    return pl.pallas_call(
        proj_grads_kernel,
        grid=(2,),
        out_shape=(S(shape, BF),) * 2,
        in_specs=[
            SM,
            pl.BlockSpec((total, half), lambda b: (0, b)),
            pl.BlockSpec(x.shape, lambda b: (0, 0), pipeline_mode=pl.Buffered(1)),
            pl.BlockSpec(tiny.shape, lambda b: (0, 0, 0), pipeline_mode=pl.Buffered(1)),
        ]
        + [ANY] * len(tokens),
        out_specs=(ANY, ANY),
        scratch_shapes=[pltpu.VMEM((2,) + shape, BF), DMA((2,))],
        compiler_params=pltpu.CompilerParams(vmem_limit_bytes=LIMIT),
        cost_estimate=QUICK,
        name="proj_grads",
    )(where, dqkv, x, tiny, *tokens)


def bits_of(axis):
    return (lax.axis_size(axis) - 1).bit_length()


def swapped(values, axis, mask):
    return lax.ppermute(values, axis, [(i, i ^ mask) for i in range(lax.axis_size(axis))])


def across(values, dc, dy, dx):
    pairs = lax.axis_size("pair")
    mask = (2 * dy + dc) * pairs + dx * (pairs // 2)
    count = lax.axis_size("mod") * pairs
    return lax.ppermute(values, ("mod", "pair"), [(i, i ^ mask) for i in range(count)])


def bit_at(axis, bit):
    return (lax.axis_index(axis) >> bit) & 1


def gather_far(slab, came=None):
    held = slab
    depth = 0
    for bit in range(bits_of("mod") - 1, 1, -1):
        other = swapped(held, "mod", 1 << bit) if depth or came is None else came
        upper = bit_at("mod", bit) == 1
        held = jnp.stack([jnp.where(upper, other, held), jnp.where(upper, held, other)], depth)
        depth += 1
    held = held.reshape((-1,) + slab.shape)
    for bit in range(bits_of("pair") - 1):
        other = swapped(held, "pair", 1 << bit)
        upper = bit_at("pair", bit) == 1
        held = jnp.concatenate([jnp.where(upper, other, held), jnp.where(upper, held, other)], -1)
    return held


def after(values, tokens):
    return lax.optimization_barrier((values, tokens))[0]


def gather_proj(slab):
    held = gather_far(slab)
    near = jnp.stack([held] + [across(held, 0, dy, dx) for dy, dx in ((0, 1), (1, 0), (1, 1))])
    return [near, across(near, 1, 0, 0)]


def gather_wide(slab, came, first):
    held = gather_far(slab, came)
    one, two = held[:, :first], held[:, first:]
    one = jnp.stack([one, across(one, 0, 0, 1)])
    two = jnp.stack([two, across(two, 0, 1, 0)])
    near = [one, across(one, 0, 1, 0), two, across(two, 0, 0, 1)]
    near, late = lax.optimization_barrier((near, (yield)))
    yield near + [across(piece, 1, 0, 0) for piece in near], late[:1]


def low(values):
    return values.astype(BF)


def wide(values):
    return values.astype(F32)


def reduce_proj(keep, send, gate_one, gate_two):
    came = across(send, 1, 0, 0)
    held = wide(keep[0]) + wide(came[0])
    ready = after([low(wide(keep[i]) + wide(came[i])) for i in (1, 2, 3)], gate_one)
    for part, (dy, dx) in zip(ready, ((0, 1), (1, 0), (1, 1))):
        held = held + wide(across(part, 0, dy, dx))
    held = after(held, gate_two)
    for bit in range(bits_of("pair") - 2, -1, -1):
        held, _ = halved(held, "pair", bit, held.ndim - 1)
    depth = bits_of("mod") - 2
    rest = held.shape[1:]
    held = held.reshape((2,) * depth + rest)
    for bit in range(2, bits_of("mod") - 2):
        held, _ = halved(held, "mod", bit, depth - 1 - (bit - 2))
    held = held.reshape((2, 2) + rest)
    top = bits_of("mod") - 1
    upper, inner = bit_at("mod", top), bit_at("mod", top - 1)

    def slab(u, v):
        part = lax.dynamic_index_in_dim(held, upper ^ u, 0, keepdims=False)
        return lax.dynamic_index_in_dim(part, inner ^ v, 0, keepdims=False)

    total = slab(0, 0)
    for u, v in ((1, 0), (1, 1), (0, 1)):
        total = total + wide(swapped(low(slab(u, v)), "mod", (u << top) | (v << (top - 1))))
    return total


def halved(held, axis, bit, dim):
    size = held.shape[dim] // 2
    mine = bit_at(axis, bit)
    away = low(lax.dynamic_slice_in_dim(held, (1 - mine) * size, size, dim))
    stay = lax.dynamic_slice_in_dim(held, mine * size, size, dim)
    got = swapped(away, axis, 1 << bit)
    return stay + wide(got), got


def reduce_wide(keep_one, send_one, keep_two, send_two):
    came = across(send_one, 1, 0, 0), across(send_two, 1, 0, 0)
    gate = yield
    came_one, came_two = after(came, gate)
    go_one = low(wide(keep_one[2:]) + wide(came_one[2:]))
    go_two = low(wide(keep_two[2:]) + wide(came_two[2:]))
    back = across(go_one, 0, 1, 0), across(go_two, 0, 0, 1)
    gate = yield [go_one, go_two]
    back_one, back_two = after(back, gate)
    next_one = low(wide(keep_one[1]) + wide(came_one[1]) + wide(back_one[1]))
    next_two = low(wide(keep_two[1]) + wide(came_two[1]) + wide(back_two[1]))
    last = across(next_one, 0, 0, 1), across(next_two, 0, 1, 0)
    gate = yield [next_one, next_two]
    last_one, last_two = after(last, gate)
    held_one = wide(keep_one[0]) + wide(came_one[0]) + wide(back_one[0]) + wide(last_one)
    held_two = wide(keep_two[0]) + wide(came_two[0]) + wide(back_two[0]) + wide(last_two)
    held = jnp.concatenate([held_one, held_two], 1)
    yield [held]
    yield from reduce_far(held)


def reduce_far(held):
    for bit in range(bits_of("pair") - 2, -1, -1):
        held, got = halved(held, "pair", bit, held.ndim - 1)
    depth = bits_of("mod") - 2
    rest = held.shape[1:]
    held = held.reshape((2,) * depth + rest)
    for bit in range(2, bits_of("mod")):
        held, got = halved(held, "mod", bit, depth - 1 - (bit - 2))
        yield [held.reshape((-1,) + rest), got]


def settle(pieces, row, rows):
    part = jnp.stack([piece[:, :, row : row + rows] for piece in pieces])
    groups, rows, cols = part.shape[2:]
    part = part.reshape((2, 2, 2) + part.shape[2:])
    bits = (bit_at("mod", 0), bit_at("mod", 1), bit_at("pair", bits_of("pair") - 1))
    for dim, bit in enumerate(bits):
        part = jnp.where(bit == 1, jnp.flip(part, dim), part)
    return part.transpose(3, 1, 0, 4, 2, 5).reshape(4 * groups, rows, 2 * cols)


def per_device(rows_input, grad_out, w_qkv, w_out, w_up, w_down, vectors, b_up, live_rows):
    mods, pairs = lax.axis_size("mod"), lax.axis_size("pair")
    groups = mods // 4
    rows, width = rows_input.shape
    moved = rows // 2
    place = lax.axis_index("mod")
    upper = place >= mods // 2
    own_start = jnp.where(upper, moved, 0)
    away_start = jnp.where(upper, 0, moved)
    where = jnp.stack([place & 1, (place >> 1) & 1, bit_at("pair", bits_of("pair") - 1), own_start])

    def over(values):
        return swapped(values, "mod", mods // 2)

    chunk = moved // CHUNKS

    def units(sizes):
        return [(sum(sizes[:i]), size) for i, size in enumerate(sizes)]

    def over_units(array, sizes, gate):
        return [
            over(after(lax.dynamic_slice_in_dim(array, away_start + c * chunk, n * chunk), gate))
            for c, n in units(sizes)
        ]

    line = w_qkv.shape[0]
    per, thin = w_qkv.shape[1], w_out.shape[1]
    small = jnp.concatenate([vectors.reshape(-1), b_up.reshape(-1)])
    small_rows = -(-small.shape[0] // line)
    small = jnp.pad(small, (0, 16 * line - small.shape[0])).reshape(16, line)
    proj_slab = jnp.concatenate([w_qkv.T, small], 0)
    down = w_down.T.reshape(thin, BLOCKS, line).transpose(1, 0, 2)
    slab = [w_out.T.reshape(1, thin, line), w_up.T.reshape(BLOCKS, thin, line), down]
    slab = jnp.concatenate(slab, 0)

    live_own = lax.dynamic_slice_in_dim(live_rows, own_start // SLOTS, moved // SLOTS)
    live_away = lax.dynamic_slice_in_dim(live_rows, away_start // SLOTS, moved // SLOTS)
    head = jnp.pad(live_away.astype(BF)[None], ((0, 15), (0, width - moved // SLOTS)))
    folded = jnp.concatenate(jnp.split(slab.reshape(-1, line), width // line, 0), 1)
    first_rows = lax.dynamic_slice_in_dim(rows_input, away_start, X_UNITS[0] * chunk)
    parcel = over(jnp.concatenate([first_rows, folded, head], 0))
    tall = folded.shape[0]
    came = parcel[first_rows.shape[0] : first_rows.shape[0] + tall]
    came = jnp.concatenate(jnp.split(came, width // line, 1), 0).reshape(slab.shape)
    live = jnp.stack([live_own, parcel[first_rows.shape[0] + tall, : moved // SLOTS].astype(jnp.int32)])

    proj = gather_proj(proj_slab)
    far_rows = [parcel]
    for c, n in units(X_UNITS)[1:]:
        part = lax.dynamic_slice_in_dim(rows_input, away_start + c * chunk, n * chunk)
        far_rows.append(over(after(part, far_rows[1:2])))
    wide_steps = gather_wide(slab, came, 1 + BLOCKS)
    next(wide_steps)
    far_grads = over_units(grad_out, FEED_UNITS, far_rows[1:2])

    tiny = settle(proj, per, small_rows).reshape(mods, small_rows, pairs, line)
    tiny = tiny.transpose(2, 0, 1, 3).reshape(pairs, mods, -1)
    count = vectors.size
    vec = tiny[:, :, :count].reshape((pairs, mods) + vectors.shape).transpose(0, 2, 1, 3)
    vec = vec.reshape(8, width).astype(F32)
    bup = tiny[:, :, count : count + b_up.size].reshape((pairs, mods) + b_up.shape).transpose(0, 2, 1, 3)
    bup = bup.reshape(pairs, BLOCKS, line).transpose(1, 0, 2).reshape(BLOCKS, width).astype(F32)

    kept = ()
    for (c0, n), far in zip(units(X_UNITS), far_rows):
        for i in range(n):
            *kept, done = attend(c0 + i, i, where, live, rows_input, far, vec, proj, kept, [])
            if c0 + i == CHUNKS - 2:
                gathered = wide_steps.send([done] + far_rows[3:] + far_grads[:1])
    wide_pieces, gates = gathered
    qkv_all, prob_all, mixed_all, x_all = kept
    fed, back_rows = (), []
    vec_sum, bup_sum = 0.0, 0.0
    for (c0, n), far in zip(units(FEED_UNITS), far_grads):
        (y0, size), = [unit for unit in units(Y_UNITS) if unit[0] <= c0 < unit[0] + unit[1]]
        fed = fed[: 7 if c0 == y0 else 8]
        out = feed(
            c0, n, c0 - y0, size * chunk, pairs, where, grad_out, far, x_all, mixed_all, vec, bup, wide_pieces, fed, gates
        )
        gates = []
        fed = out[:8]
        if c0 + n == y0 + size:
            back_rows.append(over(out[7]))
        vec_sum, bup_sum = vec_sum + out[8], bup_sum + out[9]
    result, act_all, dinner_all, first_all, dout_all, dbranch_all, dmix_all = fed[:7]
    wide_pair = wide_grads(
        pairs, where, dinner_all, act_all, first_all, dout_all, dbranch_all, mixed_all, groups, back_rows[:1]
    )
    wide_steps = reduce_wide(*after(wide_pair, back_rows[1:]))
    next(wide_steps)
    backed, back_grads = (), []
    qv_sum, done = 0.0, None
    for c0, n in units(BACK_UNITS):
        (d0, size), = [unit for unit in units(DX_UNITS) if unit[0] <= c0 < unit[0] + unit[1]]
        backed = backed[: 2 if c0 == d0 else 3]
        tokens = []
        if c0 in (1, 3):
            tokens = wide_steps.send(done)
        if c0 == 3:
            tokens = tokens + back_grads[:2]
        out = back(
            c0, n, c0 - d0, size * chunk, where, rows, qkv_all, prob_all, dbranch_all, dmix_all, proj, backed, tokens
        )
        backed, done = out[:3], out[3]
        if c0 + n == d0 + size:
            back_grads.append(over(out[2]))
        qv_sum = qv_sum + out[3]
    input_grad, dqkv_all = backed[:2]

    vec_grad = jnp.concatenate([qv_sum[:2], vec_sum[:6]], 0).reshape(pairs, -1, mods, vectors.shape[1])
    bup_grad = bup_sum.reshape(BLOCKS, pairs, line).transpose(1, 0, 2).reshape(pairs, -1, mods, b_up.shape[1])
    tiny_grad = [g.transpose(2, 0, 1, 3).reshape(mods, pairs, -1) for g in (vec_grad, bup_grad)]
    tiny_grad = jnp.concatenate(tiny_grad, -1)
    tiny_grad = jnp.pad(tiny_grad, ((0, 0), (0, 0), (0, 16 * line - small_size(vectors, b_up))))
    tiny_grad = tiny_grad.reshape(mods, pairs, 16, line).transpose(0, 2, 1, 3).reshape(mods, 16, width).astype(BF)
    tokens = wide_steps.send(done)
    proj_pair = proj_grads(where, dqkv_all, x_all, tiny_grad, groups, tokens)
    *gates, g_wide = wide_steps
    g_proj = reduce_proj(*after(proj_pair, back_grads[2:3] + gates[0][1:]), [], g_wide[1:])
    g_wide = g_wide[0][0]

    for (c0, n), part in zip(units(Y_UNITS), back_rows):
        result = lax.dynamic_update_slice_in_dim(result, part, away_start + c0 * chunk, 0)
    for (c0, n), part in zip(units(DX_UNITS), back_grads):
        input_grad = lax.dynamic_update_slice_in_dim(input_grad, wide(part), away_start + c0 * chunk, 0)
    g_small = g_proj[per:].reshape(-1)
    return (
        result,
        input_grad,
        g_proj[:per].T,
        g_wide[0].T,
        g_wide[1 : 1 + BLOCKS].reshape(-1, line).T,
        g_wide[1 + BLOCKS :].transpose(1, 0, 2).reshape(thin, -1).T,
        g_small[:count].reshape(vectors.shape),
        g_small[count : count + b_up.size].reshape(b_up.shape),
    )


def small_size(vectors, b_up):
    return vectors.size + b_up.size


def solution(mesh):
    sharded = P("pair", "mod")
    spread = P(("mod", "pair"), None)
    weights = (sharded,) * 6
    return jax.shard_map(
        per_device,
        mesh=mesh,
        in_specs=(spread, spread) + weights + (P(("mod", "pair")),),
        out_specs=(spread, spread) + weights,
        check_vma=False,
    )
```

```python
import functools

import jax
import jax.numpy as jnp
from jax import lax
from jax.experimental import pallas as pl
from jax.experimental.pallas import tpu as pltpu
from jax.sharding import PartitionSpec as P

HEADS = 12
HEAD_DIM = 64
SLOTS = 64
CHUNKS = 4
X_UNITS = (1, 1, 1, 1)
FEED_UNITS = (1, 1, 2)
Y_UNITS = (2, 2)
BACK_UNITS = (1, 1, 1, 1)
DX_UNITS = (1, 1, 1, 1)
BLOCKS = 4
EPS = 1e-05
NEG = -1000000000.0
SCALE = HEAD_DIM**-0.5
LIMIT = 60 * 2**20
F32 = jnp.float32
BF = jnp.bfloat16
ANY = pl.BlockSpec(memory_space=pl.ANY)
VM = pl.BlockSpec(memory_space=pltpu.VMEM)
SM = pl.BlockSpec(memory_space=pltpu.SMEM)
S = jax.ShapeDtypeStruct
QUICK = pl.CostEstimate(flops=1, bytes_accessed=1, transcendentals=0)
SLOW = pl.CostEstimate(flops=10**10, bytes_accessed=30 * 10**6, transcendentals=0)
DMA = pltpu.SemaphoreType.DMA


def nt(a, b):
    return lax.dot_general(a, b, (((1,), (1,)), ((), ())), preferred_element_type=F32)


def nn(a, b):
    return lax.dot_general(a, b, (((1,), (0,)), ((), ())), preferred_element_type=F32)


def tn(a, b):
    return lax.dot_general(a, b, (((0,), (0,)), ((), ())), preferred_element_type=F32)


def colsum(v):
    return jnp.sum(v, 0, keepdims=True)


def copy(src, dst, sem):
    pltpu.make_async_copy(src, dst, sem).start()


def wait_for(ref, sem):
    pltpu.make_async_copy(ref, ref, sem).wait()


def pull(where, views, part, into, sem):
    core, low, side = where[0], where[1], where[2]
    for piece, (dc, dy, dx) in views:
        slab = (low ^ dy) * 2 + (core ^ dc)
        cols = piece.shape[-1]
        lane = pl.multiple_of((side ^ dx) * cols, cols)
        mid = (slice(None),) * (len(into.shape) - 3)
        copy(piece.at[:, part], into.at[(slice(None), slab) + mid + (pl.ds(lane, cols),)], sem)


def proj_views(refs):
    return [(ref.at[2 * dy + dx], (dc, dy, dx)) for dc, ref in enumerate(refs) for dy in (0, 1) for dx in (0, 1)]


def wide_views(refs):
    first, second = [], []
    for dc in (0, 1):
        for later in (0, 1):
            for early in (0, 1):
                first.append((refs[4 * dc + later].at[early], (dc, later, early)))
                second.append((refs[4 * dc + 2 + later].at[early], (dc, early, later)))
    return first, second


def attend_kernel(c, skip, where, live, rows, far, vec, *refs):
    views, refs = proj_views(refs[:2]), refs[-11:]
    qkv_all, prob_all, mixed_all, x_all, done, wqkv, xs, qkv, prob, mixed, sems = refs
    r, width = xs.shape
    h = r // 2
    seqs = prob.shape[0]
    done[...] = jnp.zeros_like(done)
    start = pl.multiple_of(where[3] + c * h, h)
    copy(rows.at[pl.ds(start, h)], xs.at[pl.ds(0, h)], sems.at[0])
    copy(far.at[pl.ds(skip * h, h)], xs.at[pl.ds(h, h)], sems.at[0])
    halves = wqkv.shape[0] // 2
    for i in (0, 1):
        some = [(piece.at[pl.ds(i * halves, halves)], bits) for piece, bits in views]
        pull(where, some, pl.ds(0, wqkv.shape[2]), wqkv.at[pl.ds(i * halves, halves)], sems.at[(1, 6)[i]])
    wait_for(xs, sems.at[0])
    span = pl.ds(c * r, r)
    copy(xs, x_all.at[span], sems.at[2])
    flat = wqkv.reshape(3 * width, width)
    x = xs[...]
    middle = width // 2
    for part in range(2):
        cols = slice(3 * part * middle, 3 * (part + 1) * middle)
        wait_for(wqkv.at[pl.ds(part * halves, halves)], sems.at[(1, 6)[part]])
        acc = nt(x, flat[cols, :])
        if part == 0:
            bias = jnp.concatenate([vec[0:1, :], jnp.zeros((1, middle), F32)], 1)
        else:
            bias = jnp.concatenate([jnp.zeros((1, middle), F32), vec[1:2, :]], 1)
        qkv[:, cols] = (acc + bias).astype(BF)
    copy(qkv, qkv_all.at[span], sems.at[3])
    lane = lax.broadcasted_iota(jnp.int32, (2 * SLOTS, 2 * HEAD_DIM), 1)
    low_half = lane < HEAD_DIM
    key = lax.broadcasted_iota(jnp.int32, (2 * SLOTS, 4 * SLOTS), 1) % (2 * SLOTS)

    def seq(s, carry):
        a = pl.multiple_of(s * SLOTS, SLOTS)
        b = pl.multiple_of(h + s * SLOTS, SLOTS)
        at = c * seqs + s
        valid = key < jnp.where(key < SLOTS, live[0, at], live[1, at] + SLOTS)
        for p in range(HEADS // 2):

            def take(part):
                cols = slice(part * width + p * 128, part * width + (p + 1) * 128)
                return jnp.concatenate([qkv[pl.ds(a, SLOTS), cols], qkv[pl.ds(b, SLOTS), cols]], 0)

            q, k, v = take(0), take(1), take(2)
            zero = jnp.zeros_like(k)
            k2 = jnp.concatenate([jnp.where(low_half, k, zero), jnp.where(low_half, zero, k)], 0)
            v2 = jnp.concatenate([jnp.where(low_half, v, zero), jnp.where(low_half, zero, v)], 0)
            score = jnp.where(valid, nt(q * SCALE, k2), NEG)
            halves = []
            for one in (score[:, : 2 * SLOTS], score[:, 2 * SLOTS :]):
                e = jnp.exp(one - jnp.max(one, -1, keepdims=True))
                halves.append((e * (1.0 / jnp.sum(e, -1, keepdims=True))).astype(BF))
            both = jnp.concatenate(halves, 1)
            prob[s, p] = both
            o = nn(both, v2).astype(BF)
            cols = slice(p * 128, (p + 1) * 128)
            mixed[pl.ds(a, SLOTS), cols] = o[:SLOTS]
            mixed[pl.ds(b, SLOTS), cols] = o[SLOTS:]
        copy(prob.at[s], prob_all.at[at], sems.at[4])
        return carry

    lax.fori_loop(0, seqs, seq, 0, unroll=2)
    copy(mixed, mixed_all.at[span], sems.at[5])
    wait_for(xs, sems.at[2])
    wait_for(qkv, sems.at[3])
    wait_for(prob, sems.at[4])
    wait_for(mixed, sems.at[5])


def attend(c, skip, where, live, rows, far, vec, pieces, before, tokens):
    width = far.shape[1]
    total = rows.shape[0]
    r = total // CHUNKS
    seqs = r // 2 // SLOTS
    groups = pieces[0].shape[1]
    per = 3 * width // (4 * groups)
    shapes = (
        S((total, 3 * width), BF),
        S((CHUNKS * seqs, HEADS // 2, 2 * SLOTS, 4 * SLOTS), BF),
        S((total, width), BF),
        S((total, width), BF),
    )
    return pl.pallas_call(
        functools.partial(attend_kernel, c, skip),
        out_shape=shapes + (S((8, 128), F32),),
        in_specs=[SM, SM, ANY, ANY, VM] + [ANY] * (2 + len(before) + len(tokens)),
        out_specs=(ANY,) * 4 + (VM,),
        input_output_aliases={7 + i: i for i in range(len(before))},
        scratch_shapes=[
            pltpu.VMEM((groups, 4, per, width), BF),
            pltpu.VMEM((r, width), BF),
            pltpu.VMEM((r, 3 * width), BF),
            pltpu.VMEM((seqs,) + shapes[1].shape[1:], BF),
            pltpu.VMEM((r, width), BF),
            DMA((7,)),
        ],
        compiler_params=pltpu.CompilerParams(vmem_limit_bytes=LIMIT),
        cost_estimate=SLOW,
        name="attend",
    )(where, live, rows, far, vec, *pieces, *before, *tokens)


def normed(v):
    c = v - jnp.mean(v, -1, keepdims=True)
    r = lax.rsqrt(jnp.mean(c * c, -1, keepdims=True) + EPS)
    return c * r, r


def norm_back(g, n, r):
    return r * (g - jnp.mean(g, -1, keepdims=True) - n * jnp.mean(g * n, -1, keepdims=True))


def feed_kernel(c0, subs, skip, sides, where, grads, far, x_all, mixed_all, vec, bup, *refs):
    first_views, second_views = wide_views(refs[:8])
    refs = refs[-27:]
    outs, sums, refs = refs[:8], refs[8:10], refs[10:]
    y_all, act_all, dinner_all, first_all, dout_all, dbranch_all, dmix_all, y_far = outs
    vsum, bsum = sums
    wout, wup, wdown, xs_all, mixed_in, gs_all, ys, act, slope, dinner, first, dout, dbranch, dmix, acc, n1, sems = refs
    r, width = ys.shape
    h = r // 2
    for t in range(subs):
        span = pl.ds((c0 + t) * r, r)
        start = pl.multiple_of(where[3] + (c0 + t) * h, h)
        copy(x_all.at[span], xs_all.at[t], sems.at[3, t])
        copy(mixed_all.at[span], mixed_in.at[t], sems.at[3, t])
        if t == 0:
            pull(where, first_views, pl.ds(0, 1), wout, sems.at[0, 0])
            pull(where, first_views, pl.ds(1, BLOCKS), wup, sems.at[1, 0])
        copy(grads.at[pl.ds(start, h)], gs_all.at[t, pl.ds(0, h)], sems.at[4, t])
        copy(far.at[pl.ds(t * h, h)], gs_all.at[t, pl.ds(h, h)], sems.at[4, t])
        if t == 0:
            pull(where, second_views, pl.ds(0, BLOCKS), wdown, sems.at[2, 0])
    out_flat = wout.reshape(width, width)
    ff = BLOCKS * width
    up_flat = wup.reshape(ff, width)
    step = width // sides

    def up_block(b):
        parts = [up_flat[pl.ds(side * BLOCKS * step + b * step, step), :] for side in range(sides)]
        return jnp.concatenate(parts, 0)

    def down_block(b):
        return wdown[:, :, b].reshape(width, width)

    for t in range(subs):
        c = c0 + t
        span = pl.ds(c * r, r)
        start = pl.multiple_of(where[3] + c * h, h)
        xs, mixed, gs = xs_all.at[t], mixed_in.at[t], gs_all.at[t]
        wait_for(xs, sems.at[3, t])
        wait_for(mixed, sems.at[3, t])
        if t == 0:
            wait_for(wout, sems.at[0, 0])
        sum1 = xs[...].astype(F32) + nt(mixed[...], out_flat[...]) + vec[2:3, :]
        hat, r1 = normed(sum1)
        n1[...] = hat
        top = hat * vec[4:5, :] + vec[5:6, :]
        if t:
            for ref in (act, dinner, first, dout, dbranch, dmix, ys):
                wait_for(ref, sems.at[5, 0])
        first[...] = top.astype(BF)
        copy(first, first_all.at[span], sems.at[5, 0])
        acc[...] = top + vec[3:4, :]
        if t == 0:
            wait_for(wup, sems.at[1, 0])
        for b in range(BLOCKS):
            cols = slice(b * width, (b + 1) * width)
            inner = nt(first[...], up_block(b)) + bup[b : b + 1, :]
            phi = 0.5 + 0.5 * lax.erf(inner * (2**-0.5))
            low = (inner * phi).astype(BF)
            act[:, cols] = low
            copy(act.at[:, cols], act_all.at[span, cols], sems.at[5, 0])
            slope[:, cols] = (phi + inner * (jnp.exp(-0.5 * inner * inner) * 0.3989422804014327)).astype(BF)
            if t == 0 and b == 0:
                wait_for(wdown, sems.at[2, 0])
            acc[...] += nt(low, down_block(b))
        n2, r2 = normed(acc[...])
        ys[...] = (n2 * vec[6:7, :] + vec[7:8, :]).astype(BF)
        copy(ys.at[pl.ds(0, h)], y_all.at[pl.ds(start, h)], sems.at[5, 0])
        copy(ys.at[pl.ds(h, h)], y_far.at[pl.ds((skip + t) * h, h)], sems.at[5, 0])
        wait_for(gs, sems.at[4, t])
        g = gs[...].astype(F32)
        sums_of = [None] * 6
        sums_of[4] = colsum(g * n2)
        sums_of[5] = colsum(g)
        dz2 = norm_back(g * vec[6:7, :], n2, r2)
        dout[...] = dz2.astype(BF)
        copy(dout, dout_all.at[span], sems.at[5, 0])
        sums_of[1] = colsum(dz2)
        acc[...] = dz2
        for b in range(BLOCKS):
            cols = slice(b * width, (b + 1) * width)
            grad = nn(dout[...], down_block(b)) * slope[:, cols].astype(F32)
            part = colsum(grad)
            bsum[0:1, cols] = part if t == 0 else bsum[0:1, cols] + part
            low = grad.astype(BF)
            dinner[:, cols] = low
            copy(dinner.at[:, cols], dinner_all.at[span, cols], sems.at[5, 0])
            acc[...] += nn(low, up_block(b))
        d = acc[...]
        hat = n1[...]
        sums_of[2] = colsum(d * hat)
        sums_of[3] = colsum(d)
        dz1 = norm_back(d * vec[4:5, :], hat, r1)
        sums_of[0] = colsum(dz1)
        low = dz1.astype(BF)
        dbranch[...] = low
        copy(dbranch, dbranch_all.at[span], sems.at[5, 0])
        dmix[...] = nn(low, out_flat[...]).astype(BF)
        copy(dmix, dmix_all.at[span], sems.at[5, 0])
        for i, part in enumerate(sums_of):
            vsum[i : i + 1, :] = part if t == 0 else vsum[i : i + 1, :] + part
    for ref in (act, dinner, first, dout, dbranch, dmix, ys):
        wait_for(ref, sems.at[5, 0])


def feed(c0, subs, skip, y_rows, sides, where, grads, far, x_all, mixed_all, vec, bup, pieces, before, tokens):
    total, width = x_all.shape
    r = total // CHUNKS
    ff = BLOCKS * width
    groups, thin = pieces[0].shape[1], pieces[0].shape[3]
    shapes = (
        S(grads.shape, BF),
        S((total, ff), BF),
        S((total, ff), BF),
        S((total, width), BF),
        S((total, width), BF),
        S((total, width), BF),
        S((total, width), BF),
    )
    return pl.pallas_call(
        functools.partial(feed_kernel, c0, subs, skip, sides),
        out_shape=shapes + (S((y_rows, width), BF), S((8, width), F32), S((1, ff), F32)),
        in_specs=[SM, ANY, ANY, ANY, ANY, VM, VM] + [ANY] * (8 + len(before) + len(tokens)),
        out_specs=(ANY,) * 8 + (VM,) * 2,
        input_output_aliases={15 + i: i for i in range(len(before))},
        scratch_shapes=[
            pltpu.VMEM((groups, 4, 1, thin, width), BF),
            pltpu.VMEM((groups, 4, BLOCKS, thin, width), BF),
            pltpu.VMEM((groups, 4, BLOCKS, thin, width), BF),
            pltpu.VMEM((subs, r, width), BF),
            pltpu.VMEM((subs, r, width), BF),
            pltpu.VMEM((subs, r, width), BF),
            pltpu.VMEM((r, width), BF),
            pltpu.VMEM((r, ff), BF),
            pltpu.VMEM((r, ff), BF),
            pltpu.VMEM((r, ff), BF),
            pltpu.VMEM((r, width), BF),
            pltpu.VMEM((r, width), BF),
            pltpu.VMEM((r, width), BF),
            pltpu.VMEM((r, width), BF),
            pltpu.VMEM((r, width), F32),
            pltpu.VMEM((r, width), F32),
            DMA((6, subs)),
        ],
        compiler_params=pltpu.CompilerParams(vmem_limit_bytes=LIMIT),
        cost_estimate=QUICK,
        name="feed",
    )(where, grads, far, x_all, mixed_all, vec, bup, *pieces, *before, *tokens)


def back_kernel(c0, skip, where, qkv_all, prob_all, dbranch_all, dmix_all, *refs):
    views, refs = proj_views(refs[:2]), refs[-12:]
    dqkv_all, dx_far, vsum, wqkv, qkv, prob, dbranch, dmix, dqkv, dxf, sems, seq_sems = refs
    r, width = dmix.shape
    h = dqkv_all.shape[0] // (2 * CHUNKS)
    subs = r // (2 * h)
    seqs = h // SLOTS
    for t in range(subs):
        for s in range(seqs):
            sem = seq_sems.at[t * seqs + s]
            for at in (2 * h * t + s * SLOTS, 2 * h * t + h + s * SLOTS):
                rows, there = pl.ds(at, SLOTS), pl.ds(c0 * 2 * h + at, SLOTS)
                copy(qkv_all.at[there], qkv.at[rows], sem)
                copy(dmix_all.at[there], dmix.at[rows], sem)
            copy(prob_all.at[(c0 + t) * seqs + s], prob.at[t * seqs + s], sem)
    pull(where, views, pl.ds(0, wqkv.shape[2]), wqkv, sems.at[3])
    for t in range(subs):
        there = pl.ds((c0 + t) * 2 * h + h, h)
        copy(dbranch_all.at[there], dbranch.at[pl.ds(t * h, h)], sems.at[4])
    lane = lax.broadcasted_iota(jnp.int32, (2 * SLOTS, 2 * HEAD_DIM), 1)
    low_half = lane < HEAD_DIM

    def seq(t, s):
        a = pl.multiple_of(2 * h * t + s * SLOTS, SLOTS)
        b = pl.multiple_of(2 * h * t + h + s * SLOTS, SLOTS)
        for p in range(HEADS // 2):

            def take(ref, part):
                cols = slice(part * width + p * 128, part * width + (p + 1) * 128)
                return jnp.concatenate([ref[pl.ds(a, SLOTS), cols], ref[pl.ds(b, SLOTS), cols]], 0)

            q, k, v = take(qkv, 0), take(qkv, 1), take(qkv, 2)
            do = take(dmix, 0)
            zero = jnp.zeros_like(k)
            k2 = jnp.concatenate([jnp.where(low_half, k, zero), jnp.where(low_half, zero, k)], 0)
            v2 = jnp.concatenate([jnp.where(low_half, v, zero), jnp.where(low_half, zero, v)], 0)
            both = prob[t * seqs + s, p]
            dp = nt(do, v2)
            wide = both.astype(F32)
            halves = []
            for u in range(2):
                cols = slice(u * 2 * SLOTS, (u + 1) * 2 * SLOTS)
                w = wide[:, cols] * dp[:, cols]
                halves.append((w - wide[:, cols] * jnp.sum(w, -1, keepdims=True)).astype(BF))
            ds = jnp.concatenate(halves, 1)
            dq = nn(ds, k2 * SCALE)
            dk = tn(ds, q * SCALE)
            dv = tn(both, do)
            dk = jnp.where(low_half, dk[: 2 * SLOTS], dk[2 * SLOTS :])
            dv = jnp.where(low_half, dv[: 2 * SLOTS], dv[2 * SLOTS :])
            for part, val in enumerate((dq, dk, dv)):
                cols = slice(part * width + p * 128, part * width + (p + 1) * 128)
                dqkv[pl.ds(a, SLOTS), cols] = val[:SLOTS].astype(BF)
                dqkv[pl.ds(b, SLOTS), cols] = val[SLOTS:].astype(BF)

    vsum[...] = jnp.zeros_like(vsum)
    for t in range(subs):
        chunk = pl.ds(t * 2 * h, 2 * h)

        def step(s, carry, t=t):
            sem = seq_sems.at[t * seqs + s]
            wait_for(qkv.at[pl.ds(0, 2 * SLOTS)], sem)
            wait_for(dmix.at[pl.ds(0, 2 * SLOTS)], sem)
            wait_for(prob.at[0], sem)
            seq(t, s)
            return carry

        lax.fori_loop(0, seqs, step, 0)
        copy(dqkv.at[chunk], dqkv_all.at[pl.ds((c0 + t) * 2 * h, 2 * h)], sems.at[5])
        if t == 0:
            wait_for(wqkv, sems.at[3])
            wait_for(dbranch, sems.at[4])
        mine = dqkv[chunk]
        part = slice(t * h, (t + 1) * h)
        dx = dbranch[part].astype(F32) + nn(mine[h:], wqkv.reshape(3 * width, width)[...])
        dxf[part, :] = dx.astype(BF)
        copy(dxf.at[pl.ds(t * h, h)], dx_far.at[pl.ds((skip + t) * h, h)], sems.at[7])
        vsum[0:1, :] += colsum(mine[:, :width].astype(F32))
        vsum[1:2, :] += colsum(mine[:, 2 * width :].astype(F32))
    wait_for(dqkv, sems.at[5])
    wait_for(dxf, sems.at[7])


def back(c0, subs, skip, dx_rows, where, qkv_all, prob_all, dbranch_all, dmix_all, pieces, before, tokens):
    total, width = dbranch_all.shape
    r = subs * total // CHUNKS
    h = r // 2
    seqs = h // SLOTS
    groups = pieces[0].shape[1]
    per = 3 * width // (4 * groups)
    return pl.pallas_call(
        functools.partial(back_kernel, c0, skip),
        out_shape=(S((total, 3 * width), BF), S((dx_rows, width), BF), S((8, width), F32)),
        in_specs=[SM] + [ANY] * (6 + len(before) + len(tokens)),
        out_specs=(ANY, ANY, VM),
        input_output_aliases={7 + i: i for i in range(len(before))},
        scratch_shapes=[
            pltpu.VMEM((groups, 4, per, width), BF),
            pltpu.VMEM((r, 3 * width), BF),
            pltpu.VMEM((seqs,) + prob_all.shape[1:], BF),
            pltpu.VMEM((h, width), BF),
            pltpu.VMEM((r, width), BF),
            pltpu.VMEM((r, 3 * width), BF),
            pltpu.VMEM((h, width), BF),
            DMA((8,)),
            DMA((seqs,)),
        ],
        compiler_params=pltpu.CompilerParams(vmem_limit_bytes=LIMIT),
        cost_estimate=QUICK,
        name="back",
    )(where, qkv_all, prob_all, dbranch_all, dmix_all, *pieces, *before, *tokens)


def finish_kernel(n_y, n_dx, where, dqkv_all, dbranch_all, *refs):
    views = proj_views(refs[:2])
    y_parts, dx_parts = refs[3 : 3 + n_y], refs[3 + n_y : 3 + n_y + n_dx]
    dx_all, y_all, wqkv, dqkv, dbranch, dx, came, wider, ys, sems = refs[-10:]
    width = dbranch.shape[2]
    h = dbranch.shape[1]
    moved = CHUNKS * h
    away = moved - where[3]
    pull(where, views, pl.ds(0, wqkv.shape[2]), wqkv, sems.at[0])
    for c, part in enumerate(dx_parts):
        copy(part, came.at[c], sems.at[2])
    size = moved // n_y
    for i, part in enumerate(y_parts):
        copy(part, ys.at[i], sems.at[3])
    for c in range(CHUNKS):
        span = pl.ds(c * 2 * h, h)
        copy(dqkv_all.at[span], dqkv.at[c], sems.at[5 + c])
        copy(dbranch_all.at[span], dbranch.at[c], sems.at[5 + c])
    wait_for(ys, sems.at[3])
    for i in range(n_y):
        copy(ys.at[i], y_all.at[pl.ds(pl.multiple_of(away + i * size, size), size)], sems.at[3])
    wait_for(came, sems.at[2])
    for c in range(n_dx):
        wider[c] = came[c].astype(F32)
        copy(wider.at[c], dx_all.at[pl.ds(pl.multiple_of(away + c * h, h), h)], sems.at[4])
    wait_for(wqkv, sems.at[0])
    for c in range(CHUNKS):
        wait_for(dqkv.at[c], sems.at[5 + c])
        wait_for(dbranch.at[c], sems.at[5 + c])
        dx[c] = dbranch[c].astype(F32) + nn(dqkv[c], wqkv.reshape(3 * width, width)[...])
        copy(dx.at[c], dx_all.at[pl.ds(pl.multiple_of(where[3] + c * h, h), h)], sems.at[1])
    wait_for(ys, sems.at[3])
    wait_for(wider, sems.at[4])
    wait_for(dx, sems.at[1])


def finish(where, dqkv_all, dbranch_all, pieces, result, y_parts, dx_parts, tokens):
    total, width = dbranch_all.shape
    h = total // (2 * CHUNKS)
    groups = pieces[0].shape[1]
    per = 3 * width // (4 * groups)
    n_y, n_dx = len(y_parts), len(dx_parts)
    return pl.pallas_call(
        functools.partial(finish_kernel, n_y, n_dx),
        out_shape=(S(result.shape, F32), S(result.shape, BF)),
        in_specs=[SM] + [ANY] * (5 + n_y + n_dx + len(tokens)),
        out_specs=(ANY, ANY),
        input_output_aliases={5: 1},
        scratch_shapes=[
            pltpu.VMEM((groups, 4, per, width), BF),
            pltpu.VMEM((CHUNKS, h, 3 * width), BF),
            pltpu.VMEM((CHUNKS, h, width), BF),
            pltpu.VMEM((CHUNKS, h, width), F32),
            pltpu.VMEM((n_dx, h, width), BF),
            pltpu.VMEM((n_dx, h, width), F32),
            pltpu.VMEM((n_y, CHUNKS * h // n_y, width), BF),
            DMA((5 + CHUNKS,)),
        ],
        compiler_params=pltpu.CompilerParams(vmem_limit_bytes=LIMIT),
        cost_estimate=QUICK,
        name="finish",
    )(where, dqkv_all, dbranch_all, *pieces, result, *y_parts, *dx_parts, *tokens)


def put(buf, where, mod, value, dims, by_pair=False):
    core, low, side = where[0], where[1], where[2]
    cols = buf.shape[-1]
    dc = core ^ (mod & 1)
    dy = low ^ ((mod >> 1) & 1)
    for half in range(2):
        dx = side ^ half
        at = dx * 2 + dy if by_pair else dy * 2 + dx
        buf[(dc, at, mod >> 2) + dims] = value[..., half * cols : (half + 1) * cols]


def hand_over(bufs, outs, sems):
    copies = []
    for i, buf in enumerate(bufs):
        for dc in (1, 0):
            at = 2 * i + dc
            copies.append(pltpu.make_async_copy(buf.at[dc], outs[at], sems.at[at]))
    for one in copies:
        one.start()
    for one in copies:
        one.wait()


def wide_grads_kernel(sides, where, dinner, act, first, dout, dbranch, mixed, *refs):
    outs, (one, two, sems) = refs[-7:-3], refs[-3:]
    b = pl.program_id(0)
    width = first.shape[1]
    thin = one.shape[4]
    mods = 4 * one.shape[2]

    @pl.when(b == 0)
    def _():
        whole = tn(dbranch[...], mixed[...]).astype(BF)
        for mod in range(mods):
            put(one, where, mod, whole[mod * thin : (mod + 1) * thin], (0,))

    up = tn(dinner[...], first[...]).astype(BF)
    step = width // sides
    tall = BLOCKS * thin
    for side in range(sides):
        for i in range(step // tall):
            mod = side * BLOCKS * step // tall + b * (step // tall) + i
            rows = slice(side * step + i * tall, side * step + (i + 1) * tall)
            put(one, where, mod, up[rows].reshape(BLOCKS, thin, width), (pl.ds(1, BLOCKS),))
    down = tn(dout[...], act[...]).astype(BF)
    for mod in range(mods):
        put(two, where, mod, down[mod * thin : (mod + 1) * thin], (b,), True)

    @pl.when(b == BLOCKS - 1)
    def _():
        hand_over((one, two), outs, sems)


def wide_grads(sides, where, dinner, act, first, dout, dbranch, mixed, groups, tokens):
    total, width = first.shape
    thin = width // (4 * groups)
    shapes = [(4, groups, 1 + BLOCKS, thin, width // 2), (4, groups, BLOCKS, thin, width // 2)]

    def whole(array):
        return pl.BlockSpec(array.shape, lambda b: (0, 0), pipeline_mode=pl.Buffered(1))

    block = pl.BlockSpec((total, width), lambda b: (0, b))
    return pl.pallas_call(
        functools.partial(wide_grads_kernel, sides),
        grid=(BLOCKS,),
        out_shape=(S(shapes[0], BF),) * 2 + (S(shapes[1], BF),) * 2,
        in_specs=[SM, block, block, whole(first), whole(dout), whole(dbranch), whole(mixed)] + [ANY] * len(tokens),
        out_specs=(ANY,) * 4,
        scratch_shapes=[pltpu.VMEM((2,) + shapes[0], BF), pltpu.VMEM((2,) + shapes[1], BF), DMA((4,))],
        compiler_params=pltpu.CompilerParams(vmem_limit_bytes=LIMIT),
        cost_estimate=QUICK,
        name="wide_grads",
    )(where, dinner, act, first, dout, dbranch, mixed, *tokens)


def proj_grads_kernel(where, dqkv, x, tiny, *refs):
    keep, send, buf, sems = refs[-4:]
    b = pl.program_id(0)
    mods = 4 * buf.shape[2]
    per = buf.shape[3] - tiny.shape[1]
    part = tn(dqkv[...], x[...]).astype(BF)
    for i in range(mods // 2):
        put(buf, where, b * (mods // 2) + i, part[i * per : (i + 1) * per], (pl.ds(0, per),))

    @pl.when(b == 1)
    def _():
        for mod in range(mods):
            put(buf, where, mod, tiny[mod], (pl.ds(per, tiny.shape[1]),))
        hand_over((buf,), (keep, send), sems)


def proj_grads(where, dqkv, x, tiny, groups, tokens):
    total, width = x.shape
    per = 3 * width // (4 * groups)
    shape = (4, groups, per + tiny.shape[1], width // 2)
    half = dqkv.shape[1] // 2
    return pl.pallas_call(
        proj_grads_kernel,
        grid=(2,),
        out_shape=(S(shape, BF),) * 2,
        in_specs=[
            SM,
            pl.BlockSpec((total, half), lambda b: (0, b)),
            pl.BlockSpec(x.shape, lambda b: (0, 0), pipeline_mode=pl.Buffered(1)),
            pl.BlockSpec(tiny.shape, lambda b: (0, 0, 0), pipeline_mode=pl.Buffered(1)),
        ]
        + [ANY] * len(tokens),
        out_specs=(ANY, ANY),
        scratch_shapes=[pltpu.VMEM((2,) + shape, BF), DMA((2,))],
        compiler_params=pltpu.CompilerParams(vmem_limit_bytes=LIMIT),
        cost_estimate=QUICK,
        name="proj_grads",
    )(where, dqkv, x, tiny, *tokens)


def bits_of(axis):
    return (lax.axis_size(axis) - 1).bit_length()


def swapped(values, axis, mask):
    return lax.ppermute(values, axis, [(i, i ^ mask) for i in range(lax.axis_size(axis))])


def across(values, dc, dy, dx):
    pairs = lax.axis_size("pair")
    mask = (2 * dy + dc) * pairs + dx * (pairs // 2)
    count = lax.axis_size("mod") * pairs
    return lax.ppermute(values, ("mod", "pair"), [(i, i ^ mask) for i in range(count)])


def bit_at(axis, bit):
    return (lax.axis_index(axis) >> bit) & 1


def gather_far(slab, came=None):
    held = slab
    depth = 0
    for bit in range(bits_of("mod") - 1, 1, -1):
        other = swapped(held, "mod", 1 << bit) if depth or came is None else came
        upper = bit_at("mod", bit) == 1
        held = jnp.stack([jnp.where(upper, other, held), jnp.where(upper, held, other)], depth)
        depth += 1
    held = held.reshape((-1,) + slab.shape)
    for bit in range(bits_of("pair") - 1):
        other = swapped(held, "pair", 1 << bit)
        upper = bit_at("pair", bit) == 1
        held = jnp.concatenate([jnp.where(upper, other, held), jnp.where(upper, held, other)], -1)
    return held


def after(values, tokens):
    return lax.optimization_barrier((values, tokens))[0]


def gather_proj(slab, came):
    held = gather_far(slab, came)
    near = jnp.stack([held] + [across(held, 0, dy, dx) for dy, dx in ((0, 1), (1, 0), (1, 1))])
    return [near, across(near, 1, 0, 0)]


def gather_wide(slab, came, first):
    held = gather_far(slab, came)
    one, two = held[:, :first], held[:, first:]
    one = jnp.stack([one, across(one, 0, 0, 1)])
    two = jnp.stack([two, across(two, 0, 1, 0)])
    near = [one, across(one, 0, 1, 0), two, across(two, 0, 0, 1)]
    near, late = lax.optimization_barrier((near, (yield)))
    yield near + [across(piece, 1, 0, 0) for piece in near], late[:1]


def low(values):
    return values.astype(BF)


def wide(values):
    return values.astype(F32)


def reduce_proj(keep, send, gate_one, gate_two):
    came = across(send, 1, 0, 0)
    held = wide(keep[0]) + wide(came[0])
    ready = after([low(wide(keep[i]) + wide(came[i])) for i in (1, 2, 3)], gate_one)
    got = [across(part, 0, dy, dx) for part, (dy, dx) in zip(ready, ((0, 1), (1, 0), (1, 1)))]
    for part in got:
        held = held + wide(part)
    held = after(held, gate_two)
    for bit in range(bits_of("pair") - 2, -1, -1):
        held, _ = halved(held, "pair", bit, held.ndim - 1)
    depth = bits_of("mod") - 2
    rest = held.shape[1:]
    held = held.reshape((2,) * depth + rest)
    for bit in range(2, bits_of("mod") - 2):
        held, _ = halved(held, "mod", bit, depth - 1 - (bit - 2))
    held = held.reshape((2, 2) + rest)
    top = bits_of("mod") - 1
    upper, inner = bit_at("mod", top), bit_at("mod", top - 1)

    def slab(u, v):
        part = lax.dynamic_index_in_dim(held, upper ^ u, 0, keepdims=False)
        return lax.dynamic_index_in_dim(part, inner ^ v, 0, keepdims=False)

    total = slab(0, 0)
    for u, v in ((1, 0), (1, 1), (0, 1)):
        total = total + wide(swapped(low(slab(u, v)), "mod", (u << top) | (v << (top - 1))))
    return total, got[:1]


def halved(held, axis, bit, dim):
    size = held.shape[dim] // 2
    mine = bit_at(axis, bit)
    away = low(lax.dynamic_slice_in_dim(held, (1 - mine) * size, size, dim))
    stay = lax.dynamic_slice_in_dim(held, mine * size, size, dim)
    got = swapped(away, axis, 1 << bit)
    return stay + wide(got), got


def reduce_wide(keep_one, send_one, keep_two, send_two):
    came = across(send_one, 1, 0, 0), across(send_two, 1, 0, 0)
    gate = yield
    came_one, came_two = after(came, gate)
    go_one = low(wide(keep_one[2:]) + wide(came_one[2:]))
    go_two = low(wide(keep_two[2:]) + wide(came_two[2:]))
    back = across(go_one, 0, 1, 0), across(go_two, 0, 0, 1)
    gate = yield [go_one, go_two]
    back_one, back_two = after(back, gate)
    next_one = low(wide(keep_one[1]) + wide(came_one[1]) + wide(back_one[1]))
    next_two = low(wide(keep_two[1]) + wide(came_two[1]) + wide(back_two[1]))
    last = across(next_one, 0, 0, 1), across(next_two, 0, 1, 0)
    gate = yield [next_one, next_two]
    last_one, last_two = after(last, gate)
    held_one = wide(keep_one[0]) + wide(came_one[0]) + wide(back_one[0]) + wide(last_one)
    held_two = wide(keep_two[0]) + wide(came_two[0]) + wide(back_two[0]) + wide(last_two)
    held = jnp.concatenate([held_one, held_two], 1)
    yield [held]
    yield from reduce_far(held)


def reduce_far(held):
    for bit in range(bits_of("pair") - 2, -1, -1):
        held, got = halved(held, "pair", bit, held.ndim - 1)
    depth = bits_of("mod") - 2
    rest = held.shape[1:]
    held = held.reshape((2,) * depth + rest)
    for bit in range(2, bits_of("mod")):
        held, got = halved(held, "mod", bit, depth - 1 - (bit - 2))
        yield [held.reshape((-1,) + rest), got]


def settle(pieces, row, rows):
    part = jnp.stack([piece[:, :, row : row + rows] for piece in pieces])
    groups, rows, cols = part.shape[2:]
    part = part.reshape((2, 2, 2) + part.shape[2:])
    bits = (bit_at("mod", 0), bit_at("mod", 1), bit_at("pair", bits_of("pair") - 1))
    for dim, bit in enumerate(bits):
        part = jnp.where(bit == 1, jnp.flip(part, dim), part)
    return part.transpose(3, 1, 0, 4, 2, 5).reshape(4 * groups, rows, 2 * cols)


def per_device(rows_input, grad_out, w_qkv, w_out, w_up, w_down, vectors, b_up, live_rows):
    mods, pairs = lax.axis_size("mod"), lax.axis_size("pair")
    groups = mods // 4
    rows, width = rows_input.shape
    moved = rows // 2
    place = lax.axis_index("mod")
    upper = place >= mods // 2
    own_start = jnp.where(upper, moved, 0)
    away_start = jnp.where(upper, 0, moved)
    where = jnp.stack([place & 1, (place >> 1) & 1, bit_at("pair", bits_of("pair") - 1), own_start])

    def over(values):
        return swapped(values, "mod", mods // 2)

    chunk = moved // CHUNKS

    def units(sizes):
        return [(sum(sizes[:i]), size) for i, size in enumerate(sizes)]

    def over_units(array, sizes, gate):
        return [
            over(after(lax.dynamic_slice_in_dim(array, away_start + c * chunk, n * chunk), gate))
            for c, n in units(sizes)
        ]

    line = w_qkv.shape[0]
    per, thin = w_qkv.shape[1], w_out.shape[1]
    small = jnp.concatenate([vectors.reshape(-1), b_up.reshape(-1)])
    small_rows = -(-small.shape[0] // line)
    small = jnp.pad(small, (0, 16 * line - small.shape[0])).reshape(16, line)
    proj_slab = jnp.concatenate([w_qkv.T, small], 0)
    down = w_down.T.reshape(thin, BLOCKS, line).transpose(1, 0, 2)
    slab = [w_out.T.reshape(1, thin, line), w_up.T.reshape(BLOCKS, thin, line), down]
    slab = jnp.concatenate(slab, 0)

    live_own = lax.dynamic_slice_in_dim(live_rows, own_start // SLOTS, moved // SLOTS)
    live_away = lax.dynamic_slice_in_dim(live_rows, away_start // SLOTS, moved // SLOTS)
    head = jnp.pad(live_away.astype(BF)[None], ((0, 15), (0, width - moved // SLOTS)))
    folded = jnp.concatenate(jnp.split(slab.reshape(-1, line), width // line, 0), 1)
    first_rows = lax.dynamic_slice_in_dim(rows_input, away_start, X_UNITS[0] * chunk)
    proj_came = over(proj_slab)
    parcel = over(after(jnp.concatenate([first_rows, folded, head], 0), proj_came))
    tall = folded.shape[0]
    came = parcel[first_rows.shape[0] : first_rows.shape[0] + tall]
    came = jnp.concatenate(jnp.split(came, width // line, 1), 0).reshape(slab.shape)
    live = jnp.stack([live_own, parcel[first_rows.shape[0] + tall, : moved // SLOTS].astype(jnp.int32)])

    proj = gather_proj(proj_slab, proj_came)
    far_rows = [parcel]
    for c, n in units(X_UNITS)[1:]:
        part = lax.dynamic_slice_in_dim(rows_input, away_start + c * chunk, n * chunk)
        far_rows.append(over(after(part, far_rows[1:2])))
    wide_steps = gather_wide(slab, came, 1 + BLOCKS)
    next(wide_steps)
    far_grads = over_units(grad_out, FEED_UNITS, far_rows[1:2])

    tiny = settle(proj, per, small_rows).reshape(mods, small_rows, pairs, line)
    tiny = tiny.transpose(2, 0, 1, 3).reshape(pairs, mods, -1)
    count = vectors.size
    vec = tiny[:, :, :count].reshape((pairs, mods) + vectors.shape).transpose(0, 2, 1, 3)
    vec = vec.reshape(8, width).astype(F32)
    bup = tiny[:, :, count : count + b_up.size].reshape((pairs, mods) + b_up.shape).transpose(0, 2, 1, 3)
    bup = bup.reshape(pairs, BLOCKS, line).transpose(1, 0, 2).reshape(BLOCKS, width).astype(F32)

    kept = ()
    for (c0, n), far in zip(units(X_UNITS), far_rows):
        for i in range(n):
            *kept, done = attend(c0 + i, i, where, live, rows_input, far, vec, proj, kept, [])
            if c0 + i == CHUNKS - 2:
                gathered = wide_steps.send([done] + far_rows[3:] + far_grads[:1])
    wide_pieces, gates = gathered
    qkv_all, prob_all, mixed_all, x_all = kept
    fed, back_rows = (), []
    vec_sum, bup_sum = 0.0, 0.0
    for (c0, n), far in zip(units(FEED_UNITS), far_grads):
        (y0, size), = [unit for unit in units(Y_UNITS) if unit[0] <= c0 < unit[0] + unit[1]]
        fed = fed[: 7 if c0 == y0 else 8]
        out = feed(
            c0, n, c0 - y0, size * chunk, pairs, where, grad_out, far, x_all, mixed_all, vec, bup, wide_pieces, fed, gates
        )
        gates = []
        fed = out[:8]
        if c0 + n == y0 + size:
            back_rows.append(over(out[7]))
        vec_sum, bup_sum = vec_sum + out[8], bup_sum + out[9]
    result, act_all, dinner_all, first_all, dout_all, dbranch_all, dmix_all = fed[:7]
    wide_pair = wide_grads(
        pairs, where, dinner_all, act_all, first_all, dout_all, dbranch_all, mixed_all, groups, back_rows[:1]
    )
    wide_steps = reduce_wide(*after(wide_pair, back_rows[1:]))
    next(wide_steps)
    backed, back_grads = (), []
    qv_sum, done = 0.0, None
    for c0, n in units(BACK_UNITS):
        (d0, size), = [unit for unit in units(DX_UNITS) if unit[0] <= c0 < unit[0] + unit[1]]
        backed = backed[: 1 if c0 == d0 else 2]
        tokens = []
        if c0 in (1, 3):
            tokens = wide_steps.send(done)
        if c0 == 3:
            tokens = tokens + back_grads[:2]
        out = back(
            c0, n, c0 - d0, size * chunk, where, qkv_all, prob_all, dbranch_all, dmix_all, proj, backed, tokens
        )
        backed, done = out[:2], out[2]
        if c0 + n == d0 + size:
            back_grads.append(over(out[1]))
        qv_sum = qv_sum + out[2]
    dqkv_all = backed[0]

    vec_grad = jnp.concatenate([qv_sum[:2], vec_sum[:6]], 0).reshape(pairs, -1, mods, vectors.shape[1])
    bup_grad = bup_sum.reshape(BLOCKS, pairs, line).transpose(1, 0, 2).reshape(pairs, -1, mods, b_up.shape[1])
    tiny_grad = [g.transpose(2, 0, 1, 3).reshape(mods, pairs, -1) for g in (vec_grad, bup_grad)]
    tiny_grad = jnp.concatenate(tiny_grad, -1)
    tiny_grad = jnp.pad(tiny_grad, ((0, 0), (0, 0), (0, 16 * line - small_size(vectors, b_up))))
    tiny_grad = tiny_grad.reshape(mods, pairs, 16, line).transpose(0, 2, 1, 3).reshape(mods, 16, width).astype(BF)
    tokens = wide_steps.send(done)
    proj_pair = proj_grads(where, dqkv_all, x_all, tiny_grad, groups, tokens)
    *gates, g_wide = wide_steps
    g_proj, token = reduce_proj(*after(proj_pair, back_grads[2:3] + gates[0][1:]), [], g_wide[1:])
    input_grad, result = finish(where, dqkv_all, dbranch_all, proj, result, back_rows, back_grads[:-1], token)
    g_wide = g_wide[0][0]

    last = away_start + (CHUNKS - 1) * chunk
    input_grad = lax.dynamic_update_slice_in_dim(input_grad, wide(back_grads[-1]), last, 0)
    g_small = g_proj[per:].reshape(-1)
    return (
        result,
        input_grad,
        g_proj[:per].T,
        g_wide[0].T,
        g_wide[1 : 1 + BLOCKS].reshape(-1, line).T,
        g_wide[1 + BLOCKS :].transpose(1, 0, 2).reshape(thin, -1).T,
        g_small[:count].reshape(vectors.shape),
        g_small[count : count + b_up.size].reshape(b_up.shape),
    )


def small_size(vectors, b_up):
    return vectors.size + b_up.size


def solution(mesh):
    sharded = P("pair", "mod")
    spread = P(("mod", "pair"), None)
    weights = (sharded,) * 6
    return jax.shard_map(
        per_device,
        mesh=mesh,
        in_specs=(spread, spread) + weights + (P(("mod", "pair")),),
        out_specs=(spread, spread) + weights,
        check_vma=False,
    )
```

```python
import functools

import jax
import jax.numpy as jnp
from jax import lax
from jax.experimental import pallas as pl
from jax.experimental.pallas import tpu as pltpu
from jax.sharding import PartitionSpec as P

HEADS = 12
HEAD_DIM = 64
SLOTS = 64
CHUNKS = 4
X_UNITS = (1, 1, 1, 1)
FEED_UNITS = (1, 1, 2)
Y_UNITS = (2, 2)
BACK_UNITS = (1, 1, 1, 1)
DX_UNITS = (1, 1, 1, 1)
BLOCKS = 4
EPS = 1e-05
NEG = -1000000000.0
SCALE = HEAD_DIM**-0.5
LIMIT = 60 * 2**20
F32 = jnp.float32
BF = jnp.bfloat16
ANY = pl.BlockSpec(memory_space=pl.ANY)
VM = pl.BlockSpec(memory_space=pltpu.VMEM)
SM = pl.BlockSpec(memory_space=pltpu.SMEM)
S = jax.ShapeDtypeStruct
QUICK = pl.CostEstimate(flops=1, bytes_accessed=1, transcendentals=0)
SLOW = pl.CostEstimate(flops=10**10, bytes_accessed=30 * 10**6, transcendentals=0)
DMA = pltpu.SemaphoreType.DMA


def nt(a, b):
    return lax.dot_general(a, b, (((1,), (1,)), ((), ())), preferred_element_type=F32)


def nn(a, b):
    return lax.dot_general(a, b, (((1,), (0,)), ((), ())), preferred_element_type=F32)


def tn(a, b):
    return lax.dot_general(a, b, (((0,), (0,)), ((), ())), preferred_element_type=F32)


def colsum(v):
    return jnp.sum(v, 0, keepdims=True)


def copy(src, dst, sem):
    pltpu.make_async_copy(src, dst, sem).start()


def wait_for(ref, sem):
    pltpu.make_async_copy(ref, ref, sem).wait()


def pull(where, views, part, into, sem):
    core, low, side = where[0], where[1], where[2]
    for piece, (dc, dy, dx) in views:
        slab = (low ^ dy) * 2 + (core ^ dc)
        cols = piece.shape[-1]
        lane = pl.multiple_of((side ^ dx) * cols, cols)
        mid = (slice(None),) * (len(into.shape) - 3)
        copy(piece.at[:, part], into.at[(slice(None), slab) + mid + (pl.ds(lane, cols),)], sem)


def proj_views(refs):
    return [(ref.at[2 * dy + dx], (dc, dy, dx)) for dc, ref in enumerate(refs) for dy in (0, 1) for dx in (0, 1)]


def wide_views(refs):
    first, second = [], []
    for dc in (0, 1):
        for later in (0, 1):
            for early in (0, 1):
                first.append((refs[4 * dc + later].at[early], (dc, later, early)))
                second.append((refs[4 * dc + 2 + later].at[early], (dc, early, later)))
    return first, second


def attend_kernel(c, skip, where, live, rows, far, vec, *refs):
    views, refs = proj_views(refs[:2]), refs[-11:]
    qkv_all, prob_all, mixed_all, x_all, done, wqkv, xs, qkv, prob, mixed, sems = refs
    r, width = xs.shape
    h = r // 2
    seqs = prob.shape[0]
    done[...] = jnp.zeros_like(done)
    start = pl.multiple_of(where[3] + c * h, h)
    copy(rows.at[pl.ds(start, h)], xs.at[pl.ds(0, h)], sems.at[0])
    copy(far.at[pl.ds(skip * h, h)], xs.at[pl.ds(h, h)], sems.at[0])
    halves = wqkv.shape[0] // 2
    for i in (0, 1):
        some = [(piece.at[pl.ds(i * halves, halves)], bits) for piece, bits in views]
        pull(where, some, pl.ds(0, wqkv.shape[2]), wqkv.at[pl.ds(i * halves, halves)], sems.at[(1, 6)[i]])
    wait_for(xs, sems.at[0])
    span = pl.ds(c * r, r)
    copy(xs, x_all.at[span], sems.at[2])
    flat = wqkv.reshape(3 * width, width)
    x = xs[...]
    middle = width // 2
    for part in range(2):
        cols = slice(3 * part * middle, 3 * (part + 1) * middle)
        wait_for(wqkv.at[pl.ds(part * halves, halves)], sems.at[(1, 6)[part]])
        acc = nt(x, flat[cols, :])
        if part == 0:
            bias = jnp.concatenate([vec[0:1, :], jnp.zeros((1, middle), F32)], 1)
        else:
            bias = jnp.concatenate([jnp.zeros((1, middle), F32), vec[1:2, :]], 1)
        qkv[:, cols] = (acc + bias).astype(BF)
    copy(qkv, qkv_all.at[span], sems.at[3])
    lane = lax.broadcasted_iota(jnp.int32, (2 * SLOTS, 2 * HEAD_DIM), 1)
    low_half = lane < HEAD_DIM
    key = lax.broadcasted_iota(jnp.int32, (2 * SLOTS, 4 * SLOTS), 1) % (2 * SLOTS)

    def seq(s, carry):
        a = pl.multiple_of(s * SLOTS, SLOTS)
        b = pl.multiple_of(h + s * SLOTS, SLOTS)
        at = c * seqs + s
        valid = key < jnp.where(key < SLOTS, live[0, at], live[1, at] + SLOTS)
        for p in range(HEADS // 2):

            def take(part):
                cols = slice(part * width + p * 128, part * width + (p + 1) * 128)
                return jnp.concatenate([qkv[pl.ds(a, SLOTS), cols], qkv[pl.ds(b, SLOTS), cols]], 0)

            q, k, v = take(0), take(1), take(2)
            zero = jnp.zeros_like(k)
            k2 = jnp.concatenate([jnp.where(low_half, k, zero), jnp.where(low_half, zero, k)], 0)
            v2 = jnp.concatenate([jnp.where(low_half, v, zero), jnp.where(low_half, zero, v)], 0)
            score = jnp.where(valid, nt(q * SCALE, k2), NEG)
            halves = []
            for one in (score[:, : 2 * SLOTS], score[:, 2 * SLOTS :]):
                e = jnp.exp(one - jnp.max(one, -1, keepdims=True))
                halves.append((e * (1.0 / jnp.sum(e, -1, keepdims=True))).astype(BF))
            both = jnp.concatenate(halves, 1)
            prob[s, p] = both
            o = nn(both, v2).astype(BF)
            cols = slice(p * 128, (p + 1) * 128)
            mixed[pl.ds(a, SLOTS), cols] = o[:SLOTS]
            mixed[pl.ds(b, SLOTS), cols] = o[SLOTS:]
        copy(prob.at[s], prob_all.at[at], sems.at[4])
        return carry

    lax.fori_loop(0, seqs, seq, 0, unroll=2)
    copy(mixed, mixed_all.at[span], sems.at[5])
    wait_for(xs, sems.at[2])
    wait_for(qkv, sems.at[3])
    wait_for(prob, sems.at[4])
    wait_for(mixed, sems.at[5])


def attend(c, skip, where, live, rows, far, vec, pieces, before, tokens):
    width = far.shape[1]
    total = rows.shape[0]
    r = total // CHUNKS
    seqs = r // 2 // SLOTS
    groups = pieces[0].shape[1]
    per = 3 * width // (4 * groups)
    shapes = (
        S((total, 3 * width), BF),
        S((CHUNKS * seqs, HEADS // 2, 2 * SLOTS, 4 * SLOTS), BF),
        S((total, width), BF),
        S((total, width), BF),
    )
    return pl.pallas_call(
        functools.partial(attend_kernel, c, skip),
        out_shape=shapes + (S((8, 128), F32),),
        in_specs=[SM, SM, ANY, ANY, VM] + [ANY] * (2 + len(before) + len(tokens)),
        out_specs=(ANY,) * 4 + (VM,),
        input_output_aliases={7 + i: i for i in range(len(before))},
        scratch_shapes=[
            pltpu.VMEM((groups, 4, per, width), BF),
            pltpu.VMEM((r, width), BF),
            pltpu.VMEM((r, 3 * width), BF),
            pltpu.VMEM((seqs,) + shapes[1].shape[1:], BF),
            pltpu.VMEM((r, width), BF),
            DMA((7,)),
        ],
        compiler_params=pltpu.CompilerParams(vmem_limit_bytes=LIMIT),
        cost_estimate=SLOW,
        name="attend",
    )(where, live, rows, far, vec, *pieces, *before, *tokens)


def normed(v):
    c = v - jnp.mean(v, -1, keepdims=True)
    r = lax.rsqrt(jnp.mean(c * c, -1, keepdims=True) + EPS)
    return c * r, r


def norm_back(g, n, r):
    return r * (g - jnp.mean(g, -1, keepdims=True) - n * jnp.mean(g * n, -1, keepdims=True))


def feed_kernel(c0, subs, skip, sides, where, grads, far, x_all, mixed_all, vec, bup, *refs):
    first_views, second_views = wide_views(refs[:8])
    refs = refs[-27:]
    outs, sums, refs = refs[:8], refs[8:10], refs[10:]
    y_all, act_all, dinner_all, first_all, dout_all, dbranch_all, dmix_all, y_far = outs
    vsum, bsum = sums
    wout, wup, wdown, xs_all, mixed_in, gs_all, ys, act, slope, dinner, first, dout, dbranch, dmix, acc, n1, sems = refs
    r, width = ys.shape
    h = r // 2
    for t in range(subs):
        span = pl.ds((c0 + t) * r, r)
        start = pl.multiple_of(where[3] + (c0 + t) * h, h)
        copy(x_all.at[span], xs_all.at[t], sems.at[3, t])
        copy(mixed_all.at[span], mixed_in.at[t], sems.at[3, t])
        if t == 0:
            pull(where, first_views, pl.ds(0, 1), wout, sems.at[0, 0])
            pull(where, first_views, pl.ds(1, BLOCKS), wup, sems.at[1, 0])
        copy(grads.at[pl.ds(start, h)], gs_all.at[t, pl.ds(0, h)], sems.at[4, t])
        copy(far.at[pl.ds(t * h, h)], gs_all.at[t, pl.ds(h, h)], sems.at[4, t])
        if t == 0:
            pull(where, second_views, pl.ds(0, BLOCKS), wdown, sems.at[2, 0])
    out_flat = wout.reshape(width, width)
    ff = BLOCKS * width
    up_flat = wup.reshape(ff, width)
    step = width // sides

    def up_block(b):
        parts = [up_flat[pl.ds(side * BLOCKS * step + b * step, step), :] for side in range(sides)]
        return jnp.concatenate(parts, 0)

    def down_block(b):
        return wdown[:, :, b].reshape(width, width)

    for t in range(subs):
        c = c0 + t
        span = pl.ds(c * r, r)
        start = pl.multiple_of(where[3] + c * h, h)
        xs, mixed, gs = xs_all.at[t], mixed_in.at[t], gs_all.at[t]
        wait_for(xs, sems.at[3, t])
        wait_for(mixed, sems.at[3, t])
        if t == 0:
            wait_for(wout, sems.at[0, 0])
        sum1 = xs[...].astype(F32) + nt(mixed[...], out_flat[...]) + vec[2:3, :]
        hat, r1 = normed(sum1)
        n1[...] = hat
        top = hat * vec[4:5, :] + vec[5:6, :]
        if t:
            for ref in (act, dinner, first, dout, dbranch, dmix, ys):
                wait_for(ref, sems.at[5, 0])
        first[...] = top.astype(BF)
        copy(first, first_all.at[span], sems.at[5, 0])
        acc[...] = top + vec[3:4, :]
        if t == 0:
            wait_for(wup, sems.at[1, 0])
        for b in range(BLOCKS):
            cols = slice(b * width, (b + 1) * width)
            inner = nt(first[...], up_block(b)) + bup[b : b + 1, :]
            phi = 0.5 + 0.5 * lax.erf(inner * (2**-0.5))
            low = (inner * phi).astype(BF)
            act[:, cols] = low
            copy(act.at[:, cols], act_all.at[span, cols], sems.at[5, 0])
            slope[:, cols] = (phi + inner * (jnp.exp(-0.5 * inner * inner) * 0.3989422804014327)).astype(BF)
            if t == 0 and b == 0:
                wait_for(wdown, sems.at[2, 0])
            acc[...] += nt(low, down_block(b))
        n2, r2 = normed(acc[...])
        ys[...] = (n2 * vec[6:7, :] + vec[7:8, :]).astype(BF)
        copy(ys.at[pl.ds(0, h)], y_all.at[pl.ds(start, h)], sems.at[5, 0])
        copy(ys.at[pl.ds(h, h)], y_far.at[pl.ds((skip + t) * h, h)], sems.at[5, 0])
        wait_for(gs, sems.at[4, t])
        g = gs[...].astype(F32)
        sums_of = [None] * 6
        sums_of[4] = colsum(g * n2)
        sums_of[5] = colsum(g)
        dz2 = norm_back(g * vec[6:7, :], n2, r2)
        dout[...] = dz2.astype(BF)
        copy(dout, dout_all.at[span], sems.at[5, 0])
        sums_of[1] = colsum(dz2)
        acc[...] = dz2
        for b in range(BLOCKS):
            cols = slice(b * width, (b + 1) * width)
            grad = nn(dout[...], down_block(b)) * slope[:, cols].astype(F32)
            part = colsum(grad)
            bsum[0:1, cols] = part if t == 0 else bsum[0:1, cols] + part
            low = grad.astype(BF)
            dinner[:, cols] = low
            copy(dinner.at[:, cols], dinner_all.at[span, cols], sems.at[5, 0])
            acc[...] += nn(low, up_block(b))
        d = acc[...]
        hat = n1[...]
        sums_of[2] = colsum(d * hat)
        sums_of[3] = colsum(d)
        dz1 = norm_back(d * vec[4:5, :], hat, r1)
        sums_of[0] = colsum(dz1)
        low = dz1.astype(BF)
        dbranch[...] = low
        copy(dbranch, dbranch_all.at[span], sems.at[5, 0])
        dmix[...] = nn(low, out_flat[...]).astype(BF)
        copy(dmix, dmix_all.at[span], sems.at[5, 0])
        for i, part in enumerate(sums_of):
            vsum[i : i + 1, :] = part if t == 0 else vsum[i : i + 1, :] + part
    for ref in (act, dinner, first, dout, dbranch, dmix, ys):
        wait_for(ref, sems.at[5, 0])


def feed(c0, subs, skip, y_rows, sides, where, grads, far, x_all, mixed_all, vec, bup, pieces, before, tokens):
    total, width = x_all.shape
    r = total // CHUNKS
    ff = BLOCKS * width
    groups, thin = pieces[0].shape[1], pieces[0].shape[3]
    shapes = (
        S(grads.shape, BF),
        S((total, ff), BF),
        S((total, ff), BF),
        S((total, width), BF),
        S((total, width), BF),
        S((total, width), BF),
        S((total, width), BF),
    )
    return pl.pallas_call(
        functools.partial(feed_kernel, c0, subs, skip, sides),
        out_shape=shapes + (S((y_rows, width), BF), S((8, width), F32), S((1, ff), F32)),
        in_specs=[SM, ANY, ANY, ANY, ANY, VM, VM] + [ANY] * (8 + len(before) + len(tokens)),
        out_specs=(ANY,) * 8 + (VM,) * 2,
        input_output_aliases={15 + i: i for i in range(len(before))},
        scratch_shapes=[
            pltpu.VMEM((groups, 4, 1, thin, width), BF),
            pltpu.VMEM((groups, 4, BLOCKS, thin, width), BF),
            pltpu.VMEM((groups, 4, BLOCKS, thin, width), BF),
            pltpu.VMEM((subs, r, width), BF),
            pltpu.VMEM((subs, r, width), BF),
            pltpu.VMEM((subs, r, width), BF),
            pltpu.VMEM((r, width), BF),
            pltpu.VMEM((r, ff), BF),
            pltpu.VMEM((r, ff), BF),
            pltpu.VMEM((r, ff), BF),
            pltpu.VMEM((r, width), BF),
            pltpu.VMEM((r, width), BF),
            pltpu.VMEM((r, width), BF),
            pltpu.VMEM((r, width), BF),
            pltpu.VMEM((r, width), F32),
            pltpu.VMEM((r, width), F32),
            DMA((6, subs)),
        ],
        compiler_params=pltpu.CompilerParams(vmem_limit_bytes=LIMIT),
        cost_estimate=QUICK,
        name="feed",
    )(where, grads, far, x_all, mixed_all, vec, bup, *pieces, *before, *tokens)


def back_kernel(c0, skip, where, qkv_all, prob_all, dbranch_all, dmix_all, *refs):
    views, refs = proj_views(refs[:2]), refs[-12:]
    dqkv_all, dx_far, vsum, wqkv, qkv, prob, dbranch, dmix, dqkv, dxf, sems, seq_sems = refs
    r, width = dmix.shape
    h = dqkv_all.shape[0] // (2 * CHUNKS)
    subs = r // (2 * h)
    seqs = h // SLOTS
    for t in range(subs):
        for s in range(seqs):
            sem = seq_sems.at[t * seqs + s]
            for at in (2 * h * t + s * SLOTS, 2 * h * t + h + s * SLOTS):
                rows, there = pl.ds(at, SLOTS), pl.ds(c0 * 2 * h + at, SLOTS)
                copy(qkv_all.at[there], qkv.at[rows], sem)
                copy(dmix_all.at[there], dmix.at[rows], sem)
            copy(prob_all.at[(c0 + t) * seqs + s], prob.at[t * seqs + s], sem)
    pull(where, views, pl.ds(0, wqkv.shape[2]), wqkv, sems.at[3])
    for t in range(subs):
        there = pl.ds((c0 + t) * 2 * h + h, h)
        copy(dbranch_all.at[there], dbranch.at[pl.ds(t * h, h)], sems.at[4])
    lane = lax.broadcasted_iota(jnp.int32, (2 * SLOTS, 2 * HEAD_DIM), 1)
    low_half = lane < HEAD_DIM

    def seq(t, s):
        a = pl.multiple_of(2 * h * t + s * SLOTS, SLOTS)
        b = pl.multiple_of(2 * h * t + h + s * SLOTS, SLOTS)
        for p in range(HEADS // 2):

            def take(ref, part):
                cols = slice(part * width + p * 128, part * width + (p + 1) * 128)
                return jnp.concatenate([ref[pl.ds(a, SLOTS), cols], ref[pl.ds(b, SLOTS), cols]], 0)

            q, k, v = take(qkv, 0), take(qkv, 1), take(qkv, 2)
            do = take(dmix, 0)
            zero = jnp.zeros_like(k)
            k2 = jnp.concatenate([jnp.where(low_half, k, zero), jnp.where(low_half, zero, k)], 0)
            v2 = jnp.concatenate([jnp.where(low_half, v, zero), jnp.where(low_half, zero, v)], 0)
            both = prob[t * seqs + s, p]
            dp = nt(do, v2)
            wide = both.astype(F32)
            halves = []
            for u in range(2):
                cols = slice(u * 2 * SLOTS, (u + 1) * 2 * SLOTS)
                w = wide[:, cols] * dp[:, cols]
                halves.append((w - wide[:, cols] * jnp.sum(w, -1, keepdims=True)).astype(BF))
            ds = jnp.concatenate(halves, 1)
            dq = nn(ds, k2 * SCALE)
            dk = tn(ds, q * SCALE)
            dv = tn(both, do)
            dk = jnp.where(low_half, dk[: 2 * SLOTS], dk[2 * SLOTS :])
            dv = jnp.where(low_half, dv[: 2 * SLOTS], dv[2 * SLOTS :])
            for part, val in enumerate((dq, dk, dv)):
                cols = slice(part * width + p * 128, part * width + (p + 1) * 128)
                dqkv[pl.ds(a, SLOTS), cols] = val[:SLOTS].astype(BF)
                dqkv[pl.ds(b, SLOTS), cols] = val[SLOTS:].astype(BF)

    vsum[...] = jnp.zeros_like(vsum)
    for t in range(subs):
        chunk = pl.ds(t * 2 * h, 2 * h)

        def step(s, carry, t=t):
            sem = seq_sems.at[t * seqs + s]
            wait_for(qkv.at[pl.ds(0, 2 * SLOTS)], sem)
            wait_for(dmix.at[pl.ds(0, 2 * SLOTS)], sem)
            wait_for(prob.at[0], sem)
            seq(t, s)
            return carry

        lax.fori_loop(0, seqs, step, 0)
        copy(dqkv.at[chunk], dqkv_all.at[pl.ds((c0 + t) * 2 * h, 2 * h)], sems.at[5])
        if t == 0:
            wait_for(wqkv, sems.at[3])
            wait_for(dbranch, sems.at[4])
        mine = dqkv[chunk]
        part = slice(t * h, (t + 1) * h)
        dx = dbranch[part].astype(F32) + nn(mine[h:], wqkv.reshape(3 * width, width)[...])
        dxf[part, :] = dx.astype(BF)
        copy(dxf.at[pl.ds(t * h, h)], dx_far.at[pl.ds((skip + t) * h, h)], sems.at[7])
        vsum[0:1, :] += colsum(mine[:, :width].astype(F32))
        vsum[1:2, :] += colsum(mine[:, 2 * width :].astype(F32))
    wait_for(dqkv, sems.at[5])
    wait_for(dxf, sems.at[7])


def back(c0, subs, skip, dx_rows, where, qkv_all, prob_all, dbranch_all, dmix_all, pieces, before, tokens):
    total, width = dbranch_all.shape
    r = subs * total // CHUNKS
    h = r // 2
    seqs = h // SLOTS
    groups = pieces[0].shape[1]
    per = 3 * width // (4 * groups)
    return pl.pallas_call(
        functools.partial(back_kernel, c0, skip),
        out_shape=(S((total, 3 * width), BF), S((dx_rows, width), BF), S((8, width), F32)),
        in_specs=[SM] + [ANY] * (6 + len(before) + len(tokens)),
        out_specs=(ANY, ANY, VM),
        input_output_aliases={7 + i: i for i in range(len(before))},
        scratch_shapes=[
            pltpu.VMEM((groups, 4, per, width), BF),
            pltpu.VMEM((r, 3 * width), BF),
            pltpu.VMEM((seqs,) + prob_all.shape[1:], BF),
            pltpu.VMEM((h, width), BF),
            pltpu.VMEM((r, width), BF),
            pltpu.VMEM((r, 3 * width), BF),
            pltpu.VMEM((h, width), BF),
            DMA((8,)),
            DMA((seqs,)),
        ],
        compiler_params=pltpu.CompilerParams(vmem_limit_bytes=LIMIT),
        cost_estimate=QUICK,
        name="back",
    )(where, qkv_all, prob_all, dbranch_all, dmix_all, *pieces, *before, *tokens)


def finish_kernel(n_y, n_dx, where, dqkv_all, dbranch_all, *refs):
    views = proj_views(refs[:2])
    y_parts, dx_parts = refs[3 : 3 + n_y], refs[3 + n_y : 3 + n_y + n_dx]
    dx_all, y_all, wqkv, dqkv, dbranch, dx, came, wider, ys, sems = refs[-10:]
    width = dbranch.shape[2]
    h = dbranch.shape[1]
    moved = CHUNKS * h
    away = moved - where[3]
    pull(where, views, pl.ds(0, wqkv.shape[2]), wqkv, sems.at[0])
    for c, part in enumerate(dx_parts):
        copy(part, came.at[c], sems.at[2])
    size = moved // n_y
    for i, part in enumerate(y_parts):
        copy(part, ys.at[i], sems.at[3])
    for c in range(CHUNKS):
        span = pl.ds(c * 2 * h, h)
        copy(dqkv_all.at[span], dqkv.at[c], sems.at[5 + c])
        copy(dbranch_all.at[span], dbranch.at[c], sems.at[5 + c])
    wait_for(ys, sems.at[3])
    for i in range(n_y):
        copy(ys.at[i], y_all.at[pl.ds(pl.multiple_of(away + i * size, size), size)], sems.at[3])
    wait_for(came, sems.at[2])
    for c in range(n_dx):
        wider[c] = came[c].astype(F32)
        copy(wider.at[c], dx_all.at[pl.ds(pl.multiple_of(away + c * h, h), h)], sems.at[4])
    wait_for(wqkv, sems.at[0])
    for c in range(CHUNKS):
        wait_for(dqkv.at[c], sems.at[5 + c])
        wait_for(dbranch.at[c], sems.at[5 + c])
        dx[c] = dbranch[c].astype(F32) + nn(dqkv[c], wqkv.reshape(3 * width, width)[...])
        copy(dx.at[c], dx_all.at[pl.ds(pl.multiple_of(where[3] + c * h, h), h)], sems.at[1])
    wait_for(ys, sems.at[3])
    wait_for(wider, sems.at[4])
    wait_for(dx, sems.at[1])


def finish(where, dqkv_all, dbranch_all, pieces, result, y_parts, dx_parts, tokens):
    total, width = dbranch_all.shape
    h = total // (2 * CHUNKS)
    groups = pieces[0].shape[1]
    per = 3 * width // (4 * groups)
    n_y, n_dx = len(y_parts), len(dx_parts)
    return pl.pallas_call(
        functools.partial(finish_kernel, n_y, n_dx),
        out_shape=(S(result.shape, F32), S(result.shape, BF)),
        in_specs=[SM] + [ANY] * (5 + n_y + n_dx + len(tokens)),
        out_specs=(ANY, ANY),
        input_output_aliases={5: 1},
        scratch_shapes=[
            pltpu.VMEM((groups, 4, per, width), BF),
            pltpu.VMEM((CHUNKS, h, 3 * width), BF),
            pltpu.VMEM((CHUNKS, h, width), BF),
            pltpu.VMEM((CHUNKS, h, width), F32),
            pltpu.VMEM((n_dx, h, width), BF),
            pltpu.VMEM((n_dx, h, width), F32),
            pltpu.VMEM((n_y, CHUNKS * h // n_y, width), BF),
            DMA((5 + CHUNKS,)),
        ],
        compiler_params=pltpu.CompilerParams(vmem_limit_bytes=LIMIT),
        cost_estimate=QUICK,
        name="finish",
    )(where, dqkv_all, dbranch_all, *pieces, result, *y_parts, *dx_parts, *tokens)


def put(buf, where, mod, value, dims, by_pair=False):
    core, low, side = where[0], where[1], where[2]
    cols = buf.shape[-1]
    dc = core ^ (mod & 1)
    dy = low ^ ((mod >> 1) & 1)
    for half in range(2):
        dx = side ^ half
        at = dx * 2 + dy if by_pair else dy * 2 + dx
        buf[(dc, at, mod >> 2) + dims] = value[..., half * cols : (half + 1) * cols]


def hand_over(bufs, outs, sems):
    copies = []
    for i, buf in enumerate(bufs):
        for dc in (1, 0):
            at = 2 * i + dc
            copies.append(pltpu.make_async_copy(buf.at[dc], outs[at], sems.at[at]))
    for one in copies:
        one.start()
    for one in copies:
        one.wait()


def wide_grads_kernel(sides, where, dinner, act, first, dout, dbranch, mixed, *refs):
    outs, (one, two, sems) = refs[-7:-3], refs[-3:]
    b = pl.program_id(0)
    width = first.shape[1]
    thin = one.shape[4]
    mods = 4 * one.shape[2]

    @pl.when(b == 0)
    def _():
        whole = tn(dbranch[...], mixed[...]).astype(BF)
        for mod in range(mods):
            put(one, where, mod, whole[mod * thin : (mod + 1) * thin], (0,))

    up = tn(dinner[...], first[...]).astype(BF)
    step = width // sides
    tall = BLOCKS * thin
    for side in range(sides):
        for i in range(step // tall):
            mod = side * BLOCKS * step // tall + b * (step // tall) + i
            rows = slice(side * step + i * tall, side * step + (i + 1) * tall)
            put(one, where, mod, up[rows].reshape(BLOCKS, thin, width), (pl.ds(1, BLOCKS),))
    down = tn(dout[...], act[...]).astype(BF)
    for mod in range(mods):
        put(two, where, mod, down[mod * thin : (mod + 1) * thin], (b,), True)

    @pl.when(b == BLOCKS - 1)
    def _():
        hand_over((one, two), outs, sems)


def wide_grads(sides, where, dinner, act, first, dout, dbranch, mixed, groups, tokens):
    total, width = first.shape
    thin = width // (4 * groups)
    shapes = [(4, groups, 1 + BLOCKS, thin, width // 2), (4, groups, BLOCKS, thin, width // 2)]

    def whole(array):
        return pl.BlockSpec(array.shape, lambda b: (0, 0), pipeline_mode=pl.Buffered(1))

    block = pl.BlockSpec((total, width), lambda b: (0, b))
    return pl.pallas_call(
        functools.partial(wide_grads_kernel, sides),
        grid=(BLOCKS,),
        out_shape=(S(shapes[0], BF),) * 2 + (S(shapes[1], BF),) * 2,
        in_specs=[SM, block, block, whole(first), whole(dout), whole(dbranch), whole(mixed)] + [ANY] * len(tokens),
        out_specs=(ANY,) * 4,
        scratch_shapes=[pltpu.VMEM((2,) + shapes[0], BF), pltpu.VMEM((2,) + shapes[1], BF), DMA((4,))],
        compiler_params=pltpu.CompilerParams(vmem_limit_bytes=LIMIT),
        cost_estimate=QUICK,
        name="wide_grads",
    )(where, dinner, act, first, dout, dbranch, mixed, *tokens)


def proj_grads_kernel(where, dqkv, x, tiny, *refs):
    keep, send, buf, sems = refs[-4:]
    b = pl.program_id(0)
    mods = 4 * buf.shape[2]
    per = buf.shape[3] - tiny.shape[1]
    part = tn(dqkv[...], x[...]).astype(BF)
    for i in range(mods // 2):
        put(buf, where, b * (mods // 2) + i, part[i * per : (i + 1) * per], (pl.ds(0, per),))

    @pl.when(b == 1)
    def _():
        for mod in range(mods):
            put(buf, where, mod, tiny[mod], (pl.ds(per, tiny.shape[1]),))
        hand_over((buf,), (keep, send), sems)


def proj_grads(where, dqkv, x, tiny, groups, tokens):
    total, width = x.shape
    per = 3 * width // (4 * groups)
    shape = (4, groups, per + tiny.shape[1], width // 2)
    half = dqkv.shape[1] // 2
    return pl.pallas_call(
        proj_grads_kernel,
        grid=(2,),
        out_shape=(S(shape, BF),) * 2,
        in_specs=[
            SM,
            pl.BlockSpec((total, half), lambda b: (0, b)),
            pl.BlockSpec(x.shape, lambda b: (0, 0), pipeline_mode=pl.Buffered(1)),
            pl.BlockSpec(tiny.shape, lambda b: (0, 0, 0), pipeline_mode=pl.Buffered(1)),
        ]
        + [ANY] * len(tokens),
        out_specs=(ANY, ANY),
        scratch_shapes=[pltpu.VMEM((2,) + shape, BF), DMA((2,))],
        compiler_params=pltpu.CompilerParams(vmem_limit_bytes=LIMIT),
        cost_estimate=QUICK,
        name="proj_grads",
    )(where, dqkv, x, tiny, *tokens)


def bits_of(axis):
    return (lax.axis_size(axis) - 1).bit_length()


def swapped(values, axis, mask):
    return lax.ppermute(values, axis, [(i, i ^ mask) for i in range(lax.axis_size(axis))])


def across(values, dc, dy, dx):
    pairs = lax.axis_size("pair")
    mask = (2 * dy + dc) * pairs + dx * (pairs // 2)
    count = lax.axis_size("mod") * pairs
    return lax.ppermute(values, ("mod", "pair"), [(i, i ^ mask) for i in range(count)])


def bit_at(axis, bit):
    return (lax.axis_index(axis) >> bit) & 1


def gather_far(slab, came=None):
    held = slab
    depth = 0
    for bit in range(bits_of("mod") - 1, 1, -1):
        other = swapped(held, "mod", 1 << bit) if depth or came is None else came
        upper = bit_at("mod", bit) == 1
        held = jnp.stack([jnp.where(upper, other, held), jnp.where(upper, held, other)], depth)
        depth += 1
    held = held.reshape((-1,) + slab.shape)
    for bit in range(bits_of("pair") - 1):
        other = swapped(held, "pair", 1 << bit)
        upper = bit_at("pair", bit) == 1
        held = jnp.concatenate([jnp.where(upper, other, held), jnp.where(upper, held, other)], -1)
    return held


def after(values, tokens):
    return lax.optimization_barrier((values, tokens))[0]


def gather_proj(slab, came):
    held = gather_far(slab, came)
    near = jnp.stack([held] + [across(held, 0, dy, dx) for dy, dx in ((0, 1), (1, 0), (1, 1))])
    return [near, across(near, 1, 0, 0)]


def gather_wide(slab, came, first):
    held = gather_far(slab, came)
    one, two = held[:, :first], held[:, first:]
    one = jnp.stack([one, across(one, 0, 0, 1)])
    two = jnp.stack([two, across(two, 0, 1, 0)])
    near = [one, across(one, 0, 1, 0), two, across(two, 0, 0, 1)]
    near, late = lax.optimization_barrier((near, (yield)))
    yield near + [across(piece, 1, 0, 0) for piece in near], late[:1]


def low(values):
    return values.astype(BF)


def wide(values):
    return values.astype(F32)


def reduce_proj(keep, send, gate_one, gate_two):
    came = across(send, 1, 0, 0)
    held = wide(keep[0]) + wide(came[0])
    ready = after([low(wide(keep[i]) + wide(came[i])) for i in (1, 2, 3)], gate_one)
    got = [across(part, 0, dy, dx) for part, (dy, dx) in zip(ready, ((0, 1), (1, 0), (1, 1)))]
    for part in got:
        held = held + wide(part)
    held = after(held, gate_two)
    for bit in range(bits_of("pair") - 2, -1, -1):
        held, _ = halved(held, "pair", bit, held.ndim - 1)
    depth = bits_of("mod") - 2
    rest = held.shape[1:]
    held = held.reshape((2,) * depth + rest)
    for bit in range(2, bits_of("mod") - 2):
        held, _ = halved(held, "mod", bit, depth - 1 - (bit - 2))
    held = held.reshape((2, 2) + rest)
    top = bits_of("mod") - 1
    upper, inner = bit_at("mod", top), bit_at("mod", top - 1)

    def slab(u, v):
        part = lax.dynamic_index_in_dim(held, upper ^ u, 0, keepdims=False)
        return lax.dynamic_index_in_dim(part, inner ^ v, 0, keepdims=False)

    total = slab(0, 0)
    for u, v in ((1, 0), (1, 1), (0, 1)):
        total = total + wide(swapped(low(slab(u, v)), "mod", (u << top) | (v << (top - 1))))
    return total, got[:1]


def halved(held, axis, bit, dim):
    size = held.shape[dim] // 2
    mine = bit_at(axis, bit)
    away = low(lax.dynamic_slice_in_dim(held, (1 - mine) * size, size, dim))
    stay = lax.dynamic_slice_in_dim(held, mine * size, size, dim)
    got = swapped(away, axis, 1 << bit)
    return wide(stay) + wide(got), got


def reduce_wide(keep_one, send_one, keep_two, send_two):
    came = across(send_one, 1, 0, 0), across(send_two, 1, 0, 0)
    gate = yield
    came_one, came_two = after(came, gate)
    go_one = low(wide(keep_one[2:]) + wide(came_one[2:]))
    go_two = low(wide(keep_two[2:]) + wide(came_two[2:]))
    back = across(go_one, 0, 1, 0), across(go_two, 0, 0, 1)
    gate = yield [go_one, go_two]
    back_one, back_two = after(back, gate)
    next_one = low(wide(keep_one[1]) + wide(came_one[1]) + wide(back_one[1]))
    next_two = low(wide(keep_two[1]) + wide(came_two[1]) + wide(back_two[1]))
    last = across(next_one, 0, 0, 1), across(next_two, 0, 1, 0)
    gate = yield [next_one, next_two]
    last_one, last_two = after(last, gate)
    held_one = wide(keep_one[0]) + wide(came_one[0]) + wide(back_one[0]) + wide(last_one)
    held_two = wide(keep_two[0]) + wide(came_two[0]) + wide(back_two[0]) + wide(last_two)
    held = jnp.concatenate([low(held_one), low(held_two)], 1)
    yield [held]
    yield from reduce_far(held)


def reduce_far(held):
    for bit in range(bits_of("pair") - 2, -1, -1):
        held, got = halved(held, "pair", bit, held.ndim - 1)
    depth = bits_of("mod") - 2
    rest = held.shape[1:]
    held = held.reshape((2,) * depth + rest)
    for bit in range(2, bits_of("mod")):
        held, got = halved(held, "mod", bit, depth - 1 - (bit - 2))
        yield [held.reshape((-1,) + rest), got]


def settle(pieces, row, rows):
    part = jnp.stack([piece[:, :, row : row + rows] for piece in pieces])
    groups, rows, cols = part.shape[2:]
    part = part.reshape((2, 2, 2) + part.shape[2:])
    bits = (bit_at("mod", 0), bit_at("mod", 1), bit_at("pair", bits_of("pair") - 1))
    for dim, bit in enumerate(bits):
        part = jnp.where(bit == 1, jnp.flip(part, dim), part)
    return part.transpose(3, 1, 0, 4, 2, 5).reshape(4 * groups, rows, 2 * cols)


def per_device(rows_input, grad_out, w_qkv, w_out, w_up, w_down, vectors, b_up, live_rows):
    mods, pairs = lax.axis_size("mod"), lax.axis_size("pair")
    groups = mods // 4
    rows, width = rows_input.shape
    moved = rows // 2
    place = lax.axis_index("mod")
    upper = place >= mods // 2
    own_start = jnp.where(upper, moved, 0)
    away_start = jnp.where(upper, 0, moved)
    where = jnp.stack([place & 1, (place >> 1) & 1, bit_at("pair", bits_of("pair") - 1), own_start])

    def over(values):
        return swapped(values, "mod", mods // 2)

    chunk = moved // CHUNKS

    def units(sizes):
        return [(sum(sizes[:i]), size) for i, size in enumerate(sizes)]

    def over_units(array, sizes, gate):
        return [
            over(after(lax.dynamic_slice_in_dim(array, away_start + c * chunk, n * chunk), gate))
            for c, n in units(sizes)
        ]

    line = w_qkv.shape[0]
    per, thin = w_qkv.shape[1], w_out.shape[1]
    small = jnp.concatenate([vectors.reshape(-1), b_up.reshape(-1)])
    small_rows = -(-small.shape[0] // line)
    small = jnp.pad(small, (0, 16 * line - small.shape[0])).reshape(16, line)
    proj_slab = jnp.concatenate([w_qkv.T, small], 0)
    down = w_down.T.reshape(thin, BLOCKS, line).transpose(1, 0, 2)
    slab = [w_out.T.reshape(1, thin, line), w_up.T.reshape(BLOCKS, thin, line), down]
    slab = jnp.concatenate(slab, 0)

    live_own = lax.dynamic_slice_in_dim(live_rows, own_start // SLOTS, moved // SLOTS)
    live_away = lax.dynamic_slice_in_dim(live_rows, away_start // SLOTS, moved // SLOTS)
    head = jnp.pad(live_away.astype(BF)[None], ((0, 15), (0, width - moved // SLOTS)))
    folded = jnp.concatenate(jnp.split(slab.reshape(-1, line), width // line, 0), 1)
    first_rows = lax.dynamic_slice_in_dim(rows_input, away_start, X_UNITS[0] * chunk)
    proj_came = over(proj_slab)
    parcel = over(after(jnp.concatenate([first_rows, folded, head], 0), proj_came))
    tall = folded.shape[0]
    came = parcel[first_rows.shape[0] : first_rows.shape[0] + tall]
    came = jnp.concatenate(jnp.split(came, width // line, 1), 0).reshape(slab.shape)
    live = jnp.stack([live_own, parcel[first_rows.shape[0] + tall, : moved // SLOTS].astype(jnp.int32)])

    proj = gather_proj(proj_slab, proj_came)
    far_rows = [parcel]
    for c, n in units(X_UNITS)[1:]:
        part = lax.dynamic_slice_in_dim(rows_input, away_start + c * chunk, n * chunk)
        far_rows.append(over(after(part, far_rows[1:2])))
    wide_steps = gather_wide(slab, came, 1 + BLOCKS)
    next(wide_steps)
    far_grads = over_units(grad_out, FEED_UNITS, far_rows[1:2])

    tiny = settle(proj, per, small_rows).reshape(mods, small_rows, pairs, line)
    tiny = tiny.transpose(2, 0, 1, 3).reshape(pairs, mods, -1)
    count = vectors.size
    vec = tiny[:, :, :count].reshape((pairs, mods) + vectors.shape).transpose(0, 2, 1, 3)
    vec = vec.reshape(8, width).astype(F32)
    bup = tiny[:, :, count : count + b_up.size].reshape((pairs, mods) + b_up.shape).transpose(0, 2, 1, 3)
    bup = bup.reshape(pairs, BLOCKS, line).transpose(1, 0, 2).reshape(BLOCKS, width).astype(F32)

    kept = ()
    for (c0, n), far in zip(units(X_UNITS), far_rows):
        for i in range(n):
            *kept, done = attend(c0 + i, i, where, live, rows_input, far, vec, proj, kept, [])
            if c0 + i == CHUNKS - 2:
                gathered = wide_steps.send([done] + far_rows[3:] + far_grads[:1])
    wide_pieces, gates = gathered
    qkv_all, prob_all, mixed_all, x_all = kept
    fed, back_rows = (), []
    vec_sum, bup_sum = 0.0, 0.0
    for (c0, n), far in zip(units(FEED_UNITS), far_grads):
        (y0, size), = [unit for unit in units(Y_UNITS) if unit[0] <= c0 < unit[0] + unit[1]]
        fed = fed[: 7 if c0 == y0 else 8]
        out = feed(
            c0, n, c0 - y0, size * chunk, pairs, where, grad_out, far, x_all, mixed_all, vec, bup, wide_pieces, fed, gates
        )
        gates = []
        fed = out[:8]
        if c0 + n == y0 + size:
            back_rows.append(over(out[7]))
        vec_sum, bup_sum = vec_sum + out[8], bup_sum + out[9]
    result, act_all, dinner_all, first_all, dout_all, dbranch_all, dmix_all = fed[:7]
    wide_pair = wide_grads(
        pairs, where, dinner_all, act_all, first_all, dout_all, dbranch_all, mixed_all, groups, back_rows[:1]
    )
    wide_steps = reduce_wide(*after(wide_pair, back_rows[1:]))
    next(wide_steps)
    backed, back_grads = (), []
    qv_sum, done = 0.0, None
    for c0, n in units(BACK_UNITS):
        (d0, size), = [unit for unit in units(DX_UNITS) if unit[0] <= c0 < unit[0] + unit[1]]
        backed = backed[: 1 if c0 == d0 else 2]
        tokens = []
        if c0 in (1, 3):
            tokens = wide_steps.send(done)
        if c0 == 3:
            tokens = tokens + back_grads[:2]
        out = back(
            c0, n, c0 - d0, size * chunk, where, qkv_all, prob_all, dbranch_all, dmix_all, proj, backed, tokens
        )
        backed, done = out[:2], out[2]
        if c0 + n == d0 + size:
            back_grads.append(over(out[1]))
        qv_sum = qv_sum + out[2]
    dqkv_all = backed[0]

    vec_grad = jnp.concatenate([qv_sum[:2], vec_sum[:6]], 0).reshape(pairs, -1, mods, vectors.shape[1])
    bup_grad = bup_sum.reshape(BLOCKS, pairs, line).transpose(1, 0, 2).reshape(pairs, -1, mods, b_up.shape[1])
    tiny_grad = [g.transpose(2, 0, 1, 3).reshape(mods, pairs, -1) for g in (vec_grad, bup_grad)]
    tiny_grad = jnp.concatenate(tiny_grad, -1)
    tiny_grad = jnp.pad(tiny_grad, ((0, 0), (0, 0), (0, 16 * line - small_size(vectors, b_up))))
    tiny_grad = tiny_grad.reshape(mods, pairs, 16, line).transpose(0, 2, 1, 3).reshape(mods, 16, width).astype(BF)
    tokens = wide_steps.send(done)
    proj_pair = proj_grads(where, dqkv_all, x_all, tiny_grad, groups, tokens)
    *gates, g_wide = wide_steps
    g_proj, token = reduce_proj(*after(proj_pair, back_grads[2:3] + gates[0][1:]), [], g_wide[1:])
    input_grad, result = finish(where, dqkv_all, dbranch_all, proj, result, back_rows, back_grads[:-1], token)
    g_wide = g_wide[0][0]

    last = away_start + (CHUNKS - 1) * chunk
    input_grad = lax.dynamic_update_slice_in_dim(input_grad, wide(back_grads[-1]), last, 0)
    g_small = g_proj[per:].reshape(-1)
    return (
        result,
        input_grad,
        g_proj[:per].T,
        g_wide[0].T,
        g_wide[1 : 1 + BLOCKS].reshape(-1, line).T,
        g_wide[1 + BLOCKS :].transpose(1, 0, 2).reshape(thin, -1).T,
        g_small[:count].reshape(vectors.shape),
        g_small[count : count + b_up.size].reshape(b_up.shape),
    )


def small_size(vectors, b_up):
    return vectors.size + b_up.size


def solution(mesh):
    sharded = P("pair", "mod")
    spread = P(("mod", "pair"), None)
    weights = (sharded,) * 6
    return jax.shard_map(
        per_device,
        mesh=mesh,
        in_specs=(spread, spread) + weights + (P(("mod", "pair")),),
        out_specs=(spread, spread) + weights,
        check_vma=False,
    )
```
